32 devices in a mesh: grp: 2 (over x), section: 16 (over z, y, core).
Axes of the slice: x: 2, y: 2, z: 4, core: 2. Of those that a mesh axis runs over, the one named last changes fastest.
Arguments:
- low_feat: bfloat16 [256, 8192], P(('grp', 'section')), parts along dimension 0, may hold values from -80 to 80
- mid_feat: bfloat16 [256, 8192], P(('grp', 'section')), parts along dimension 0, may hold values from -80 to 80
- high_feat: bfloat16 [256, 8192], P(('grp', 'section')), parts along dimension 0, may hold values from -80 to 80
- w_fc: bfloat16 [3, 8192, 8192], P(None, 'section'), may hold values from -0.0546875 to 0.0546875
- gain: float32 [8192], P('section'), may hold values from 0.1 to 1.9
- w_lm: bfloat16 [8192, 16384], P(None, 'section'), may hold values from -2.5 to 2.5
- targets: int32 [256], P('grp'), parts along dimension 0, may hold values from 0 to 16383
Outputs:
- token_loss: float32 [256], P('grp'), parts along dimension 0
- grad_fc: bfloat16 [6, 8192, 8192], P('grp', 'section'), parts along dimension 0
- grad_gain: float32 [16384], P(('grp', 'section')), parts along dimension 0
- grad_lm: bfloat16 [16384, 16384], P('grp', 'section'), parts along dimension 0
The draws below stay inside these ranges and needn't reach their ends.
There are 2 independent parts, one for each index of `grp`. The reference program is written for one: setup_inputs(seed, part) draws one part's arguments, and reference() takes and returns one part's arrays. A program takes and returns all parts, laid end to end along the dimension named above; an argument that names none is the same for every part. Nothing has to cross between parts.
All inputs are finite; a program needn't handle non-finite values.
Results may differ from the reference program's by a relative error of at most 0.0049.
The reference program's roundings to bfloat16 on the way (of `normed`, `dlogits` and `dfused`) count: a program that leaves them out, or rounds other values in their place, can miss the bound.
Values may be sent and summed in bfloat16 or wider, within the bound.
No kernel may reach another device: no remote copies, remote signals or barrier semaphores. Data moves between devices by JAX's collectives and lax.ppermute only.
A program may use at most 192 MiB of HBM per device.

```python
import math
import jax
import jax.numpy as jnp
from jax import lax

D = 8192
V = 16384
TOKENS = 128


def draw_low_feat(key, part):
    key = jax.random.fold_in(key, 11)
    key_vals, key_rows = jax.random.split(key, 2)
    values = jax.random.normal(key_vals, (TOKENS, D), jnp.float32)
    row_scale = jnp.exp(jax.random.uniform(key_rows, (TOKENS, 1), jnp.float32, 0.0, math.log(10.0)))
    return jnp.clip(values * row_scale, -80.0, 80.0).astype(jnp.bfloat16)


def draw_mid_feat(key, part):
    key = jax.random.fold_in(key, 12)
    key_vals, key_rows = jax.random.split(key, 2)
    values = jax.random.normal(key_vals, (TOKENS, D), jnp.float32)
    row_scale = jnp.exp(jax.random.uniform(key_rows, (TOKENS, 1), jnp.float32, 0.0, math.log(10.0)))
    return jnp.clip(values * row_scale, -80.0, 80.0).astype(jnp.bfloat16)


def draw_high_feat(key, part):
    key = jax.random.fold_in(key, 13)
    key_vals, key_rows = jax.random.split(key, 2)
    values = jax.random.normal(key_vals, (TOKENS, D), jnp.float32)
    row_scale = jnp.exp(jax.random.uniform(key_rows, (TOKENS, 1), jnp.float32, 0.0, math.log(10.0)))
    return jnp.clip(values * row_scale, -80.0, 80.0).astype(jnp.bfloat16)


def draw_w_lm(key, part):
    key = jax.random.fold_in(key, 21)
    key_vals = jax.random.fold_in(key, 0)
    values = jax.random.normal(key_vals, (D, V), jnp.float32)
    col_scale = 2.4
    return jnp.clip(values * col_scale / math.sqrt(D), -2.5, 2.5).astype(jnp.bfloat16)


def touch_ends(drawn, rng, low, largest):
    spot = [jax.random.randint(jax.random.fold_in(rng, axis), (), 0, length) for axis, length in enumerate(drawn.shape)]
    longest = drawn.shape.index(max(drawn.shape))
    next_to = spot[:longest] + [(spot[longest] + 1) % drawn.shape[longest]] + spot[longest + 1:]
    return drawn.at[tuple(spot)].set(low).at[tuple(next_to)].set(largest)


def spiked(result, key, source, target, blocks, factor):
    owner, partner = [(jnp.arange(result.shape[axis_at]) // (result.shape[axis_at] // blocks)).reshape([-1 if axis == axis_at else 1 for axis in range(result.ndim)]) for axis_at in (source, target)]
    chosen = jax.random.permutation(key, blocks)[partner]
    strong = (owner == chosen) | (owner == (partner + blocks // 2) % blocks)
    return jnp.where(strong, factor * result, result)


def block_scale(rng, dims, cuts, least, largest):
    def one(axis_at, parts):
        draws = jax.random.uniform(jax.random.fold_in(jax.random.fold_in(rng, 6), axis_at), (parts,), jnp.float32, least / len(cuts), largest / len(cuts))
        return jnp.repeat(jnp.exp(draws), dims[axis_at] // parts).reshape((-1,) + (1,) * (len(dims) - axis_at - 1))

    factor_of = one(*cuts[0])
    for cut in cuts[1:]:
        factor_of = factor_of * one(*cut)
    return factor_of


def bell_draw_with(own_key, extent, deviation, most, cuts, heavy, kind=jnp.bfloat16):
    values = deviation * jax.random.normal(own_key, extent, jnp.float32)
    if cuts:
        values = values * block_scale(own_key, extent, cuts, -0.22, 0.18)
    return jnp.clip(spiked(values, jax.random.fold_in(own_key, 3), *heavy), -most, most).astype(kind)


def setup_inputs(seed: int = 0, part: int = 0) -> dict:
    key_list = jax.random.split(jax.random.key(seed), 8)
    part_keys = jax.random.split(jax.random.fold_in(key_list[7], part), 8)
    return {
        "low_feat": draw_low_feat(jax.random.fold_in(jax.random.fold_in(key_list[7], part), 71), part),
        "mid_feat": draw_mid_feat(jax.random.fold_in(jax.random.fold_in(key_list[7], part), 71), part),
        "high_feat": draw_high_feat(jax.random.fold_in(jax.random.fold_in(key_list[7], part), 71), part),
        "w_fc": bell_draw_with(key_list[3], (3, D, D), (3 * D) ** -0.5, 0.0546875, ((1, 16),), (1, 2, 16, 2.0)),
        "gain": jnp.clip(1.0 + 0.18 * jax.random.normal(key_list[4], (D,), jnp.float32), 0.1, 1.9),
        "w_lm": draw_w_lm(jax.random.fold_in(key_list[7], 71), part),
        "targets": touch_ends(jax.random.randint(part_keys[6], (TOKENS,), 0, V), jax.random.fold_in(part_keys[6], 1), 0, V - 1).astype(jnp.int32),
    }


def reference(low_feat, mid_feat, high_feat, w_fc, gain, w_lm, targets):
    joined_sum = jnp.dot(low_feat, w_fc[0], preferred_element_type=jnp.float32)
    joined_sum = joined_sum + jnp.dot(mid_feat, w_fc[1], preferred_element_type=jnp.float32)
    joined_sum = joined_sum + jnp.dot(high_feat, w_fc[2], preferred_element_type=jnp.float32)
    inv_rms = lax.rsqrt(lax.optimization_barrier(jnp.mean(joined_sum * joined_sum, axis=1, keepdims=True)) + 1e-06)
    normed = (joined_sum * inv_rms * gain[None, :]).astype(jnp.bfloat16)
    logits = jnp.dot(normed, w_lm, preferred_element_type=jnp.float32)
    row_peak = lax.optimization_barrier(jnp.max(logits, axis=1, keepdims=True))
    log_total = row_peak + jnp.log(lax.optimization_barrier(jnp.sum(jnp.exp(logits - row_peak), axis=1, keepdims=True)))
    onehot = (jnp.arange(V, dtype=jnp.int32)[None, :] == targets[:, None]).astype(jnp.float32)
    picked = lax.optimization_barrier(jnp.sum(logits * onehot, axis=1))
    token_loss = log_total[:, 0] - picked
    soft_probs = jnp.exp(logits - log_total)
    dlogits = ((soft_probs - onehot) / TOKENS).astype(jnp.bfloat16)
    grad_lm = jnp.dot(normed.T, dlogits, preferred_element_type=jnp.float32).astype(jnp.bfloat16)
    dnormed = jnp.dot(dlogits, w_lm.T, preferred_element_type=jnp.float32)
    grad_gain = lax.optimization_barrier(jnp.sum(dnormed * joined_sum * inv_rms, axis=0))
    dscaled = dnormed * gain[None, :]
    rowdot = lax.optimization_barrier(jnp.sum(dscaled * joined_sum, axis=1, keepdims=True))
    dfused = (inv_rms * dscaled - joined_sum * inv_rms * inv_rms * inv_rms * rowdot / D).astype(jnp.bfloat16)
    grad_fc = jnp.stack([jnp.dot(low_feat.T, dfused, preferred_element_type=jnp.float32), jnp.dot(mid_feat.T, dfused, preferred_element_type=jnp.float32), jnp.dot(high_feat.T, dfused, preferred_element_type=jnp.float32)]).astype(jnp.bfloat16)
    return (token_loss, grad_fc, grad_gain, grad_lm)
```

```python
import functools

import jax
import jax.numpy as jnp
import numpy as np
from jax import lax
from jax.experimental import pallas as pl
from jax.experimental.pallas import tpu as pltpu
from jax.sharding import PartitionSpec as P

epsilon = 1e-06
VMEM_LIMIT = 48 * 1024 * 1024


def places(order):
    count = len(order)
    out = []
    for q in range(1 << count):
        out.append(sum(((q >> (count - 1 - k)) & 1) << bit for k, bit in enumerate(order)))
    return np.array(out, np.int32)


def exchange(x, bit, size):
    return lax.ppermute(x, "section", [(i, i ^ (1 << bit)) for i in range(size)])


def reduce_halves(low, high, order, size):
    received = exchange(high, order[0], size)
    for bit in order[1:]:
        half = low.shape[0] // 2
        high = low[half:] + received[half:]
        fresh = exchange(high, bit, size)
        low = low[:half] + received[:half]
        received = fresh
    return low[0] + received[0]


def gather_halves(own, order, size):
    held = own[None]
    for bit in order[:0:-1]:
        held = jnp.concatenate([held, exchange(held, bit, size)], axis=0)
    return held, exchange(held, order[0], size)


def params(steps_flops, steps_bytes):
    return dict(
        compiler_params=pltpu.CompilerParams(vmem_limit_bytes=VMEM_LIMIT),
        cost_estimate=pl.CostEstimate(flops=steps_flops, bytes_accessed=steps_bytes, transcendentals=0),
    )


def join_kernel(table, x_ref, w_ref, first_ref, second_ref):
    rows = w_ref.shape[1]
    total = jnp.dot(x_ref[:, :rows], w_ref[0], preferred_element_type=jnp.float32)
    total += jnp.dot(x_ref[:, rows : 2 * rows], w_ref[1], preferred_element_type=jnp.float32)
    total += jnp.dot(x_ref[:, 2 * rows :], w_ref[2], preferred_element_type=jnp.float32)
    half = total.shape[0] // 2
    first_ref[0] = total[:half]
    second_ref[0] = total[half:]


def join(table, x, w_fc):
    count = table.shape[1]
    tokens = x.shape[0]
    rows = w_fc.shape[1]
    shape = jax.ShapeDtypeStruct((count, tokens // 2, rows), jnp.float32)
    if rows % 128:
        total = jnp.dot(x, w_fc.reshape(-1, w_fc.shape[2]), preferred_element_type=jnp.float32)
        total = total.reshape(2, tokens // 2, -1, rows).transpose(0, 2, 1, 3)
        chosen = jnp.take(total, table[0], axis=1)
        return jnp.take(chosen[0], table[1], axis=0), jnp.take(chosen[1], table[2], axis=0)
    return pl.pallas_call(
        join_kernel,
        out_shape=(shape, shape),
        grid_spec=pltpu.PrefetchScalarGridSpec(
            num_scalar_prefetch=1,
            grid=(count,),
            in_specs=[
                pl.BlockSpec(x.shape, lambda g, t: (0, 0)),
                pl.BlockSpec((3, rows, rows), lambda g, t: (0, 0, t[0, g])),
            ],
            out_specs=(
                pl.BlockSpec((1, tokens // 2, rows), lambda g, t: (t[1, g], 0, 0)),
                pl.BlockSpec((1, tokens // 2, rows), lambda g, t: (t[2, g], 0, 0)),
            ),
        ),
        name="join",
        **params(6 * tokens * rows * rows * count, count * (6 * rows * rows + 4 * tokens * rows)),
    )(table, x, w_fc)


def logits_kernel(table, first_ref, second_ref, w_ref, out_ref):
    block = jnp.concatenate([first_ref[0], second_ref[0]], axis=0)
    part = jnp.dot(block, w_ref[...], preferred_element_type=jnp.float32)

    @pl.when(pl.program_id(0) == 0)
    def _():
        out_ref[...] = part

    @pl.when(pl.program_id(0) != 0)
    def _():
        out_ref[...] += part


def natural(table, first, second):
    chosen = jnp.concatenate([jnp.take(first, table[1], axis=0), jnp.take(second, table[2], axis=0)], axis=1)
    return chosen


def head(table, first, second, w_lm):
    count, half, rows = first.shape
    share = w_lm.shape[1]
    if rows % 128:
        block = natural(table, first, second)
        weights = jnp.take(w_lm.reshape(-1, rows, share), table[0], axis=0)
        return jnp.einsum("ctr,crv->tv", block, weights, preferred_element_type=jnp.float32)
    return pl.pallas_call(
        logits_kernel,
        out_shape=jax.ShapeDtypeStruct((2 * half, share), jnp.float32),
        grid_spec=pltpu.PrefetchScalarGridSpec(
            num_scalar_prefetch=1,
            grid=(count,),
            in_specs=[
                pl.BlockSpec((1, half, rows), lambda g, t: (t[1, g], 0, 0)),
                pl.BlockSpec((1, half, rows), lambda g, t: (t[2, g], 0, 0)),
                pl.BlockSpec((rows, share), lambda g, t: (t[0, g], 0)),
            ],
            out_specs=pl.BlockSpec((2 * half, share), lambda g, t: (0, 0)),
        ),
        name="head",
        **params(4 * half * rows * share * count, count * rows * (2 * share + 4 * half)),
    )(table, first, second, w_lm)


def back_kernel(table, d_ref, w_ref, first_ref, second_ref):
    total = lax.dot_general(
        d_ref[...], w_ref[...], (((1,), (1,)), ((), ())), preferred_element_type=jnp.float32
    )
    half = total.shape[0] // 2
    first_ref[0] = total[:half]
    second_ref[0] = total[half:]


def back(table, dlogits, w_lm, rows):
    count = table.shape[1]
    tokens, share = dlogits.shape
    shape = jax.ShapeDtypeStruct((count, tokens // 2, rows), jnp.float32)
    if rows % 128:
        total = lax.dot_general(
            dlogits, w_lm, (((1,), (1,)), ((), ())), preferred_element_type=jnp.float32
        )
        total = total.reshape(2, tokens // 2, -1, rows).transpose(0, 2, 1, 3)
        chosen = jnp.take(total, table[0], axis=1)
        return jnp.take(chosen[0], table[1], axis=0), jnp.take(chosen[1], table[2], axis=0)
    return pl.pallas_call(
        back_kernel,
        out_shape=(shape, shape),
        grid_spec=pltpu.PrefetchScalarGridSpec(
            num_scalar_prefetch=1,
            grid=(count,),
            in_specs=[
                pl.BlockSpec(dlogits.shape, lambda g, t: (0, 0)),
                pl.BlockSpec((rows, share), lambda g, t: (t[0, g], 0)),
            ],
            out_specs=(
                pl.BlockSpec((1, tokens // 2, rows), lambda g, t: (t[1, g], 0, 0)),
                pl.BlockSpec((1, tokens // 2, rows), lambda g, t: (t[2, g], 0, 0)),
            ),
        ),
        name="back",
        **params(2 * tokens * rows * share * count, count * rows * (2 * share + 4 * tokens)),
    )(table, dlogits, w_lm)


def head_grad_kernel(table, fl_ref, sl_ref, fh_ref, sh_ref, d_ref, out_ref):
    step = pl.program_id(0)
    half_steps = pl.num_programs(0) // 2

    def fill(first_ref, second_ref):
        block = jnp.concatenate([first_ref[0], second_ref[0]], axis=0)
        out_ref[...] = lax.dot_general(
            block, d_ref[...], (((0,), (0,)), ((), ())), preferred_element_type=jnp.float32
        ).astype(out_ref.dtype)

    @pl.when(step < half_steps)
    def _():
        fill(fl_ref, sl_ref)

    @pl.when(step >= half_steps)
    def _():
        fill(fh_ref, sh_ref)


def paired_specs(count, half, rows):
    low = lambda row: lambda g, t: (t[row, jnp.minimum(g, count - 1)], 0, 0)
    high = lambda row: lambda g, t: (t[row, jnp.maximum(g - count, 0)], 0, 0)
    shape = (1, half, rows)
    return [pl.BlockSpec(shape, low(1)), pl.BlockSpec(shape, low(2)), pl.BlockSpec(shape, high(1)), pl.BlockSpec(shape, high(2))]


def head_grad(table, low, high, dlogits):
    count, half, rows = low[0].shape
    tokens, share = dlogits.shape
    if rows % 128:
        block = jnp.concatenate(
            [natural(table[:, :count], *low), natural(table[:, :count], *high)], axis=0
        )
        block = jnp.take(block, jnp.argsort(table[0]), axis=0)
        return jnp.einsum("ctr,tv->crv", block, dlogits, preferred_element_type=jnp.float32).astype(
            jnp.bfloat16
        ).reshape(-1, share)
    return pl.pallas_call(
        head_grad_kernel,
        out_shape=jax.ShapeDtypeStruct((2 * count * rows, share), jnp.bfloat16),
        grid_spec=pltpu.PrefetchScalarGridSpec(
            num_scalar_prefetch=1,
            grid=(2 * count,),
            in_specs=paired_specs(count, half, rows) + [pl.BlockSpec(dlogits.shape, lambda g, t: (0, 0))],
            out_specs=pl.BlockSpec((rows, share), lambda g, t: (t[0, g], 0)),
        ),
        name="head_grad",
        **params(4 * tokens * rows * share * count, 2 * count * rows * (2 * share + 2 * tokens)),
    )(table, low[0], low[1], high[0], high[1], dlogits)


def join_grad_kernel(table, fl_ref, sl_ref, fh_ref, sh_ref, x_ref, out_ref):
    step = pl.program_id(0)
    half_steps = pl.num_programs(0) // 2
    rows = out_ref.shape[1]

    def fill(first_ref, second_ref):
        block = jnp.concatenate([first_ref[0], second_ref[0]], axis=0)
        for j in range(3):
            out_ref[j] = jnp.dot(
                x_ref[j * rows : (j + 1) * rows, :], block, preferred_element_type=jnp.float32
            ).astype(out_ref.dtype)

    @pl.when(step < half_steps)
    def _():
        fill(fl_ref, sl_ref)

    @pl.when(step >= half_steps)
    def _():
        fill(fh_ref, sh_ref)


def join_grad(table, low, high, x_turned):
    count, half, rows = low[0].shape
    tokens = 2 * half
    if rows % 128:
        block = jnp.concatenate(
            [natural(table[:, :count], *low), natural(table[:, :count], *high)], axis=0
        )
        block = jnp.take(block, jnp.argsort(table[0]), axis=0)
        return jnp.einsum(
            "jrt,cts->jrcs", x_turned.reshape(3, rows, tokens), block, preferred_element_type=jnp.float32
        ).astype(jnp.bfloat16).reshape(3, rows, -1)
    return pl.pallas_call(
        join_grad_kernel,
        out_shape=jax.ShapeDtypeStruct((3, rows, 2 * count * rows), jnp.bfloat16),
        grid_spec=pltpu.PrefetchScalarGridSpec(
            num_scalar_prefetch=1,
            grid=(2 * count,),
            in_specs=paired_specs(count, half, rows) + [pl.BlockSpec(x_turned.shape, lambda g, t: (0, 0))],
            out_specs=pl.BlockSpec((3, rows, rows), lambda g, t: (0, 0, t[0, g])),
        ),
        name="join_grad",
        **params(12 * tokens * rows * rows * count, 2 * count * rows * (6 * rows + 2 * tokens)),
    )(table, low[0], low[1], high[0], high[1], x_turned)


def merge_sums(a, b):
    peak = jnp.maximum(a[0], b[0])
    shift_a, shift_b = a[0] - peak, b[0] - peak
    scale_a, scale_b = jnp.exp(shift_a), jnp.exp(shift_b)
    return jnp.stack(
        [
            peak,
            a[1] * scale_a + b[1] * scale_b,
            (a[2] + a[1] * shift_a) * scale_a + (b[2] + b[1] * shift_b) * scale_b,
            a[3] + b[3],
        ]
    )


def on_device(size, low_feat, mid_feat, high_feat, w_fc, gain, w_lm, targets):
    me = lax.axis_index("section")
    rows, full_width = w_fc.shape[1], w_fc.shape[2]
    tokens = targets.shape[0]
    half = tokens // 2
    bits = size.bit_length() - 1
    orders = (list(range(bits)), [0, 2, 1] + list(range(3, bits)))

    place_first, place_second = places(orders[0]), places(orders[1])
    where_second = np.argsort(place_second)[place_first]
    count = size // 2
    within = np.stack([np.arange(size) % count, where_second % count])
    chunk = jnp.asarray(place_first) ^ me
    table = jnp.concatenate([chunk[None], jnp.asarray(within, jnp.int32)], axis=0).astype(jnp.int32)
    table_low, table_high = table[:, :count], table[:, count:]

    sent = jnp.concatenate(
        [f.reshape(-1, size, rows) for f in (low_feat, mid_feat, high_feat)], axis=2
    ).transpose(1, 0, 2)
    x = lax.all_to_all(sent, "section", split_axis=0, concat_axis=0, tiled=True).reshape(tokens, 3 * rows)

    joined_high = join(table_high, x, w_fc)
    joined_low = join(table_low, x, w_fc)
    joined = jnp.concatenate(
        [reduce_halves(joined_low[s], joined_high[s], orders[s], size) for s in range(2)], axis=0
    )

    squares_own = jnp.sum(joined * joined, axis=1)
    squares = jnp.sum(
        lax.all_to_all(
            jnp.broadcast_to(squares_own[None], (size, tokens)), "section", split_axis=0, concat_axis=0, tiled=True
        ),
        axis=0,
    )
    inv_rms = lax.rsqrt(squares / full_width + epsilon)[:, None]
    normed = (joined * inv_rms * gain[None, :]).astype(jnp.bfloat16)
    parts = [gather_halves(normed[s * half : (s + 1) * half], orders[s], size) for s in range(2)]
    normed_low = [p[0] for p in parts]
    normed_high = [p[1] for p in parts]

    logits = head(table_low, *normed_low, w_lm) + head(table_high, *normed_high, w_lm)
    share = w_lm.shape[1]
    column = me * share + lax.iota(jnp.int32, share)
    is_target = column[None, :] == targets[:, None]
    peak = jnp.max(logits, axis=1)
    shifted = logits - peak[:, None]
    weight = jnp.exp(shifted)
    sums = jnp.stack(
        [
            peak,
            jnp.sum(weight, axis=1),
            jnp.sum(weight * shifted, axis=1),
            jnp.sum(jnp.where(is_target, logits, 0.0), axis=1),
        ]
    )
    for bit in range(bits):
        sums = merge_sums(sums, exchange(sums, bit, size))
    peak, exp_total, exp_moment, picked = sums
    log_total = peak + jnp.log(exp_total)
    token_loss = log_total - picked
    dlogits = (
        (jnp.exp(logits - log_total[:, None]) - is_target.astype(jnp.float32)) / tokens
    ).astype(jnp.bfloat16)
    rowdot = ((exp_moment / exp_total - (picked - peak)) / tokens)[:, None] / inv_rms

    back_high = back(table_high, dlogits, w_lm, rows)
    back_low = back(table_low, dlogits, w_lm, rows)
    grad_lm = head_grad(table, normed_low, normed_high, dlogits)
    dnormed = jnp.concatenate(
        [reduce_halves(back_low[s], back_high[s], orders[s], size) for s in range(2)], axis=0
    )

    grad_gain = jnp.sum(dnormed * joined * inv_rms, axis=0)
    dfused = (
        inv_rms * (dnormed * gain[None, :]) - joined * (inv_rms * inv_rms * inv_rms * rowdot / full_width)
    ).astype(jnp.bfloat16)
    parts = [gather_halves(dfused[s * half : (s + 1) * half], orders[s], size) for s in range(2)]
    grad_fc = join_grad(table, [p[0] for p in parts], [p[1] for p in parts], x.T)
    return (token_loss, grad_fc, grad_gain, grad_lm)


def solution(mesh):
    return jax.shard_map(
        functools.partial(on_device, mesh.shape["section"]),
        mesh=mesh,
        in_specs=(
            P(("grp", "section"), None),
            P(("grp", "section"), None),
            P(("grp", "section"), None),
            P(None, "section", None),
            P("section"),
            P(None, "section"),
            P("grp"),
        ),
        out_specs=(P("grp"), P("grp", "section", None), P(("grp", "section")), P("grp", "section")),
        check_vma=False,
    )
```

```python
import functools

import jax
import jax.numpy as jnp
import numpy as np
from jax import lax
from jax.experimental import pallas as pl
from jax.experimental.pallas import tpu as pltpu
from jax.sharding import PartitionSpec as P

epsilon = 1e-06
MIB = 1024 * 1024
SMALL_LIMIT = 12 * MIB
SLOTS = 6


def places(order):
    count = len(order)
    out = []
    for q in range(1 << count):
        out.append(sum(((q >> (count - 1 - k)) & 1) << bit for k, bit in enumerate(order)))
    return np.array(out, np.int32)


def exchange(x, mask, size):
    return lax.ppermute(x, "section", [(i, i ^ mask) for i in range(size)])


def settings(flops, bytes_moved, limit=SMALL_LIMIT):
    return dict(
        compiler_params=pltpu.CompilerParams(vmem_limit_bytes=limit),
        cost_estimate=pl.CostEstimate(flops=flops, bytes_accessed=bytes_moved, transcendentals=0),
    )


ANYWHERE = pl.BlockSpec(memory_space=pl.ANY)
IN_VMEM = pl.BlockSpec(memory_space=pltpu.VMEM)
IN_SMEM = pl.BlockSpec(memory_space=pltpu.SMEM)


vmem_out = pltpu.VMEM


def near(x):
    return pltpu.with_memory_space_constraint(x, pltpu.VMEM)


def stage_kernel(pieces, w_ref, after_ref, out_ref, token_ref, sems):
    copies = []
    for k, piece in enumerate(pieces):
        copies.append(pltpu.make_async_copy(w_ref.at[piece], out_ref.at[piece], sems.at[k]))
    for copy in copies:
        copy.start()
    token_ref[...] = jnp.ones_like(token_ref)
    for copy in copies:
        copy.wait()


def stage(w, after, half):
    pieces = []
    if w.ndim == 3:
        step = w.shape[1] // 8
        pieces = [(j, pl.ds(k * step, step)) for j in range(w.shape[0]) for k in range(8)]
    else:
        step = w.shape[0] // 16
        pieces = [pl.ds(k * step, step) for k in range(16)]
    return pl.pallas_call(
        functools.partial(stage_kernel, pieces),
        out_shape=(vmem_out(w.shape, w.dtype), jax.ShapeDtypeStruct((1, half), jnp.float32)),
        in_specs=[ANYWHERE, ANYWHERE],
        out_specs=(IN_VMEM, IN_VMEM),
        scratch_shapes=[pltpu.SemaphoreType.DMA((len(pieces),))],
        name="stage",
        **settings(0, w.size * 2),
    )(w, after)


def join_kernel(first, count, chunks, x_ref, w_ref, a_ref, b_ref):
    rows = w_ref.shape[1]
    half = rows // 2

    @pl.loop(0, count)
    def _(q):
        for s, out in enumerate((a_ref, b_ref)):
            column = pl.multiple_of(chunks[s, first + q] * rows + s * half, 128)
            total = jnp.dot(x_ref[:, :rows], w_ref[0, :, pl.ds(column, half)], preferred_element_type=jnp.float32)
            for j in (1, 2):
                total += jnp.dot(
                    x_ref[:, j * rows : (j + 1) * rows],
                    w_ref[j, :, pl.ds(column, half)],
                    preferred_element_type=jnp.float32,
                )
            out[q] = total


def join(chunks, first, count, x, w_fc):
    tokens = x.shape[0]
    rows = w_fc.shape[1]
    half = rows // 2
    out = vmem_out((count, tokens, half), jnp.float32)
    return pl.pallas_call(
        functools.partial(join_kernel, first, count),
        out_shape=(out, out),
        in_specs=[IN_SMEM, IN_VMEM, IN_VMEM],
        out_specs=(IN_VMEM, IN_VMEM),
        name="join",
        **settings(6 * tokens * rows * rows * count, 4 * tokens * rows * count),
    )(chunks, near(x), near(w_fc))


def head_kernel(first, count, chunks, a_ref, b_ref, w_ref, before_ref, out_ref, token_ref):
    half = a_ref.shape[2]
    out_ref[...] = before_ref[...]
    token_ref[...] = jnp.ones_like(token_ref)

    @pl.loop(0, count)
    def _(q):
        total = out_ref[...]
        for s, piece in enumerate((a_ref, b_ref)):
            row = pl.multiple_of(chunks[s, first + q] * (2 * half) + s * half, 128)
            total += jnp.dot(piece[q], w_ref[pl.ds(row, half), :], preferred_element_type=jnp.float32)
        out_ref[...] = total


def head(chunks, first, pieces, w_lm, before):
    count, tokens, half = pieces[0].shape
    share = w_lm.shape[1]
    return pl.pallas_call(
        functools.partial(head_kernel, first, count),
        out_shape=(vmem_out(before.shape, jnp.float32), vmem_out((1, half), jnp.float32)),
        in_specs=[IN_SMEM, IN_VMEM, IN_VMEM, IN_VMEM, IN_VMEM],
        out_specs=(IN_VMEM, IN_VMEM),
        name="head",
        **settings(4 * tokens * half * share * count, 8 * tokens * share),
    )(chunks, near(pieces[0]), near(pieces[1]), near(w_lm), near(before))


def back_kernel(first, count, chunks, d_ref, w_ref, a_ref, b_ref):
    half = a_ref.shape[2]

    @pl.loop(0, count)
    def _(q):
        for s, out in enumerate((a_ref, b_ref)):
            row = pl.multiple_of(chunks[s, first + q] * (2 * half) + s * half, 128)
            out[q] = lax.dot_general(
                d_ref[...],
                w_ref[pl.ds(row, half), :],
                (((1,), (1,)), ((), ())),
                preferred_element_type=jnp.float32,
            )


def back(chunks, first, count, dlogits, w_lm, half):
    tokens, share = dlogits.shape
    out = vmem_out((count, tokens, half), jnp.float32)
    return pl.pallas_call(
        functools.partial(back_kernel, first, count),
        out_shape=(out, out),
        in_specs=[IN_SMEM, IN_VMEM, IN_VMEM],
        out_specs=(IN_VMEM, IN_VMEM),
        name="back",
        **settings(4 * tokens * half * share * count, 8 * tokens * half * count),
    )(chunks, near(dlogits), near(w_lm))


def head_grad_kernel(first, count, aliased, chunks, a_ref, b_ref, d_ref, *rest):
    out_ref, token_ref, slots, sems = rest[1 + aliased :]
    half = a_ref.shape[2]
    token_ref[...] = jnp.ones_like(token_ref)
    started = []
    for q in range(count):
        for s, piece in enumerate((a_ref, b_ref)):
            slot = len(started) % SLOTS
            if len(started) >= SLOTS:
                started[-SLOTS].wait()
            row = pl.multiple_of(chunks[s, first + q] * (2 * half) + s * half, 128)
            slots[slot] = lax.dot_general(
                piece[q], d_ref[...], (((0,), (0,)), ((), ())), preferred_element_type=jnp.float32
            ).astype(slots.dtype)
            copy = pltpu.make_async_copy(slots.at[slot], out_ref.at[pl.ds(row, half), :], sems.at[slot])
            copy.start()
            started.append(copy)
    for copy in started[-SLOTS:]:
        copy.wait()


def head_grad(chunks, first, pieces, dlogits, width, after, into=None):
    count, tokens, half = pieces[0].shape
    share = dlogits.shape[1]
    aliased = into is not None
    extra = (into,) if aliased else ()
    return pl.pallas_call(
        functools.partial(head_grad_kernel, first, count, aliased),
        out_shape=(
            jax.ShapeDtypeStruct((width, share), jnp.bfloat16),
            jax.ShapeDtypeStruct((1, half), jnp.float32),
        ),
        in_specs=[IN_SMEM, IN_VMEM, IN_VMEM, IN_VMEM, ANYWHERE] + [ANYWHERE] * len(extra),
        out_specs=(ANYWHERE, IN_VMEM),
        scratch_shapes=[pltpu.VMEM((SLOTS, half, share), jnp.bfloat16), pltpu.SemaphoreType.DMA((SLOTS,))],
        input_output_aliases={5: 0} if aliased else {},
        name="head_grad",
        **settings(4 * tokens * half * share * count, 4 * half * share * count),
    )(chunks, near(pieces[0]), near(pieces[1]), near(dlogits), after, *extra)


def join_grad_kernel(first, count, aliased, chunks, a_ref, b_ref, x_ref, *rest):
    out_ref, token_ref, slots, sems = rest[aliased:]
    half = a_ref.shape[2]
    rows = 2 * half
    token_ref[...] = jnp.ones_like(token_ref)
    started = []
    for q in range(count):
        for s, piece in enumerate((a_ref, b_ref)):
            slot = len(started) % SLOTS
            if len(started) >= SLOTS:
                started[-SLOTS].wait()
            column = pl.multiple_of(chunks[s, first + q] * rows + s * half, 128)
            for j in range(3):
                slots[slot, j] = jnp.dot(
                    x_ref[j * rows : (j + 1) * rows, :], piece[q], preferred_element_type=jnp.float32
                ).astype(slots.dtype)
            copy = pltpu.make_async_copy(slots.at[slot], out_ref.at[:, :, pl.ds(column, half)], sems.at[slot])
            copy.start()
            started.append(copy)
    for copy in started[-SLOTS:]:
        copy.wait()


def join_grad(chunks, first, pieces, x_turned, width, into=None):
    count, tokens, half = pieces[0].shape
    rows = 2 * half
    aliased = into is not None
    extra = (into,) if aliased else ()
    return pl.pallas_call(
        functools.partial(join_grad_kernel, first, count, aliased),
        out_shape=(
            jax.ShapeDtypeStruct((3, rows, width), jnp.bfloat16),
            jax.ShapeDtypeStruct((1, half), jnp.float32),
        ),
        in_specs=[IN_SMEM, IN_VMEM, IN_VMEM, IN_VMEM] + [ANYWHERE] * len(extra),
        out_specs=(ANYWHERE, IN_VMEM),
        scratch_shapes=[pltpu.VMEM((SLOTS, 3, rows, half), jnp.bfloat16), pltpu.SemaphoreType.DMA((SLOTS,))],
        input_output_aliases={4: 0} if aliased else {},
        name="join_grad",
        **settings(12 * tokens * rows * rows * count, 6 * rows * rows * count),
    )(chunks, near(pieces[0]), near(pieces[1]), near(x_turned), *extra)


def cut(total, chunks, rows):
    tokens = total.shape[0]
    blocks = total.reshape(tokens, -1, 2, rows // 2).transpose(2, 1, 0, 3)
    parts = [jnp.take(blocks[s], chunks[s], axis=0) for s in range(2)]
    count = chunks.shape[1] // 2
    return [p[:count] for p in parts], [p[count:] for p in parts]


def whole(pieces, chunks):
    parts = [jnp.take(pieces[s], jnp.argsort(chunks[s]), axis=0) for s in range(2)]
    return jnp.concatenate(parts, axis=2).transpose(1, 0, 2).reshape(pieces[0].shape[1], -1)


def groups_of(bits):
    later = [list(range(at, min(at + 3, bits))) for at in range(1, bits, 3)]
    return later + [[0]]


def contributions(x, group, size):
    masks = [sum(1 << b for k, b in enumerate(group) if (m >> k) & 1) for m in range(1 << len(group))]
    return [x] + [exchange(x, m, size) for m in masks[1:]]


def tree_sum(items):
    while len(items) > 1:
        items = [items[k] + items[k + 1] for k in range(0, len(items), 2)]
    return items[0]


def merge_sums(items):
    peak = functools.reduce(jnp.maximum, [i[0] for i in items])
    shifts = [i[0] - peak for i in items]
    scales = [jnp.exp(s) for s in shifts]
    return jnp.stack(
        [
            peak,
            tree_sum([i[1] * c for i, c in zip(items, scales)]),
            tree_sum([(i[2] + i[1] * s) * c for i, s, c in zip(items, shifts, scales)]),
            tree_sum([i[3] for i in items]),
        ]
    )


def reduce_halves(low, high, orders, size, pack, unpack, work):
    received = [exchange(pack(high[s]), 1 << orders[s][0], size) for s in range(2)]
    token = None
    for k in range(1, len(orders[0])):
        half = low[0].shape[0] // 2
        arrived = [unpack(r, token) for r in received]
        high = [low[s][half:] + arrived[s][half:] for s in range(2)]
        received = [exchange(pack(high[s]), 1 << orders[s][k], size) for s in range(2)]
        low = [low[s][:half] + arrived[s][:half] for s in range(2)]
        token = work(k, high[0])
    return [low[s][0] + unpack(received[s], token)[0] for s in range(2)]


def gather_doubling(own, orders, size, work):
    held = [o[None] for o in own]
    fresh = held
    first = 0
    for k in range(len(orders[0]) - 1, -1, -1):
        arrived = [exchange(held[s], 1 << orders[s][k], size) for s in range(2)]
        token = work(first, fresh)
        first = held[0].shape[0]
        if k:
            if token is not None:
                arrived = [(a.astype(jnp.float32) * token[None]).astype(a.dtype) for a in arrived]
            held = [jnp.concatenate([held[s], arrived[s]], axis=0) for s in range(2)]
        fresh = arrived
    work(first, fresh)
    return held, fresh


HALF_SCALE = 2.0**20


def on_device(size, low_feat, mid_feat, high_feat, w_fc, gain, w_lm, targets):
    me = lax.axis_index("section")
    rows, full_width = w_fc.shape[1], w_fc.shape[2]
    share = w_lm.shape[1]
    tokens = targets.shape[0]
    half = rows // 2
    bits = size.bit_length() - 1
    count = size // 2
    orders = (list(range(bits)), [0, 2, 1] + list(range(3, bits)))
    chunks = jnp.asarray(np.stack([places(o) for o in orders])) ^ me
    kernels = half % 128 == 0

    sent = jnp.concatenate(
        [f.reshape(-1, size, rows) for f in (low_feat, mid_feat, high_feat)], axis=2
    ).transpose(1, 0, 2)
    x = lax.all_to_all(sent, "section", split_axis=0, concat_axis=0, tiled=True).reshape(tokens, 3 * rows)
    x_turned = x.T

    held = {}
    if kernels:
        near_fc, _ = stage(w_fc, sent, half)
        high = join(chunks, count, count, x, near_fc)
        low = join(chunks, 0, count, x, near_fc)
    else:
        total = jnp.dot(x, w_fc.reshape(3 * rows, full_width), preferred_element_type=jnp.float32)
        low, high = cut(total, chunks, rows)

    def bring_head(k, sent):
        if kernels and k == 1:
            held["lm"], token = stage(w_lm, sent, half)
            return token

    def plain(x, token):
        return x if token is None else x * token[None]

    joined = jnp.concatenate(
        reduce_halves(low, high, orders, size, lambda x: x, plain, bring_head), axis=1
    )

    squares = jnp.sum(joined * joined, axis=1)
    for group in groups_of(bits):
        squares = tree_sum(contributions(squares, group, size))
    inv_rms = lax.rsqrt(squares / full_width + epsilon)[:, None]
    normed = (joined * inv_rms * gain[None, :]).astype(jnp.bfloat16)

    held["logits"] = jnp.zeros((tokens, share), jnp.float32)

    def add_logits(first, pieces):
        if kernels:
            held["logits"], token = head(chunks, first, pieces, held["lm"], held["logits"])
            return token

    normed_low, normed_high = gather_doubling(
        [normed[:, :half], normed[:, half:]], orders, size, add_logits
    )
    if kernels:
        logits = held["logits"]
    else:
        normed_all = whole(
            [jnp.concatenate([normed_low[s], normed_high[s]], axis=0) for s in range(2)], chunks
        )
        logits = jnp.dot(normed_all, w_lm, preferred_element_type=jnp.float32)

    column = me * share + lax.iota(jnp.int32, share)
    is_target = column[None, :] == targets[:, None]
    peak = jnp.max(logits, axis=1)
    shifted = logits - peak[:, None]
    weight = jnp.exp(shifted)
    sums = jnp.stack(
        [
            peak,
            jnp.sum(weight, axis=1),
            jnp.sum(weight * shifted, axis=1),
            jnp.sum(jnp.where(is_target, logits, 0.0), axis=1),
        ]
    )
    for group in groups_of(bits):
        sums = merge_sums(contributions(sums, group, size))
    peak, exp_total, exp_moment, picked = sums
    log_total = peak + jnp.log(exp_total)
    token_loss = log_total - picked
    dlogits = (
        (jnp.exp(logits - log_total[:, None]) - is_target.astype(jnp.float32)) / tokens
    ).astype(jnp.bfloat16)
    rowdot = ((exp_moment / exp_total - (picked - peak)) / tokens)[:, None] / inv_rms

    if kernels:
        high = back(chunks, count, count, dlogits, held["lm"], half)
        low = back(chunks, 0, count, dlogits, held["lm"], half)
    else:
        total = lax.dot_general(
            dlogits, w_lm, (((1,), (1,)), ((), ())), preferred_element_type=jnp.float32
        )
        low, high = cut(total, chunks, rows)

    def fill_grad_lm(k, sent):
        if not kernels:
            return None
        if k == 1:
            held["grad_lm"], token = head_grad(chunks, 0, normed_low, dlogits, full_width, sent)
            return token
        if k == bits - 1:
            held["grad_lm"], token = head_grad(
                chunks, count, normed_high, dlogits, full_width, sent, held["grad_lm"]
            )
            return token

    scale = HALF_SCALE * (tokens / 128)

    def pack_half(x):
        return (x * scale).astype(jnp.float16)

    def unpack_half(x, token):
        wide = x.astype(jnp.float32) * (1.0 / scale)
        return wide if token is None else wide * token[None]

    dnormed = jnp.concatenate(
        reduce_halves(low, high, orders, size, pack_half, unpack_half, fill_grad_lm), axis=1
    )
    if kernels:
        grad_lm = held["grad_lm"]
    else:
        grad_lm = lax.dot_general(
            normed_all, dlogits, (((0,), (0,)), ((), ())), preferred_element_type=jnp.float32
        ).astype(jnp.bfloat16)

    grad_gain = jnp.sum(dnormed * joined * inv_rms, axis=0)
    dfused = (
        inv_rms * (dnormed * gain[None, :]) - joined * (inv_rms * inv_rms * inv_rms * rowdot / full_width)
    ).astype(jnp.bfloat16)

    held["grad_fc"] = None

    def fill_grad_fc(first, pieces):
        if kernels:
            held["grad_fc"], token = join_grad(chunks, first, pieces, x_turned, full_width, held["grad_fc"])
            return token

    dfused_low, dfused_high = gather_doubling(
        [dfused[:, :half], dfused[:, half:]], orders, size, fill_grad_fc
    )
    if kernels:
        grad_fc = held["grad_fc"]
    else:
        dfused_all = whole(
            [jnp.concatenate([dfused_low[s], dfused_high[s]], axis=0) for s in range(2)], chunks
        )
        grad_fc = jnp.dot(x_turned, dfused_all, preferred_element_type=jnp.float32).astype(jnp.bfloat16)
        grad_fc = grad_fc.reshape(3, rows, full_width)
    return (token_loss, grad_fc, grad_gain, grad_lm)


def solution(mesh):
    return jax.shard_map(
        functools.partial(on_device, mesh.shape["section"]),
        mesh=mesh,
        in_specs=(
            P(("grp", "section"), None),
            P(("grp", "section"), None),
            P(("grp", "section"), None),
            P(None, "section", None),
            P("section"),
            P(None, "section"),
            P("grp"),
        ),
        out_specs=(P("grp"), P("grp", "section", None), P(("grp", "section")), P("grp", "section")),
        check_vma=False,
    )
```

```python
import functools

import jax
import jax.numpy as jnp
import numpy as np
from jax import lax
from jax.experimental import pallas as pl
from jax.experimental.pallas import tpu as pltpu
from jax.sharding import PartitionSpec as P

epsilon = 1e-06
MIB = 1024 * 1024
HALF_SCALE = 2.0**20
TILE = 256


def reduce_places(bits):
    later = range(1, bits)
    low = [
        sum(((q >> (bits - 2 - k)) & 1) << bit for k, bit in enumerate(later)) for q in range(1 << (bits - 1))
    ]
    return low + [p + 1 for p in low]


def gather_rounds(bits):
    later = [[1, 2]] if bits > 2 else [[1]]
    at = 3
    while at < bits:
        later.append([at, at + 1] if at + 1 < bits and (bits - at) % 2 == 0 else [at])
        at += len(later[-1])
    return later[::-1]


def masks_of(group):
    return [sum(1 << b for k, b in enumerate(group) if (m >> k) & 1) for m in range(1, 1 << len(group))]


def gather_places(bits):
    held = [0]
    for group in gather_rounds(bits):
        held = held + [p ^ m for m in masks_of(group) for p in held]
    return held


def exchange(x, mask, size):
    return lax.ppermute(x, "section", [(i, i ^ mask) for i in range(size)])


def settings(flops, bytes_moved, limit):
    return dict(
        compiler_params=pltpu.CompilerParams(vmem_limit_bytes=limit),
        cost_estimate=pl.CostEstimate(flops=flops, bytes_accessed=bytes_moved, transcendentals=0),
    )


ANYWHERE = pl.BlockSpec(memory_space=pl.ANY)
IN_VMEM = pl.BlockSpec(memory_space=pltpu.VMEM)
IN_SMEM = pl.BlockSpec(memory_space=pltpu.SMEM)
vmem_out = pltpu.VMEM


def near(x):
    return pltpu.with_memory_space_constraint(x, pltpu.VMEM)


def far(x):
    return pltpu.with_memory_space_constraint(x, pltpu.HBM)


def stage_kernel(pieces, table, w_ref, after_ref, out_ref, token_ref, sems):
    copies = []
    for k, piece in enumerate(pieces):
        copies.append(pltpu.make_async_copy(w_ref.at[piece], out_ref.at[piece], sems.at[k]))
    for copy in copies:
        copy.start()
    token_ref[...] = jnp.ones_like(token_ref)
    for copy in copies:
        copy.wait()


def stage(table, w, after, rows):
    step = w.shape[0] // 16
    pieces = [pl.ds(k * step, step) for k in range(16)]
    return pl.pallas_call(
        functools.partial(stage_kernel, pieces),
        out_shape=(vmem_out(w.shape, w.dtype), vmem_out((1, rows), jnp.float32)),
        in_specs=[IN_SMEM, ANYWHERE, ANYWHERE],
        out_specs=(IN_VMEM, IN_VMEM),
        scratch_shapes=[pltpu.SemaphoreType.DMA((len(pieces),))],
        name="stage",
        **settings(0, w.size * 2, 2 * MIB),
    )(table, far(w), after)


def join_kernel(first, count, table, x_ref, w_ref, *rest):
    out_ref, slots, sems = rest[0], rest[-2], rest[-1]
    rows = w_ref.shape[1]

    def copy(q):
        column = pl.multiple_of(table[0, first + q] * rows, 128)
        return pltpu.make_async_copy(w_ref.at[:, :, pl.ds(column, rows)], slots.at[q], sems.at[q])

    for q in range(count):
        copy(q).start()
    if len(rest) == 4:
        rest[1][...] = x_ref[...].T

    @pl.loop(0, count)
    def _(q):
        copy(q).wait()
        for column in range(0, rows, TILE):
            total = jnp.dot(
                x_ref[:, :rows], slots[q, 0, :, column : column + TILE], preferred_element_type=jnp.float32
            )
            for j in (1, 2):
                total += jnp.dot(
                    x_ref[:, j * rows : (j + 1) * rows],
                    slots[q, j, :, column : column + TILE],
                    preferred_element_type=jnp.float32,
                )
            out_ref[q, :, column : column + TILE] = total


def join(table, first, count, x, w_fc, turn):
    tokens = x.shape[0]
    rows = w_fc.shape[1]
    shapes = [vmem_out((count, tokens, rows), jnp.float32)]
    if turn:
        shapes.append(jax.ShapeDtypeStruct(x.shape[::-1], x.dtype))
    return pl.pallas_call(
        functools.partial(join_kernel, first, count),
        out_shape=tuple(shapes),
        in_specs=[IN_SMEM, IN_VMEM, ANYWHERE],
        out_specs=(IN_VMEM,) * len(shapes),
        scratch_shapes=[pltpu.VMEM((count, 3, rows, rows), jnp.bfloat16), pltpu.SemaphoreType.DMA((count,))],
        name="join",
        **settings(6 * tokens * rows * rows * count, 6 * rows * rows * count, 20 * MIB),
    )(table, near(x), far(w_fc))


def columns_of(rows_of_stats):
    count, tokens = rows_of_stats.shape
    padded = jnp.concatenate([rows_of_stats, jnp.zeros((tokens - count, tokens), jnp.float32)], axis=0)
    return padded.T


def target_mask(table, targets_ref, share):
    column = table[0, 0] * share + lax.broadcasted_iota(jnp.int32, (targets_ref.shape[1], share), 1)
    return column == columns_of(targets_ref[...].astype(jnp.float32))[:, :1].astype(jnp.int32)


def head_kernel(first, count, last, table, piece_ref, w_ref, before_ref, targets_ref, out_ref, extra_ref):
    rows = piece_ref.shape[2]
    out_ref[...] = before_ref[...]

    @pl.loop(0, count)
    def _(q):
        row = pl.multiple_of(table[1, first + q] * rows, 128)
        out_ref[...] += jnp.dot(piece_ref[q], w_ref[pl.ds(row, rows), :], preferred_element_type=jnp.float32)

    if not last:
        extra_ref[...] = jnp.ones_like(extra_ref)
        return
    logits = out_ref[...]
    tokens, share = logits.shape
    peak = jnp.max(logits, axis=1, keepdims=True)
    shifted = logits - peak
    weight = jnp.exp(shifted)
    picked = jnp.where(target_mask(table, targets_ref, share), logits, 0.0)
    lane = lax.broadcasted_iota(jnp.int32, (tokens, tokens), 1)
    stats = jnp.where(lane == 0, peak, 0.0)
    for k, part in enumerate((weight, weight * shifted, picked)):
        stats = jnp.where(lane == k + 1, jnp.sum(part, axis=1, keepdims=True), stats)
    extra_ref[...] = stats.T[: extra_ref.shape[0]]


def head(table, first, piece, w_lm, before, targets, last):
    count, tokens, rows = piece.shape
    share = w_lm.shape[1]
    extra = (8, tokens) if last else (1, rows)
    return pl.pallas_call(
        functools.partial(head_kernel, first, count, last),
        out_shape=(vmem_out(before.shape, jnp.float32), vmem_out(extra, jnp.float32)),
        in_specs=[IN_SMEM] + [IN_VMEM] * 4,
        out_specs=(IN_VMEM, IN_VMEM),
        name="head",
        **settings(2 * tokens * rows * share * count, 8 * tokens * share, 6 * MIB),
    )(table, near(piece), near(w_lm), near(before), near(targets))


def back_products(first, count, table, d_ref, w_ref, out_ref):
    rows = out_ref.shape[2]

    @pl.loop(0, count)
    def _(q):
        row = pl.multiple_of(table[0, first + q] * rows, 128)
        for step in range(0, rows, TILE):
            out_ref[q, :, step : step + TILE] = lax.dot_general(
                d_ref[...],
                w_ref[pl.ds(row + step, TILE), :],
                (((1,), (1,)), ((), ())),
                preferred_element_type=jnp.float32,
            )


def back_first_kernel(first, count, table, logits_ref, stats_ref, targets_ref, w_ref, out_ref, d_ref):
    logits = logits_ref[...]
    tokens, share = logits.shape
    log_total = columns_of(stats_ref[...])[:, :1]
    hit = jnp.where(target_mask(table, targets_ref, share), 1.0, 0.0)
    d_ref[...] = ((jnp.exp(logits - log_total) - hit) / tokens).astype(d_ref.dtype)
    back_products(first, count, table, d_ref, w_ref, out_ref)


def back_first(table, first, count, logits, stats, targets, w_lm, rows):
    tokens, share = logits.shape
    return pl.pallas_call(
        functools.partial(back_first_kernel, first, count),
        out_shape=(vmem_out((count, tokens, rows), jnp.float32), vmem_out((tokens, share), jnp.bfloat16)),
        in_specs=[IN_SMEM] + [IN_VMEM] * 4,
        out_specs=(IN_VMEM, IN_VMEM),
        name="back_first",
        **settings(2 * tokens * rows * share * count, 4 * tokens * rows * count, 6 * MIB),
    )(table, near(logits), near(stats), near(targets), near(w_lm))


def back_rest_kernel(first, count, table, d_ref, w_ref, out_ref):
    back_products(first, count, table, d_ref, w_ref, out_ref)


def back_rest(table, first, count, dlogits, w_lm, rows):
    tokens, share = dlogits.shape
    return pl.pallas_call(
        functools.partial(back_rest_kernel, first, count),
        out_shape=vmem_out((count, tokens, rows), jnp.float32),
        in_specs=[IN_SMEM, IN_VMEM, IN_VMEM],
        out_specs=IN_VMEM,
        name="back_rest",
        **settings(2 * tokens * rows * share * count, 4 * tokens * rows * count, 6 * MIB),
    )(table, near(dlogits), near(w_lm))


def head_grad_kernel(first, counts, aliased, table, a_ref, b_ref, d_ref, *rest):
    out_ref, token_ref, slots, sems = rest[1 + aliased :]
    rows = a_ref.shape[2]
    share = d_ref.shape[1]
    token_ref[...] = jnp.ones_like(token_ref)

    def copy(at):
        row = pl.multiple_of(table[1, first + at] * rows, 128)
        return pltpu.make_async_copy(slots.at[at], out_ref.at[pl.ds(row, rows), :], sems.at[at])

    for piece, offset, count in ((a_ref, 0, counts[0]), (b_ref, counts[0], counts[1])):

        @pl.loop(0, count)
        def _(q):
            turned = piece[q].T
            for column in range(0, share, TILE):
                for row in range(0, rows, TILE):
                    slots[offset + q, row : row + TILE, column : column + TILE] = jnp.dot(
                        turned[row : row + TILE],
                        d_ref[:, column : column + TILE],
                        preferred_element_type=jnp.float32,
                    ).astype(slots.dtype)
            copy(offset + q).start()

    for at in range(sum(counts)):
        copy(at).wait()


def head_grad(table, first, a, b, dlogits, width, after, into=None):
    tokens, rows = a.shape[1:]
    counts = (a.shape[0], b.shape[0])
    share = dlogits.shape[1]
    aliased = into is not None
    extra = (into,) if aliased else ()
    blocks = sum(counts)
    return pl.pallas_call(
        functools.partial(head_grad_kernel, first, counts, aliased),
        out_shape=(
            jax.ShapeDtypeStruct((width, share), jnp.bfloat16),
            vmem_out((1, rows), jnp.float32),
        ),
        in_specs=[IN_SMEM, IN_VMEM, IN_VMEM, IN_VMEM, ANYWHERE] + [ANYWHERE] * len(extra),
        out_specs=(ANYWHERE, IN_VMEM),
        scratch_shapes=[pltpu.VMEM((blocks, rows, share), jnp.bfloat16), pltpu.SemaphoreType.DMA((blocks,))],
        input_output_aliases={5: 0} if aliased else {},
        name="head_grad",
        **settings(2 * tokens * rows * share * blocks, 2 * rows * share * blocks, 16 * MIB),
    )(table, near(a), near(b), near(dlogits), after, *extra)


def join_grad_kernel(first, count, aliased, table, piece_ref, x_ref, *rest):
    out_ref, token_ref, slots, sems = rest[aliased:]
    rows = piece_ref.shape[2]
    token_ref[...] = jnp.ones_like(token_ref)

    def copy(at):
        column = pl.multiple_of(table[1, first + at] * rows, 128)
        return pltpu.make_async_copy(slots.at[at], out_ref.at[:, :, pl.ds(column, rows)], sems.at[at])

    @pl.loop(0, count)
    def _(q):
        for column in range(0, rows, TILE):
            for j in range(3):
                for row in range(0, rows, TILE):
                    slots[q, j, row : row + TILE, column : column + TILE] = jnp.dot(
                        x_ref[j * rows + row : j * rows + row + TILE, :],
                        piece_ref[q, :, column : column + TILE],
                        preferred_element_type=jnp.float32,
                    ).astype(slots.dtype)
        copy(q).start()

    for at in range(count):
        copy(at).wait()


def join_grad(table, first, piece, x_turned, width, into=None):
    count, tokens, rows = piece.shape
    aliased = into is not None
    extra = (into,) if aliased else ()
    return pl.pallas_call(
        functools.partial(join_grad_kernel, first, count, aliased),
        out_shape=(
            jax.ShapeDtypeStruct((3, rows, width), jnp.bfloat16),
            vmem_out((1, rows), jnp.float32),
        ),
        in_specs=[IN_SMEM, IN_VMEM, IN_VMEM] + [ANYWHERE] * len(extra),
        out_specs=(ANYWHERE, IN_VMEM),
        scratch_shapes=[pltpu.VMEM((count, 3, rows, rows), jnp.bfloat16), pltpu.SemaphoreType.DMA((count,))],
        input_output_aliases={3: 0} if aliased else {},
        name="join_grad",
        **settings(6 * tokens * rows * rows * count, 6 * rows * rows * count, 20 * MIB),
    )(table, near(piece), near(x_turned), *extra)


def cut(total, chunks, rows):
    tokens = total.shape[0]
    blocks = jnp.take(total.reshape(tokens, -1, rows).transpose(1, 0, 2), chunks, axis=0)
    count = chunks.shape[0] // 2
    return blocks[:count], blocks[count:]


def whole(pieces, chunks):
    blocks = jnp.take(jnp.concatenate(pieces, axis=0), jnp.argsort(chunks), axis=0)
    return blocks.transpose(1, 0, 2).reshape(blocks.shape[1], -1)


def contributions(x, group, size):
    return [x] + [exchange(x, m, size) for m in masks_of(group)]


def tree_sum(items):
    while len(items) > 1:
        items = [items[k] + items[k + 1] for k in range(0, len(items), 2)]
    return items[0]


def merge_sums(items):
    peak = functools.reduce(jnp.maximum, [i[0:1] for i in items])
    shifts = [i[0:1] - peak for i in items]
    scales = [jnp.exp(s) for s in shifts]
    return jnp.concatenate(
        [
            peak,
            tree_sum([i[1:2] * c for i, c in zip(items, scales)]),
            tree_sum([(i[2:3] + i[1:2] * s) * c for i, s, c in zip(items, shifts, scales)]),
            tree_sum([i[3:4] for i in items]),
        ],
        axis=0,
    )


def with_token(x, token):
    return x if token is None else (x.astype(jnp.float32) * token).astype(x.dtype)


def reduce_halves(low, high, bits, size, pack, unpack, work):
    received = exchange(pack(high), 1, size)
    total = low + unpack(received)
    count, tokens, rows = total.shape
    half = rows // 2
    total = total.reshape(2, 2, count // 4, tokens, rows)
    a, b = total[..., :half], total[..., half:]
    send_a, send_b = a[1], b[:, 1]
    got_a, got_b = exchange(pack(send_a), 2, size), exchange(pack(send_b), 4, size)
    token = work(1, send_a)
    a = a[0] + with_token(unpack(got_a), None if token is None else token[:, :half])
    b = b[:, 0] + unpack(got_b)
    got_a, got_b = exchange(pack(a[1]), 4, size), exchange(pack(b[1]), 2, size)
    a, b = a[0] + unpack(got_a), b[0] + unpack(got_b)
    total = jnp.concatenate([a, b], axis=-1)
    for bit in range(3, bits):
        half_count = total.shape[0] // 2
        send = total[half_count:]
        got = exchange(pack(send), 1 << bit, size)
        token = work(bit, send)
        total = total[:half_count] + with_token(unpack(got), token)
    return total[0]


def gather(own, bits, size, work):
    held = own[None]
    rounds = gather_rounds(bits)
    token = None
    first = 0
    fresh = held
    across = []
    for at, group in enumerate(rounds):
        pieces = [exchange(held, m, size) for m in masks_of(group)]
        token = work(first, fresh, False)
        if at == len(rounds) - 1 and at > 0:
            across.append(exchange(held, 1, size))
            token = work(size // 2, across[0], False)
        first += fresh.shape[0]
        fresh = with_token(pieces[0] if len(pieces) == 1 else jnp.concatenate(pieces, axis=0), token)
        if at < len(rounds) - 1:
            held = jnp.concatenate([held, fresh], axis=0)
    across.append(exchange(fresh, 1, size))
    work(first, fresh, False)
    work(size // 2 + first, across[-1], True)
    return [held, fresh], across


def on_device(size, low_feat, mid_feat, high_feat, w_fc, gain, w_lm, targets):
    me = lax.axis_index("section")
    rows, full_width = w_fc.shape[1], w_fc.shape[2]
    share = w_lm.shape[1]
    tokens = targets.shape[0]
    bits = size.bit_length() - 1
    count = size // 2
    gather_list = gather_places(bits)
    gather_list = gather_list + [p + 1 for p in gather_list]
    table = jnp.asarray(np.array([reduce_places(bits), gather_list], np.int32)) ^ me
    kernels = rows % TILE == 0
    target_row = targets.reshape(1, tokens)

    sent = jnp.concatenate(
        [f.reshape(-1, size, rows) for f in (low_feat, mid_feat, high_feat)], axis=2
    ).transpose(1, 0, 2)
    x = lax.all_to_all(sent, "section", split_axis=0, concat_axis=0, tiled=True).reshape(tokens, 3 * rows)

    held = {"logits": jnp.zeros((tokens, share), jnp.float32), "grad_lm": None, "grad_fc": None}
    if kernels:
        high, x_turned = join(table, count, count, x, w_fc, True)
        (low,) = join(table, 0, count, x, w_fc, False)
    else:
        total = jnp.dot(x, w_fc.reshape(3 * rows, full_width), preferred_element_type=jnp.float32)
        low, high = cut(total, table[0], rows)

    def bring_head(k, after):
        if kernels and k == 1:
            held["lm"], token = stage(table, w_lm, after, rows)
            return token

    joined = reduce_halves(low, high, bits, size, lambda x: x, lambda x: x, bring_head)

    squares = jnp.sum(joined * joined, axis=1)
    for group in gather_rounds(bits) + [[0]]:
        squares = tree_sum(contributions(squares, group, size))
    inv_rms = lax.rsqrt(squares / full_width + epsilon)[:, None]
    normed = (joined * inv_rms * gain[None, :]).astype(jnp.bfloat16)

    def add_logits(first, piece, last):
        if kernels:
            held["logits"], extra = head(table, first, piece, held["lm"], held["logits"], target_row, last)
            if last:
                held["stats"] = extra
            return extra

    normed_near, normed_across = gather(normed, bits, size, add_logits)
    logits = held["logits"]
    if kernels:
        stats = held["stats"][:4]
    else:
        normed_all = whole(normed_near + normed_across, table[1])
        logits = jnp.dot(normed_all, w_lm, preferred_element_type=jnp.float32)
        is_target = (me * share + lax.iota(jnp.int32, share))[None, :] == targets[:, None]
        peak = jnp.max(logits, axis=1)
        shifted = logits - peak[:, None]
        weight = jnp.exp(shifted)
        stats = jnp.stack(
            [
                peak,
                jnp.sum(weight, axis=1),
                jnp.sum(weight * shifted, axis=1),
                jnp.sum(jnp.where(is_target, logits, 0.0), axis=1),
            ]
        )
    for group in gather_rounds(bits) + [[0]]:
        stats = merge_sums(contributions(stats, group, size))
    peak, exp_total, exp_moment, picked = stats[0], stats[1], stats[2], stats[3]
    log_total = peak + jnp.log(exp_total)
    token_loss = log_total - picked
    rowdot = ((exp_moment / exp_total - (picked - peak)) / tokens)[:, None] / inv_rms

    if kernels:
        spread = jnp.broadcast_to(log_total[None], (8, tokens))
        high, dlogits = back_first(table, count, count, logits, spread, target_row, held["lm"], rows)
        low = back_rest(table, 0, count, dlogits, held["lm"], rows)
    else:
        dlogits = (
            (jnp.exp(logits - log_total[:, None]) - is_target.astype(jnp.float32)) / tokens
        ).astype(jnp.bfloat16)
        total = lax.dot_general(
            dlogits, w_lm, (((1,), (1,)), ((), ())), preferred_element_type=jnp.float32
        )
        low, high = cut(total, table[0], rows)

    def fill_grad_lm(k, after):
        if kernels and k in (1, bits - 1):
            at, pieces = (0, normed_near) if k == 1 else (count, normed_across)
            held["grad_lm"], token = head_grad(
                table, at, *pieces, dlogits, full_width, after, held["grad_lm"]
            )
            return token

    scale = HALF_SCALE * (tokens / 128)

    def pack_half(x):
        return (x * scale).astype(jnp.float16)

    def unpack_half(x):
        return x.astype(jnp.float32) * (1.0 / scale)

    dnormed = reduce_halves(low, high, bits, size, pack_half, unpack_half, fill_grad_lm)
    if kernels:
        grad_lm = held["grad_lm"]
    else:
        grad_lm = lax.dot_general(
            normed_all, dlogits, (((0,), (0,)), ((), ())), preferred_element_type=jnp.float32
        ).astype(jnp.bfloat16)

    grad_gain = jnp.sum(dnormed * joined * inv_rms, axis=0)
    dfused = (
        inv_rms * (dnormed * gain[None, :]) - joined * (inv_rms * inv_rms * inv_rms * rowdot / full_width)
    ).astype(jnp.bfloat16)

    def fill_grad_fc(first, piece, last):
        if kernels:
            held["grad_fc"], token = join_grad(table, first, piece, x_turned, full_width, held["grad_fc"])
            return token

    dfused_near, dfused_across = gather(dfused, bits, size, fill_grad_fc)
    if kernels:
        grad_fc = held["grad_fc"]
    else:
        dfused_all = whole(dfused_near + dfused_across, table[1])
        grad_fc = jnp.dot(x.T, dfused_all, preferred_element_type=jnp.float32).astype(jnp.bfloat16)
        grad_fc = grad_fc.reshape(3, rows, full_width)
    return (token_loss, grad_fc, grad_gain, grad_lm)


def solution(mesh):
    return jax.shard_map(
        functools.partial(on_device, mesh.shape["section"]),
        mesh=mesh,
        in_specs=(
            P(("grp", "section"), None),
            P(("grp", "section"), None),
            P(("grp", "section"), None),
            P(None, "section", None),
            P("section"),
            P(None, "section"),
            P("grp"),
        ),
        out_specs=(P("grp"), P("grp", "section", None), P(("grp", "section")), P("grp", "section")),
        check_vma=False,
    )
```

```python
import functools

import jax
import jax.numpy as jnp
import numpy as np
from jax import lax
from jax.experimental import pallas as pl
from jax.experimental.pallas import tpu as pltpu
from jax.sharding import PartitionSpec as P

epsilon = 1e-06
MIB = 1024 * 1024
HALF_SCALE = 2.0**20
TILE = 256
DEPTH = 4


def reduce_places(bits, order):
    return [
        sum(((q >> (bits - 2 - k)) & 1) << bit for k, bit in enumerate(order)) for q in range(1 << (bits - 1))
    ]


def gather_places(bits):
    held = fresh = np.zeros((2, 1), np.int32)
    out, across = [], [fresh ^ 1]
    for bit in range(bits - 1, 2, -1):
        out.append(fresh)
        fresh = held ^ (1 << bit)
        across.append(fresh ^ 1)
        held = np.concatenate([held, fresh], axis=1)
    first = held ^ np.array([[4], [2]], np.int32)
    second = np.concatenate([held, first], axis=1) ^ np.array([[2], [4]], np.int32)
    out += [fresh, *across, first, first ^ 1, second, second ^ 1]
    places = np.concatenate([p.reshape(-1) for p in out])
    streams = np.concatenate([np.repeat(np.arange(2), p.shape[1]) for p in out])
    return places.astype(np.int32), streams.astype(np.int32)


def masks_of(group):
    return [sum(1 << b for k, b in enumerate(group) if (m >> k) & 1) for m in range(1, 1 << len(group))]


def sum_rounds(bits):
    return [[bit] for bit in range(bits - 1, 2, -1)] + [[1, 2], [0]]


def exchange(x, mask, size):
    return lax.ppermute(x, "section", [(i, i ^ mask) for i in range(size)])


def settings(flops, bytes_moved, limit):
    return dict(
        compiler_params=pltpu.CompilerParams(vmem_limit_bytes=limit),
        cost_estimate=pl.CostEstimate(flops=flops, bytes_accessed=bytes_moved, transcendentals=0),
    )


ANYWHERE = pl.BlockSpec(memory_space=pl.ANY)
IN_VMEM = pl.BlockSpec(memory_space=pltpu.VMEM)
IN_SMEM = pl.BlockSpec(memory_space=pltpu.SMEM)
vmem_out = pltpu.VMEM


def near(x):
    return pltpu.with_memory_space_constraint(x, pltpu.VMEM)


def far(x):
    return pltpu.with_memory_space_constraint(x, pltpu.HBM)


def stage_kernel(pieces, table, w_ref, after_ref, out_ref, token_ref, sems):
    copies = []
    for k, piece in enumerate(pieces):
        copies.append(pltpu.make_async_copy(w_ref.at[piece], out_ref.at[piece], sems.at[k]))
    for copy in copies:
        copy.start()
    token_ref[...] = jnp.ones_like(token_ref)
    for copy in copies:
        copy.wait()


def stage(table, w, after, rows):
    step = w.shape[0] // 16
    pieces = [pl.ds(k * step, step) for k in range(16)]
    return pl.pallas_call(
        functools.partial(stage_kernel, pieces),
        out_shape=(vmem_out(w.shape, w.dtype), vmem_out((1, rows), jnp.float32)),
        in_specs=[IN_SMEM, ANYWHERE, ANYWHERE],
        out_specs=(IN_VMEM, IN_VMEM),
        scratch_shapes=[pltpu.SemaphoreType.DMA((len(pieces),))],
        name="stage",
        **settings(0, w.size * 2, 2 * MIB),
    )(table, far(w), after)


def join_kernel(first, count, offset, table, x_ref, w_ref, after_ref, *rest):
    out_ref, token_ref, slots, sems = rest[0], rest[1], rest[-2], rest[-1]
    rows = w_ref.shape[1]
    width = slots.shape[3]
    half = width // 2
    middle = table.shape[1] // 2

    def copy(q):
        column = pl.multiple_of(table[0, first + q] * rows + offset, 128)
        return pltpu.make_async_copy(w_ref.at[:, :, pl.ds(column, width)], slots.at[q], sems.at[q])

    for q in range(min(DEPTH, count)):
        copy(q).start()
    token_ref[...] = jnp.ones_like(token_ref)
    if len(rest) == 5:
        rest[2][...] = x_ref[...].T

    @pl.loop(0, count)
    def _(q):
        copy(q).wait()

        @pl.when(q + DEPTH < count)
        def _():
            copy(q + DEPTH).start()

        total = jnp.dot(x_ref[:, :rows], slots[q, 0], preferred_element_type=jnp.float32)
        for j in (1, 2):
            total += jnp.dot(
                x_ref[:, j * rows : (j + 1) * rows], slots[q, j], preferred_element_type=jnp.float32
            )
        out_ref[0, q] = total[:, :half]
        out_ref[1, table[1, first + q] + (q // middle) * middle] = total[:, half:]


def join(table, first, count, offset, width, x, w_fc, after, turn):
    tokens = x.shape[0]
    rows = w_fc.shape[1]
    shapes = [vmem_out((2, count, tokens, width // 2), jnp.float32), vmem_out((1, width // 2), jnp.float32)]
    if turn:
        shapes.append(jax.ShapeDtypeStruct(x.shape[::-1], x.dtype))
    return pl.pallas_call(
        functools.partial(join_kernel, first, count, offset),
        out_shape=tuple(shapes),
        in_specs=[IN_SMEM, IN_VMEM, ANYWHERE, ANYWHERE],
        out_specs=(IN_VMEM,) * len(shapes),
        scratch_shapes=[pltpu.VMEM((count, 3, rows, width), jnp.bfloat16), pltpu.SemaphoreType.DMA((count,))],
        name="join",
        **settings(6 * tokens * rows * width * count, 6 * rows * width * count, 20 * MIB),
    )(table, near(x), far(w_fc), after)


def columns_of(rows_of_stats):
    count, tokens = rows_of_stats.shape
    padded = jnp.concatenate([rows_of_stats, jnp.zeros((tokens - count, tokens), jnp.float32)], axis=0)
    return padded.T


def target_mask(me, targets_ref, share):
    column = me * share + lax.broadcasted_iota(jnp.int32, (targets_ref.shape[1], share), 1)
    return column == columns_of(targets_ref[...].astype(jnp.float32))[:, :1].astype(jnp.int32)


def head_kernel(first, counts, last, starts, w_ref, before_ref, targets_ref, *rest):
    pieces, (out_ref, extra_ref) = rest[:-2], rest[-2:]
    width = pieces[0].shape[2]
    out_ref[...] = before_ref[...]
    at = first
    for piece_ref, count in zip(pieces, counts):

        @pl.loop(0, count)
        def _(q):
            row = pl.multiple_of(starts[at + q], 128)
            out_ref[...] += jnp.dot(piece_ref[q], w_ref[pl.ds(row, width), :], preferred_element_type=jnp.float32)

        at += count
    if not last:
        extra_ref[...] = jnp.ones_like(extra_ref)
        return
    logits = out_ref[...]
    tokens, share = logits.shape
    peak = jnp.max(logits, axis=1, keepdims=True)
    shifted = logits - peak
    weight = jnp.exp(shifted)
    picked = jnp.where(target_mask(starts[starts.shape[0] - 1], targets_ref, share), logits, 0.0)
    lane = lax.broadcasted_iota(jnp.int32, (tokens, tokens), 1)
    stats = jnp.where(lane == 0, peak, 0.0)
    for k, part in enumerate((weight, weight * shifted, picked)):
        stats = jnp.where(lane == k + 1, jnp.sum(part, axis=1, keepdims=True), stats)
    extra_ref[...] = stats.T[: extra_ref.shape[0]]


def head(starts, first, pieces, w_lm, before, targets, last):
    tokens, width = pieces[0].shape[1:]
    counts = tuple(p.shape[0] for p in pieces)
    share = w_lm.shape[1]
    extra = (8, tokens) if last else (1, width)
    return pl.pallas_call(
        functools.partial(head_kernel, first, counts, last),
        out_shape=(vmem_out(before.shape, jnp.float32), vmem_out(extra, jnp.float32)),
        in_specs=[IN_SMEM] + [IN_VMEM] * (3 + len(pieces)),
        out_specs=(IN_VMEM, IN_VMEM),
        name="head",
        **settings(2 * tokens * width * share * sum(counts), 8 * tokens * share, 6 * MIB),
    )(starts, near(w_lm), near(before), near(targets), *[near(p) for p in pieces])


def back_products(first, count, table, d_ref, w_ref, out_ref):
    width = out_ref.shape[3]

    @pl.loop(0, count)
    def _(q):
        row = pl.multiple_of(table[0, first + q] * (2 * width), 128)
        for stream, at in ((0, q), (1, table[1, first + q])):
            out_ref[stream, at] = lax.dot_general(
                d_ref[...],
                w_ref[pl.ds(row + stream * width, width), :],
                (((1,), (1,)), ((), ())),
                preferred_element_type=jnp.float32,
            )


def back_first_kernel(first, count, table, logits_ref, stats_ref, targets_ref, w_ref, out_ref, d_ref):
    logits = logits_ref[...]
    tokens, share = logits.shape
    log_total = columns_of(stats_ref[...])[:, :1]
    hit = jnp.where(target_mask(table[0, 0], targets_ref, share), 1.0, 0.0)
    d_ref[...] = ((jnp.exp(logits - log_total) - hit) / tokens).astype(d_ref.dtype)
    back_products(first, count, table, d_ref, w_ref, out_ref)


def back_first(table, first, count, logits, stats, targets, w_lm, width):
    tokens, share = logits.shape
    return pl.pallas_call(
        functools.partial(back_first_kernel, first, count),
        out_shape=(vmem_out((2, count, tokens, width), jnp.float32), vmem_out((tokens, share), jnp.bfloat16)),
        in_specs=[IN_SMEM] + [IN_VMEM] * 4,
        out_specs=(IN_VMEM, IN_VMEM),
        name="back_first",
        **settings(4 * tokens * width * share * count, 8 * tokens * width * count, 6 * MIB),
    )(table, near(logits), near(stats), near(targets), near(w_lm))


def back_rest_kernel(first, count, table, d_ref, w_ref, out_ref):
    back_products(first, count, table, d_ref, w_ref, out_ref)


def back_rest(table, first, count, dlogits, w_lm, width):
    tokens, share = dlogits.shape
    return pl.pallas_call(
        functools.partial(back_rest_kernel, first, count),
        out_shape=vmem_out((2, count, tokens, width), jnp.float32),
        in_specs=[IN_SMEM, IN_VMEM, IN_VMEM],
        out_specs=IN_VMEM,
        name="back_rest",
        **settings(4 * tokens * width * share * count, 8 * tokens * width * count, 6 * MIB),
    )(table, near(dlogits), near(w_lm))


def head_grad_kernel(first, counts, aliased, starts, d_ref, after_ref, *rest):
    pieces = rest[aliased : aliased + len(counts)]
    out_ref, token_ref, slots, sems = rest[-4:]
    width = pieces[0].shape[2]
    share = d_ref.shape[1]
    token_ref[...] = jnp.ones_like(token_ref)

    def copy(at):
        row = pl.multiple_of(starts[first + at], 128)
        return pltpu.make_async_copy(slots.at[at], out_ref.at[pl.ds(row, width), :], sems.at[at])

    offset = 0
    for piece_ref, count in zip(pieces, counts):

        @pl.loop(0, count)
        def _(q):
            turned = piece_ref[q].T
            for column in range(0, share, TILE):
                slots[offset + q, :, column : column + TILE] = jnp.dot(
                    turned, d_ref[:, column : column + TILE], preferred_element_type=jnp.float32
                ).astype(slots.dtype)
            copy(offset + q).start()

        offset += count

    for at in range(sum(counts)):
        copy(at).wait()


def head_grad(starts, first, pieces, dlogits, full_width, after, into):
    tokens, width = pieces[0].shape[1:]
    counts = tuple(p.shape[0] for p in pieces)
    share = dlogits.shape[1]
    extra = () if into is None else (into,)
    blocks = sum(counts)
    return pl.pallas_call(
        functools.partial(head_grad_kernel, first, counts, len(extra)),
        out_shape=(
            jax.ShapeDtypeStruct((full_width, share), jnp.bfloat16),
            vmem_out((1, width), jnp.float32),
        ),
        in_specs=[IN_SMEM, IN_VMEM, ANYWHERE] + [ANYWHERE] * len(extra) + [IN_VMEM] * len(pieces),
        out_specs=(ANYWHERE, IN_VMEM),
        scratch_shapes=[pltpu.VMEM((blocks, width, share), jnp.bfloat16), pltpu.SemaphoreType.DMA((blocks,))],
        input_output_aliases={3: 0} if extra else {},
        name="head_grad",
        **settings(2 * tokens * width * share * blocks, 2 * width * share * blocks, 14 * MIB),
    )(starts, near(dlogits), after, *extra, *[near(p) for p in pieces])


def join_grad_kernel(first, counts, aliased, starts, x_ref, *rest):
    pieces = rest[aliased : aliased + len(counts)]
    out_ref, token_ref, slots, sems = rest[-4:]
    rows, width = slots.shape[2:]
    token_ref[...] = jnp.ones_like(token_ref)

    def copy(at):
        column = pl.multiple_of(starts[first + at], 128)
        return pltpu.make_async_copy(slots.at[at], out_ref.at[:, :, pl.ds(column, width)], sems.at[at])

    offset = 0
    for piece_ref, count in zip(pieces, counts):

        @pl.loop(0, count)
        def _(q):
            for j in range(3):
                for row in range(0, rows, TILE):
                    slots[offset + q, j, row : row + TILE, :] = jnp.dot(
                        x_ref[j * rows + row : j * rows + row + TILE, :],
                        piece_ref[q],
                        preferred_element_type=jnp.float32,
                    ).astype(slots.dtype)
            copy(offset + q).start()

        offset += count

    for at in range(sum(counts)):
        copy(at).wait()


def join_grad(starts, first, pieces, x_turned, full_width, into):
    tokens, width = pieces[0].shape[1:]
    rows = x_turned.shape[0] // 3
    counts = tuple(p.shape[0] for p in pieces)
    extra = () if into is None else (into,)
    blocks = sum(counts)
    return pl.pallas_call(
        functools.partial(join_grad_kernel, first, counts, len(extra)),
        out_shape=(
            jax.ShapeDtypeStruct((3, rows, full_width), jnp.bfloat16),
            vmem_out((1, width), jnp.float32),
        ),
        in_specs=[IN_SMEM, IN_VMEM] + [ANYWHERE] * len(extra) + [IN_VMEM] * len(pieces),
        out_specs=(ANYWHERE, IN_VMEM),
        scratch_shapes=[pltpu.VMEM((blocks, 3, rows, width), jnp.bfloat16), pltpu.SemaphoreType.DMA((blocks,))],
        input_output_aliases={2: 0} if extra else {},
        name="join_grad",
        **settings(6 * tokens * rows * width * blocks, 6 * rows * width * blocks, 14 * MIB),
    )(starts, near(x_turned), *extra, *[near(p) for p in pieces])


def cut(total, table, rows, offset, width):
    tokens = total.shape[0]
    blocks = jnp.take(total.reshape(tokens, -1, rows).transpose(1, 0, 2), table[0], axis=0)
    count = table.shape[1] // 2
    blocks = blocks[:, :, offset : offset + width].reshape(2, count, tokens, 2, width // 2)
    out = []
    for side in range(2):
        second = jnp.take(blocks[side, :, :, 1], jnp.argsort(table[1, side * count : (side + 1) * count]), axis=0)
        out.append(jnp.stack([blocks[side, :, :, 0], second]))
    return out


def whole(pieces, starts):
    blocks = jnp.take(jnp.concatenate(pieces, axis=0), jnp.argsort(starts[:-1]), axis=0)
    return blocks.transpose(1, 0, 2).reshape(blocks.shape[1], -1)


def contributions(x, group, size):
    return [x] + [exchange(x, m, size) for m in masks_of(group)]


def tree_sum(items):
    while len(items) > 1:
        items = [items[k] + items[k + 1] for k in range(0, len(items), 2)]
    return items[0]


def merge_sums(items):
    peak = functools.reduce(jnp.maximum, [i[0:1] for i in items])
    shifts = [i[0:1] - peak for i in items]
    scales = [jnp.exp(s) for s in shifts]
    return jnp.concatenate(
        [
            peak,
            tree_sum([i[1:2] * c for i, c in zip(items, scales)]),
            tree_sum([(i[2:3] + i[1:2] * s) * c for i, s, c in zip(items, shifts, scales)]),
            tree_sum([i[3:4] for i in items]),
        ],
        axis=0,
    )


def with_token(x, token):
    return x if token is None else (x.astype(jnp.float32) * token).astype(x.dtype)


def reduce_halves(low, high, bits, size, pack, unpack, work):
    total = low + unpack(exchange(pack(high), 1, size))
    streams = [total[0], total[1]]
    for k, order in ((1, (1, 2)), (2, (2, 1))):
        half = streams[0].shape[0] // 2
        sent = [t[half:] for t in streams]
        got = [exchange(pack(t), 1 << bit, size) for t, bit in zip(sent, order)]
        token = work(k, sent[0])
        streams = [t[:half] + with_token(unpack(g), token) for t, g in zip(streams, got)]
    total = jnp.stack(streams)
    for bit in range(3, bits):
        half = total.shape[1] // 2
        sent = total[:, half:]
        got = exchange(pack(sent), 1 << bit, size)
        token = work(bit, sent)
        total = total[:, :half] + with_token(unpack(got), token)
    return [total[0, 0], total[1, 0]]


def gather(own, bits, size, work):
    def flat(x):
        return x.reshape((-1,) + x.shape[2:])

    held = fresh = jnp.stack(own)[:, None]
    across = [exchange(fresh, 1, size)]
    for bit in range(bits - 1, 2, -1):
        arrived = exchange(held, 1 << bit, size)
        token = work([flat(fresh)], False)
        fresh = with_token(arrived, token)
        across.append(exchange(fresh, 1, size))
        held = jnp.concatenate([held, fresh], axis=1)
    first = [exchange(held[0], 4, size), exchange(held[1], 2, size)]
    token = work([flat(fresh)] + [flat(a) for a in across], False)
    first = with_token(jnp.stack(first), token)
    across = exchange(first, 1, size)
    both = jnp.concatenate([held, first], axis=1)
    second = [exchange(both[0], 2, size), exchange(both[1], 4, size)]
    token = work([flat(first), flat(across)], False)
    second = with_token(jnp.stack(second), token)
    across = exchange(second, 1, size)
    work([flat(second)], False)
    work([flat(across)], True)


def on_device(size, low_feat, mid_feat, high_feat, w_fc, gain, w_lm, targets):
    me = lax.axis_index("section")
    rows, full_width = w_fc.shape[1], w_fc.shape[2]
    share = w_lm.shape[1]
    tokens = targets.shape[0]
    half = rows // 2
    bits = size.bit_length() - 1
    count = size // 2
    first_order = reduce_places(bits, [1, 2] + list(range(3, bits)))
    second_order = reduce_places(bits, [2, 1] + list(range(3, bits)))
    where = [second_order.index(p) for p in first_order]
    chunks = jnp.asarray(np.array(first_order + [p + 1 for p in first_order], np.int32)) ^ me
    table = jnp.stack([chunks, jnp.asarray(np.array(where + where, np.int32))])
    places, streams = gather_places(bits)
    starts = jnp.concatenate([(jnp.asarray(places) ^ me) * rows + jnp.asarray(streams * half), me[None]])
    kernels = half % TILE == 0
    target_row = targets.reshape(1, tokens)

    sent = jnp.concatenate(
        [f.reshape(-1, size, rows) for f in (low_feat, mid_feat, high_feat)], axis=2
    ).transpose(1, 0, 2)
    x = lax.all_to_all(sent, "section", split_axis=0, concat_axis=0, tiled=True).reshape(tokens, 3 * rows)

    held = {"logits": jnp.zeros((tokens, share), jnp.float32), "grad_lm": None, "grad_fc": None}
    if not kernels:
        total = jnp.dot(x, w_fc.reshape(3 * rows, full_width), preferred_element_type=jnp.float32)

    if kernels:
        high, _, held["x"] = join(table, count, count, 0, rows, x, w_fc, sent, True)
        low, _ = join(table, 0, count, 0, rows, x, w_fc, sent, False)
    else:
        low, high = cut(total, table, rows, 0, rows)

    def bring_head(k, after):
        if kernels and k == 1:
            held["lm"], token = stage(table, w_lm, after, half)
            return token

    joined = jnp.concatenate(
        reduce_halves(low, high, bits, size, lambda x: x, lambda x: x, bring_head), axis=1
    )

    squares = jnp.sum(joined * joined, axis=1)
    for group in sum_rounds(bits):
        squares = tree_sum(contributions(squares, group, size))
    inv_rms = lax.rsqrt(squares / full_width + epsilon)[:, None]
    normed = (joined * inv_rms * gain[None, :]).astype(jnp.bfloat16)

    all_normed, all_dfused = [], []

    def add_logits(pieces, last):
        first = sum(p.shape[0] for p in all_normed)
        all_normed.extend(pieces)
        if kernels:
            held["logits"], extra = head(starts, first, pieces, held["lm"], held["logits"], target_row, last)
            if last:
                held["stats"] = extra
            return extra

    gather([normed[:, :half], normed[:, half:]], bits, size, add_logits)
    logits = held["logits"]
    if kernels:
        stats = held["stats"][:4]
    else:
        normed_all = whole(all_normed, starts)
        logits = jnp.dot(normed_all, w_lm, preferred_element_type=jnp.float32)
        is_target = (me * share + lax.iota(jnp.int32, share))[None, :] == targets[:, None]
        peak = jnp.max(logits, axis=1)
        shifted = logits - peak[:, None]
        weight = jnp.exp(shifted)
        stats = jnp.stack(
            [
                peak,
                jnp.sum(weight, axis=1),
                jnp.sum(weight * shifted, axis=1),
                jnp.sum(jnp.where(is_target, logits, 0.0), axis=1),
            ]
        )
    for group in sum_rounds(bits):
        stats = merge_sums(contributions(stats, group, size))
    peak, exp_total, exp_moment, picked = stats[0], stats[1], stats[2], stats[3]
    log_total = peak + jnp.log(exp_total)
    token_loss = log_total - picked
    rowdot = ((exp_moment / exp_total - (picked - peak)) / tokens)[:, None] / inv_rms

    if kernels:
        spread = jnp.broadcast_to(log_total[None], (8, tokens))
        high, dlogits = back_first(table, count, count, logits, spread, target_row, held["lm"], half)
        low = back_rest(table, 0, count, dlogits, held["lm"], half)
    else:
        dlogits = (
            (jnp.exp(logits - log_total[:, None]) - is_target.astype(jnp.float32)) / tokens
        ).astype(jnp.bfloat16)
        total = lax.dot_general(
            dlogits, w_lm, (((1,), (1,)), ((), ())), preferred_element_type=jnp.float32
        )
        low, high = cut(total, table, rows, 0, rows)

    def fill_grad_lm(k, after):
        if kernels and k in (1, bits - 1):
            middle = len(all_normed) - 2
            pieces = all_normed[:middle] if k == 1 else all_normed[middle:]
            first = 0 if k == 1 else sum(p.shape[0] for p in all_normed[:middle])
            held["grad_lm"], token = head_grad(
                starts, first, pieces, dlogits, full_width, after, held["grad_lm"]
            )
            return token

    scale = HALF_SCALE * (tokens / 128)

    def pack_half(x):
        return (x * scale).astype(jnp.float16)

    def unpack_half(x):
        return x.astype(jnp.float32) * (1.0 / scale)

    dnormed = jnp.concatenate(
        reduce_halves(low, high, bits, size, pack_half, unpack_half, fill_grad_lm), axis=1
    )
    if kernels:
        grad_lm = held["grad_lm"]
    else:
        grad_lm = lax.dot_general(
            normed_all, dlogits, (((0,), (0,)), ((), ())), preferred_element_type=jnp.float32
        ).astype(jnp.bfloat16)

    grad_gain = jnp.sum(dnormed * joined * inv_rms, axis=0)
    dfused = (
        inv_rms * (dnormed * gain[None, :]) - joined * (inv_rms * inv_rms * inv_rms * rowdot / full_width)
    ).astype(jnp.bfloat16)

    def fill_grad_fc(pieces, last):
        first = sum(p.shape[0] for p in all_dfused)
        all_dfused.extend(pieces)
        if kernels:
            held["grad_fc"], token = join_grad(starts, first, pieces, held["x"], full_width, held["grad_fc"])
            return token

    gather([dfused[:, :half], dfused[:, half:]], bits, size, fill_grad_fc)
    if kernels:
        grad_fc = held["grad_fc"]
    else:
        grad_fc = jnp.dot(x.T, whole(all_dfused, starts), preferred_element_type=jnp.float32)
        grad_fc = grad_fc.astype(jnp.bfloat16).reshape(3, rows, full_width)
    return (token_loss, grad_fc, grad_gain, grad_lm)


def solution(mesh):
    return jax.shard_map(
        functools.partial(on_device, mesh.shape["section"]),
        mesh=mesh,
        in_specs=(
            P(("grp", "section"), None),
            P(("grp", "section"), None),
            P(("grp", "section"), None),
            P(None, "section", None),
            P("section"),
            P(None, "section"),
            P("grp"),
        ),
        out_specs=(P("grp"), P("grp", "section", None), P(("grp", "section")), P("grp", "section")),
        check_vma=False,
    )
```

```python
import functools

import jax
import jax.numpy as jnp
import numpy as np
from jax import lax
from jax.experimental import pallas as pl
from jax.experimental.pallas import tpu as pltpu
from jax.sharding import PartitionSpec as P

epsilon = 1e-06
MIB = 1024 * 1024
HALF_SCALE = 2.0**20
TILE = 256


def reduce_places(bits, order):
    return [
        sum(((q >> (bits - 2 - k)) & 1) << bit for k, bit in enumerate(order)) for q in range(1 << (bits - 1))
    ]


def gather_places(bits):
    held = fresh = np.array([[0, 1 << (bits - 1)]] * 2, np.int32)
    out, across = [held], []
    for bit in range(bits - 2, 2, -1):
        across.append(fresh ^ 1)
        fresh = held ^ (1 << bit)
        held = np.concatenate([held, fresh], axis=1)
        out.append(fresh)
    first = held ^ np.array([[4], [2]], np.int32)
    second = np.concatenate([held, first], axis=1) ^ np.array([[2], [4]], np.int32)
    out += [*across, fresh ^ 1, first, first ^ 1, second, second ^ 1]
    places = np.concatenate([p.reshape(-1) for p in out])
    streams = np.concatenate([np.repeat(np.arange(2), p.shape[1]) for p in out])
    return places.astype(np.int32), streams.astype(np.int32)


def masks_of(group):
    return [sum(1 << b for k, b in enumerate(group) if (m >> k) & 1) for m in range(1, 1 << len(group))]


def sum_rounds(top):
    return [[bit] for bit in range(top - 1, 2, -1)] + [[1, 2], [0]]


def exchange(x, mask, size):
    return lax.ppermute(x, "section", [(i, i ^ mask) for i in range(size)])


def settings(flops, bytes_moved, limit):
    return dict(
        compiler_params=pltpu.CompilerParams(vmem_limit_bytes=limit),
        cost_estimate=pl.CostEstimate(flops=flops, bytes_accessed=bytes_moved, transcendentals=0),
    )


ANYWHERE = pl.BlockSpec(memory_space=pl.ANY)
IN_VMEM = pl.BlockSpec(memory_space=pltpu.VMEM)
IN_SMEM = pl.BlockSpec(memory_space=pltpu.SMEM)
vmem_out = pltpu.VMEM


def near(x):
    return pltpu.with_memory_space_constraint(x, pltpu.VMEM)


def far(x):
    return pltpu.with_memory_space_constraint(x, pltpu.HBM)


def stage_kernel(pieces, w_ref, after_ref, out_ref, token_ref, sems):
    copies = []
    for k, piece in enumerate(pieces):
        copies.append(pltpu.make_async_copy(w_ref.at[piece], out_ref.at[piece], sems.at[k]))
    for copy in copies:
        copy.start()
    token_ref[...] = jnp.ones_like(token_ref)
    for copy in copies:
        copy.wait()


def stage(w, after, rows):
    step = w.shape[0] // 16
    pieces = [pl.ds(k * step, step) for k in range(16)]
    return pl.pallas_call(
        functools.partial(stage_kernel, pieces),
        out_shape=(vmem_out(w.shape, w.dtype), vmem_out((1, rows), jnp.float32)),
        in_specs=[ANYWHERE, ANYWHERE],
        out_specs=(IN_VMEM, IN_VMEM),
        scratch_shapes=[pltpu.SemaphoreType.DMA((len(pieces),))],
        name="stage",
        **settings(0, w.size * 2, 2 * MIB),
    )(far(w), after)


def join_kernel(first, count, order, x_ref, w_ref, after_ref, *rest):
    out_ref, token_ref, slots, sems = rest[0], rest[1], rest[-2], rest[-1]
    rows = w_ref.shape[1]
    width = slots.shape[3]

    def copy(q, s):
        column = pl.multiple_of(order[s, first + q], 128)
        at = 2 * q + s
        return pltpu.make_async_copy(w_ref.at[:, :, pl.ds(column, width)], slots.at[at], sems.at[at])

    for q in range(count):
        for s in range(2):
            copy(q, s).start()
    token_ref[...] = jnp.ones_like(token_ref)
    if len(rest) == 5:
        rest[2][...] = x_ref[...].T

    @pl.loop(0, count)
    def _(q):
        for s in range(2):
            copy(q, s).wait()
            total = jnp.dot(x_ref[:, :rows], slots[2 * q + s, 0], preferred_element_type=jnp.float32)
            for j in (1, 2):
                total += jnp.dot(
                    x_ref[:, j * rows : (j + 1) * rows], slots[2 * q + s, j], preferred_element_type=jnp.float32
                )
            out_ref[s, q] = total


def join(order, first, count, x, w_fc, after, turn):
    tokens = x.shape[0]
    rows = w_fc.shape[1]
    width = rows // 2
    shapes = [vmem_out((2, count, tokens, width), jnp.float32), vmem_out((1, width), jnp.float32)]
    if turn:
        shapes.append(jax.ShapeDtypeStruct(x.shape[::-1], x.dtype))
    return pl.pallas_call(
        functools.partial(join_kernel, first, count),
        out_shape=tuple(shapes),
        in_specs=[IN_SMEM, IN_VMEM, ANYWHERE, ANYWHERE],
        out_specs=(IN_VMEM,) * len(shapes),
        scratch_shapes=[
            pltpu.VMEM((2 * count, 3, rows, width), jnp.bfloat16),
            pltpu.SemaphoreType.DMA((2 * count,)),
        ],
        name="join",
        **settings(6 * tokens * rows * rows * count, 6 * rows * rows * count, 20 * MIB),
    )(order, near(x), far(w_fc), after)


def columns_of(rows_of_stats):
    count, tokens = rows_of_stats.shape
    padded = jnp.concatenate([rows_of_stats, jnp.zeros((tokens - count, tokens), jnp.float32)], axis=0)
    return padded.T


def target_mask(me, targets_ref, share):
    column = me * share + lax.broadcasted_iota(jnp.int32, (targets_ref.shape[1], share), 1)
    return column == columns_of(targets_ref[...].astype(jnp.float32))[:, :1].astype(jnp.int32)


def head_kernel(first, counts, last, starts, w_ref, before_ref, targets_ref, *rest):
    pieces, (out_ref, extra_ref) = rest[:-2], rest[-2:]
    width = pieces[0].shape[2]
    out_ref[...] = before_ref[...]
    at = first
    for piece_ref, count in zip(pieces, counts):

        @pl.loop(0, count)
        def _(q):
            row = pl.multiple_of(starts[at + q], 128)
            out_ref[...] += jnp.dot(piece_ref[q], w_ref[pl.ds(row, width), :], preferred_element_type=jnp.float32)

        at += count
    if not last:
        extra_ref[...] = jnp.ones_like(extra_ref)
        return
    logits = out_ref[...]
    tokens, share = logits.shape
    peak = jnp.max(logits, axis=1, keepdims=True)
    shifted = logits - peak
    weight = jnp.exp(shifted)
    picked = jnp.where(target_mask(starts[starts.shape[0] - 1], targets_ref, share), logits, 0.0)
    lane = lax.broadcasted_iota(jnp.int32, (tokens, tokens), 1)
    stats = jnp.where(lane == 0, peak, 0.0)
    for k, part in enumerate((weight, weight * shifted, picked)):
        stats = jnp.where(lane == k + 1, jnp.sum(part, axis=1, keepdims=True), stats)
    extra_ref[...] = stats.T[: extra_ref.shape[0]]


def head(starts, first, pieces, w_lm, before, targets, last):
    tokens, width = pieces[0].shape[1:]
    counts = tuple(p.shape[0] for p in pieces)
    share = w_lm.shape[1]
    extra = (8, tokens) if last else (1, width)
    return pl.pallas_call(
        functools.partial(head_kernel, first, counts, last),
        out_shape=(vmem_out(before.shape, jnp.float32), vmem_out(extra, jnp.float32)),
        in_specs=[IN_SMEM] + [IN_VMEM] * (3 + len(pieces)),
        out_specs=(IN_VMEM, IN_VMEM),
        name="head",
        **settings(2 * tokens * width * share * sum(counts), 8 * tokens * share, 6 * MIB),
    )(starts, near(w_lm), near(before), near(targets), *[near(p) for p in pieces])


def back_products(first, count, order, d_ref, w_ref, out_ref):
    width = out_ref.shape[3]

    @pl.loop(0, count)
    def _(q):
        for s in range(2):
            row = pl.multiple_of(order[s, first + q], 128)
            out_ref[s, q] = lax.dot_general(
                d_ref[...],
                w_ref[pl.ds(row, width), :],
                (((1,), (1,)), ((), ())),
                preferred_element_type=jnp.float32,
            )


def back_first_kernel(first, count, order, starts, logits_ref, stats_ref, targets_ref, w_ref, out_ref, d_ref):
    logits = logits_ref[...]
    tokens, share = logits.shape
    log_total = columns_of(stats_ref[...])[:, :1]
    hit = jnp.where(target_mask(starts[starts.shape[0] - 1], targets_ref, share), 1.0, 0.0)
    d_ref[...] = ((jnp.exp(logits - log_total) - hit) / tokens).astype(d_ref.dtype)
    back_products(first, count, order, d_ref, w_ref, out_ref)


def back_first(order, starts, first, count, logits, stats, targets, w_lm, width):
    tokens, share = logits.shape
    return pl.pallas_call(
        functools.partial(back_first_kernel, first, count),
        out_shape=(vmem_out((2, count, tokens, width), jnp.float32), vmem_out((tokens, share), jnp.bfloat16)),
        in_specs=[IN_SMEM] * 2 + [IN_VMEM] * 4,
        out_specs=(IN_VMEM, IN_VMEM),
        name="back_first",
        **settings(4 * tokens * width * share * count, 8 * tokens * width * count, 6 * MIB),
    )(order, starts, near(logits), near(stats), near(targets), near(w_lm))


def back_rest_kernel(first, count, order, d_ref, w_ref, after_ref, out_ref, token_ref):
    token_ref[...] = jnp.ones_like(token_ref)
    back_products(first, count, order, d_ref, w_ref, out_ref)


def back_rest(order, first, count, dlogits, w_lm, width, after):
    tokens, share = dlogits.shape
    return pl.pallas_call(
        functools.partial(back_rest_kernel, first, count),
        out_shape=(vmem_out((2, count, tokens, width), jnp.float32), vmem_out((1, width), jnp.float32)),
        in_specs=[IN_SMEM, IN_VMEM, IN_VMEM, ANYWHERE],
        out_specs=(IN_VMEM, IN_VMEM),
        name="back_rest",
        **settings(4 * tokens * width * share * count, 8 * tokens * width * count, 6 * MIB),
    )(order, near(dlogits), near(w_lm), after)


def head_grad_kernel(first, counts, aliased, starts, d_ref, after_ref, *rest):
    pieces = rest[aliased : aliased + len(counts)]
    out_ref, token_ref, slots, sems = rest[-4:]
    width = pieces[0].shape[2]
    share = d_ref.shape[1]
    token_ref[...] = jnp.ones_like(token_ref)

    def copy(at):
        row = pl.multiple_of(starts[first + at], 128)
        return pltpu.make_async_copy(slots.at[at], out_ref.at[pl.ds(row, width), :], sems.at[at])

    offset = 0
    for piece_ref, count in zip(pieces, counts):

        @pl.loop(0, count)
        def _(q):
            turned = piece_ref[q].T
            for column in range(0, share, TILE):
                for row in range(0, width, TILE):
                    slots[offset + q, row : row + TILE, column : column + TILE] = jnp.dot(
                        turned[row : row + TILE],
                        d_ref[:, column : column + TILE],
                        preferred_element_type=jnp.float32,
                    ).astype(slots.dtype)
            copy(offset + q).start()

        offset += count

    for at in range(sum(counts)):
        copy(at).wait()


def head_grad(starts, first, pieces, dlogits, full_width, after, into):
    tokens, width = pieces[0].shape[1:]
    counts = tuple(p.shape[0] for p in pieces)
    share = dlogits.shape[1]
    extra = () if into is None else (into,)
    blocks = sum(counts)
    return pl.pallas_call(
        functools.partial(head_grad_kernel, first, counts, len(extra)),
        out_shape=(
            jax.ShapeDtypeStruct((full_width, share), jnp.bfloat16),
            vmem_out((1, width), jnp.float32),
        ),
        in_specs=[IN_SMEM, IN_VMEM, ANYWHERE] + [ANYWHERE] * len(extra) + [IN_VMEM] * len(pieces),
        out_specs=(ANYWHERE, IN_VMEM),
        scratch_shapes=[pltpu.VMEM((blocks, width, share), jnp.bfloat16), pltpu.SemaphoreType.DMA((blocks,))],
        input_output_aliases={3: 0} if extra else {},
        name="head_grad",
        **settings(1024, 1024, 14 * MIB),
    )(starts, near(dlogits), after, *extra, *[near(p) for p in pieces])


def join_grad_kernel(first, counts, aliased, starts, x_ref, *rest):
    pieces = rest[aliased : aliased + len(counts)]
    out_ref, token_ref, slots, sems = rest[-4:]
    rows, width = slots.shape[2:]
    token_ref[...] = jnp.ones_like(token_ref)

    def copy(at):
        column = pl.multiple_of(starts[first + at], 128)
        return pltpu.make_async_copy(slots.at[at], out_ref.at[:, :, pl.ds(column, width)], sems.at[at])

    offset = 0
    for piece_ref, count in zip(pieces, counts):

        @pl.loop(0, count)
        def _(q):
            for j in range(3):
                for row in range(0, rows, TILE):
                    slots[offset + q, j, row : row + TILE, :] = jnp.dot(
                        x_ref[j * rows + row : j * rows + row + TILE, :],
                        piece_ref[q],
                        preferred_element_type=jnp.float32,
                    ).astype(slots.dtype)
            copy(offset + q).start()

        offset += count

    for at in range(sum(counts)):
        copy(at).wait()


def join_grad(starts, first, pieces, x_turned, full_width, into):
    tokens, width = pieces[0].shape[1:]
    rows = x_turned.shape[0] // 3
    counts = tuple(p.shape[0] for p in pieces)
    extra = () if into is None else (into,)
    blocks = sum(counts)
    return pl.pallas_call(
        functools.partial(join_grad_kernel, first, counts, len(extra)),
        out_shape=(
            jax.ShapeDtypeStruct((3, rows, full_width), jnp.bfloat16),
            vmem_out((1, width), jnp.float32),
        ),
        in_specs=[IN_SMEM, IN_VMEM] + [ANYWHERE] * len(extra) + [IN_VMEM] * len(pieces),
        out_specs=(ANYWHERE, IN_VMEM),
        scratch_shapes=[pltpu.VMEM((blocks, 3, rows, width), jnp.bfloat16), pltpu.SemaphoreType.DMA((blocks,))],
        input_output_aliases={2: 0} if extra else {},
        name="join_grad",
        **settings(6 * tokens * rows * width * blocks, 6 * rows * width * blocks, 14 * MIB),
    )(starts, near(x_turned), *extra, *[near(p) for p in pieces])


def cut(total, order, width):
    tokens = total.shape[0]
    blocks = total.reshape(tokens, -1, width).transpose(1, 0, 2)
    blocks = jnp.take(blocks, order // width, axis=0)
    quarter = order.shape[1] // 4
    return blocks[:, :quarter], blocks[:, quarter : 2 * quarter], blocks[:, 2 * quarter :]


def whole(pieces, starts):
    blocks = jnp.take(jnp.concatenate(pieces, axis=0), jnp.argsort(starts[:-1]), axis=0)
    return blocks.transpose(1, 0, 2).reshape(blocks.shape[1], -1)


def contributions(x, group, size):
    return [x] + [exchange(x, m, size) for m in masks_of(group)]


def tree_sum(items):
    while len(items) > 1:
        items = [items[k] + items[k + 1] for k in range(0, len(items), 2)]
    return items[0]


def merge_sums(items):
    peak = functools.reduce(jnp.maximum, [i[0:1] for i in items])
    shifts = [i[0:1] - peak for i in items]
    scales = [jnp.exp(s) for s in shifts]
    return jnp.concatenate(
        [
            peak,
            tree_sum([i[1:2] * c for i, c in zip(items, scales)]),
            tree_sum([(i[2:3] + i[1:2] * s) * c for i, s, c in zip(items, shifts, scales)]),
            tree_sum([i[3:4] for i in items]),
        ],
        axis=0,
    )


def with_token(x, token):
    return x if token is None else (x.astype(jnp.float32) * token).astype(x.dtype)


def reduce_halves(low, high, rest, bits, size, pack, unpack, work):
    got = unpack(exchange(pack(high), 1, size))
    quarter = low.shape[1]
    sent = low + got[:, quarter:]
    passed = [exchange(pack(sent[0]), 2, size), exchange(pack(sent[1]), 4, size)]
    remaining, token = rest(sent)
    token = work(1, remaining, token)
    total = remaining + got[:, :quarter]
    total = total + with_token(unpack(jnp.stack(passed)), token)
    half = quarter // 2
    sent = total[:, half:]
    passed = [exchange(pack(sent[0]), 4, size), exchange(pack(sent[1]), 2, size)]
    token = work(2, sent, None)
    total = total[:, :half] + with_token(unpack(jnp.stack(passed)), token)
    for bit in range(3, bits - 1):
        half = total.shape[1] // 2
        total = total[:, :half] + unpack(exchange(pack(total[:, half:]), 1 << bit, size))
    passed = exchange(pack(total), 1 << (bits - 1), size)
    token = work(bits - 1, total, None)
    return total + with_token(unpack(jnp.stack([passed[:, 1], passed[:, 0]], axis=1)), token)


def gather(held, bits, size, work):
    def flat(x):
        return x.reshape((-1,) + x.shape[2:])

    fresh = held
    across = []
    for bit in range(bits - 2, 2, -1):
        arrived = exchange(held, 1 << bit, size)
        across.append(exchange(fresh, 1, size))
        token = work([flat(fresh)], False)
        fresh = with_token(arrived, token)
        held = jnp.concatenate([held, fresh], axis=1)
    first = [exchange(held[0], 4, size), exchange(held[1], 2, size)]
    across.append(exchange(fresh, 1, size))
    token = work([flat(fresh)], False)
    first = with_token(jnp.stack(first), token)
    across += [first, exchange(first, 1, size)]
    both = jnp.concatenate([held, first], axis=1)
    second = [exchange(both[0], 2, size), exchange(both[1], 4, size)]
    token = work([flat(a) for a in across], False)
    second = with_token(jnp.stack(second), token)
    across = exchange(second, 1, size)
    work([flat(second)], False)
    work([flat(across)], True)


def on_device(size, low_feat, mid_feat, high_feat, w_fc, gain, w_lm, targets):
    me = lax.axis_index("section")
    rows, full_width = w_fc.shape[1], w_fc.shape[2]
    share = w_lm.shape[1]
    tokens = targets.shape[0]
    half = rows // 2
    bits = size.bit_length() - 1
    count = size // 2
    last = list(range(3, bits))
    orders = np.array([reduce_places(bits, [1, 2] + last), reduce_places(bits, [2, 1] + last)], np.int32)
    orders = np.concatenate([orders, orders + 1], axis=1)
    order = (jnp.asarray(orders) ^ me) * rows + jnp.asarray(np.array([[0], [half]], np.int32))
    places, streams = gather_places(bits)
    starts = jnp.concatenate([(jnp.asarray(places) ^ me) * rows + jnp.asarray(streams * half), me[None]])
    kernels = half % TILE == 0
    target_row = targets.reshape(1, tokens)

    sent = jnp.concatenate(
        [f.reshape(-1, size, rows) for f in (low_feat, mid_feat, high_feat)], axis=2
    ).transpose(1, 0, 2)
    x = lax.all_to_all(sent, "section", split_axis=0, concat_axis=0, tiled=True).reshape(tokens, 3 * rows)

    held = {"logits": jnp.zeros((tokens, share), jnp.float32), "grad_lm": None, "grad_fc": None}
    quarter = size // 4
    if kernels:
        high, _, held["x"] = join(order, count, count, x, w_fc, sent, True)
        low, _ = join(order, quarter, quarter, x, w_fc, sent, False)
    else:
        total = jnp.dot(x, w_fc.reshape(3 * rows, full_width), preferred_element_type=jnp.float32)
        remaining, low, high = cut(total, order, half)

    def join_rest(after):
        return join(order, 0, quarter, x, w_fc, after, False) if kernels else (remaining, None)

    def bring_head(k, after, token):
        if kernels and k == 1:
            held["lm"], token = stage(w_lm, after, half)
        return token

    joined = reduce_halves(low, high, join_rest, bits, size, lambda x: x, lambda x: x, bring_head)

    squares = jnp.sum(joined * joined, axis=(0, 3))
    squares = squares[0] + squares[1]
    for group in sum_rounds(bits - 1):
        squares = tree_sum(contributions(squares, group, size))
    inv_rms = lax.rsqrt(squares / full_width + epsilon)[:, None]
    gains = gain.reshape(2, 1, 1, half)
    gains = jnp.concatenate([gains, exchange(gain, 1 << (bits - 1), size).reshape(2, 1, 1, half)], axis=1)
    normed = (joined * inv_rms * gains).astype(jnp.bfloat16)

    all_normed, all_dfused = [], []

    def add_logits(pieces, last):
        first = sum(p.shape[0] for p in all_normed)
        all_normed.extend(pieces)
        if kernels:
            held["logits"], extra = head(starts, first, pieces, held["lm"], held["logits"], target_row, last)
            if last:
                held["stats"] = extra
            return extra

    gather(normed, bits, size, add_logits)
    logits = held["logits"]
    if kernels:
        stats = held["stats"][:4]
    else:
        normed_all = whole(all_normed, starts)
        logits = jnp.dot(normed_all, w_lm, preferred_element_type=jnp.float32)
        is_target = (me * share + lax.iota(jnp.int32, share))[None, :] == targets[:, None]
        peak = jnp.max(logits, axis=1)
        shifted = logits - peak[:, None]
        weight = jnp.exp(shifted)
        stats = jnp.stack(
            [
                peak,
                jnp.sum(weight, axis=1),
                jnp.sum(weight * shifted, axis=1),
                jnp.sum(jnp.where(is_target, logits, 0.0), axis=1),
            ]
        )
    for group in sum_rounds(bits):
        stats = merge_sums(contributions(stats, group, size))
    peak, exp_total, exp_moment, picked = stats[0], stats[1], stats[2], stats[3]
    log_total = peak + jnp.log(exp_total)
    token_loss = log_total - picked
    rowdot = ((exp_moment / exp_total - (picked - peak)) / tokens)[:, None] / inv_rms

    if kernels:
        spread = jnp.broadcast_to(log_total[None], (8, tokens))
        high, dlogits = back_first(order, starts, count, count, logits, spread, target_row, held["lm"], half)
        low, _ = back_rest(order, quarter, quarter, dlogits, held["lm"], half, high)
    else:
        dlogits = (
            (jnp.exp(logits - log_total[:, None]) - is_target.astype(jnp.float32)) / tokens
        ).astype(jnp.bfloat16)
        total = lax.dot_general(
            dlogits, w_lm, (((1,), (1,)), ((), ())), preferred_element_type=jnp.float32
        )
        left, low, high = cut(total, order, half)

    def back_last(after):
        return back_rest(order, 0, quarter, dlogits, held["lm"], half, after) if kernels else (left, None)

    def fill_grad_lm(k, after, token):
        if kernels and k != 2:
            middle = len(all_normed) - 3
            pieces = all_normed[:middle] if k == 1 else all_normed[middle:]
            first = 0 if k == 1 else sum(p.shape[0] for p in all_normed[:middle])
            held["grad_lm"], token = head_grad(
                starts, first, pieces, dlogits, full_width, after, held["grad_lm"]
            )
        return token

    scale = HALF_SCALE * (tokens / 128)

    def pack_half(x):
        return (x * scale).astype(jnp.float16)

    def unpack_half(x):
        return x.astype(jnp.float32) * (1.0 / scale)

    dnormed = reduce_halves(low, high, back_last, bits, size, pack_half, unpack_half, fill_grad_lm)
    if kernels:
        grad_lm = held["grad_lm"]
    else:
        grad_lm = lax.dot_general(
            normed_all, dlogits, (((0,), (0,)), ((), ())), preferred_element_type=jnp.float32
        ).astype(jnp.bfloat16)

    grad_gain = jnp.sum(dnormed[:, 0] * joined[:, 0] * inv_rms, axis=1).reshape(rows)
    dfused = (
        inv_rms * (dnormed * gains) - joined * (inv_rms * inv_rms * inv_rms * rowdot / full_width)
    ).astype(jnp.bfloat16)

    def fill_grad_fc(pieces, last):
        first = sum(p.shape[0] for p in all_dfused)
        all_dfused.extend(pieces)
        if kernels:
            held["grad_fc"], token = join_grad(starts, first, pieces, held["x"], full_width, held["grad_fc"])
            return token

    gather(dfused, bits, size, fill_grad_fc)
    if kernels:
        grad_fc = held["grad_fc"]
    else:
        grad_fc = jnp.dot(x.T, whole(all_dfused, starts), preferred_element_type=jnp.float32)
        grad_fc = grad_fc.astype(jnp.bfloat16).reshape(3, rows, full_width)
    return (token_loss, grad_fc, grad_gain, grad_lm)


def solution(mesh):
    return jax.shard_map(
        functools.partial(on_device, mesh.shape["section"]),
        mesh=mesh,
        in_specs=(
            P(("grp", "section"), None),
            P(("grp", "section"), None),
            P(("grp", "section"), None),
            P(None, "section", None),
            P("section"),
            P(None, "section"),
            P("grp"),
        ),
        out_specs=(P("grp"), P("grp", "section", None), P(("grp", "section")), P("grp", "section")),
        check_vma=False,
    )
```

```python
import functools

import jax
import jax.numpy as jnp
import numpy as np
from jax import lax
from jax.experimental import pallas as pl
from jax.experimental.pallas import tpu as pltpu
from jax.sharding import PartitionSpec as P

epsilon = 1e-06
MIB = 1024 * 1024
HALF_SCALE = 2.0**20
TILE = 256


def reduce_places(bits):
    out = []
    for stream, order in enumerate(([1, 2], [2, 1])):
        order = order + list(range(3, bits - 1))
        spread = [
            sum(((q >> (len(order) - 1 - k)) & 1) << bit for k, bit in enumerate(order))
            for q in range(1 << len(order))
        ]
        spread = [p | (stream << (bits - 1)) for p in spread]
        out.append(spread + [p + 1 for p in spread])
    return np.array(out, np.int32)


def gather_places(bits):
    held = fresh = np.array([[0], [1 << (bits - 1)]], np.int32)
    out, across = [held], []
    for bit in range(bits - 2, 2, -1):
        across.append(fresh ^ 1)
        fresh = held ^ (1 << bit)
        held = np.concatenate([held, fresh], axis=1)
        out.append(fresh)
    first = held ^ np.array([[4], [2]], np.int32)
    second = np.concatenate([held, first], axis=1) ^ np.array([[2], [4]], np.int32)
    out += [*across, fresh ^ 1, first, first ^ 1, second, second ^ 1]
    return np.concatenate([p.reshape(-1) for p in out]).astype(np.int32)


def masks_of(group):
    return [sum(1 << b for k, b in enumerate(group) if (m >> k) & 1) for m in range(1, 1 << len(group))]


def sum_rounds(top):
    return [[bit] for bit in range(top - 1, 2, -1)] + [[1, 2], [0]]


def exchange(x, mask, size):
    return lax.ppermute(x, "section", [(i, i ^ mask) for i in range(size)])


def settings(flops, bytes_moved, limit):
    return dict(
        compiler_params=pltpu.CompilerParams(vmem_limit_bytes=limit),
        cost_estimate=pl.CostEstimate(flops=flops, bytes_accessed=bytes_moved, transcendentals=0),
    )


ANYWHERE = pl.BlockSpec(memory_space=pl.ANY)
IN_VMEM = pl.BlockSpec(memory_space=pltpu.VMEM)
IN_SMEM = pl.BlockSpec(memory_space=pltpu.SMEM)
vmem_out = pltpu.VMEM


def near(x):
    return pltpu.with_memory_space_constraint(x, pltpu.VMEM)


def far(x):
    return pltpu.with_memory_space_constraint(x, pltpu.HBM)


def stage_kernel(pieces, w_ref, after_ref, out_ref, token_ref, sems):
    copies = []
    for k, piece in enumerate(pieces):
        copies.append(pltpu.make_async_copy(w_ref.at[piece], out_ref.at[piece], sems.at[k]))
    for copy in copies:
        copy.start()
    token_ref[...] = jnp.ones_like(token_ref)
    for copy in copies:
        copy.wait()


def stage(w, after, rows):
    step = w.shape[0] // 16
    pieces = [pl.ds(k * step, step) for k in range(16)]
    return pl.pallas_call(
        functools.partial(stage_kernel, pieces),
        out_shape=(vmem_out(w.shape, w.dtype), vmem_out((1, rows), jnp.float32)),
        in_specs=[ANYWHERE, ANYWHERE],
        out_specs=(IN_VMEM, IN_VMEM),
        scratch_shapes=[pltpu.SemaphoreType.DMA((len(pieces),))],
        name="stage",
        **settings(0, w.size * 2, 2 * MIB),
    )(far(w), after)


def join_kernel(first, count, order, x_ref, w_ref, after_ref, *rest):
    out_ref, token_ref, slots, sems = rest[0], rest[1], rest[-2], rest[-1]
    rows = w_ref.shape[1]
    width = slots.shape[3]

    def copy(q, s):
        column = pl.multiple_of(order[s, first + q], 128)
        at = 2 * q + s
        return pltpu.make_async_copy(w_ref.at[:, :, pl.ds(column, width)], slots.at[at], sems.at[at])

    for q in range(count):
        for s in range(2):
            copy(q, s).start()
    token_ref[...] = jnp.ones_like(token_ref)
    if len(rest) == 5:
        rest[2][...] = x_ref[...].T

    @pl.loop(0, count)
    def _(q):
        for s in range(2):
            copy(q, s).wait()
            for at in range(0, width, TILE):
                total = jnp.dot(
                    x_ref[:, :rows], slots[2 * q + s, 0, :, at : at + TILE], preferred_element_type=jnp.float32
                )
                for j in (1, 2):
                    total += jnp.dot(
                        x_ref[:, j * rows : (j + 1) * rows],
                        slots[2 * q + s, j, :, at : at + TILE],
                        preferred_element_type=jnp.float32,
                    )
                out_ref[s, q, :, at : at + TILE] = total


def join(order, first, count, x, w_fc, after, turn):
    tokens = x.shape[0]
    rows = w_fc.shape[1]
    width = rows
    shapes = [vmem_out((2, count, tokens, width), jnp.float32), vmem_out((1, width), jnp.float32)]
    if turn:
        shapes.append(jax.ShapeDtypeStruct(x.shape[::-1], x.dtype))
    return pl.pallas_call(
        functools.partial(join_kernel, first, count),
        out_shape=tuple(shapes),
        in_specs=[IN_SMEM, IN_VMEM, ANYWHERE, ANYWHERE],
        out_specs=(IN_VMEM,) * len(shapes),
        scratch_shapes=[
            pltpu.VMEM((2 * count, 3, rows, width), jnp.bfloat16),
            pltpu.SemaphoreType.DMA((2 * count,)),
        ],
        name="join",
        **settings(12 * tokens * rows * rows * count, 12 * rows * rows * count, 20 * MIB),
    )(order, near(x), far(w_fc), after)


def columns_of(rows_of_stats):
    count, tokens = rows_of_stats.shape
    padded = jnp.concatenate([rows_of_stats, jnp.zeros((tokens - count, tokens), jnp.float32)], axis=0)
    return padded.T


def target_mask(me, targets_ref, share):
    column = me * share + lax.broadcasted_iota(jnp.int32, (targets_ref.shape[1], share), 1)
    return column == columns_of(targets_ref[...].astype(jnp.float32))[:, :1].astype(jnp.int32)


def head_kernel(first, counts, last, starts, w_ref, before_ref, targets_ref, *rest):
    pieces, (out_ref, extra_ref) = rest[:-2], rest[-2:]
    width = pieces[0].shape[2]
    out_ref[...] = before_ref[...]
    at = first
    for piece_ref, count in zip(pieces, counts):

        @pl.loop(0, count)
        def _(q):
            row = pl.multiple_of(starts[at + q], 128)
            out_ref[...] += jnp.dot(piece_ref[q], w_ref[pl.ds(row, width), :], preferred_element_type=jnp.float32)

        at += count
    if not last:
        extra_ref[...] = jnp.ones_like(extra_ref)
        return
    logits = out_ref[...]
    tokens, share = logits.shape
    peak = jnp.max(logits, axis=1, keepdims=True)
    shifted = logits - peak
    weight = jnp.exp(shifted)
    picked = jnp.where(target_mask(starts[starts.shape[0] - 1], targets_ref, share), logits, 0.0)
    lane = lax.broadcasted_iota(jnp.int32, (tokens, tokens), 1)
    stats = jnp.where(lane == 0, peak, 0.0)
    for k, part in enumerate((weight, weight * shifted, picked)):
        stats = jnp.where(lane == k + 1, jnp.sum(part, axis=1, keepdims=True), stats)
    extra_ref[...] = stats.T[: extra_ref.shape[0]]


def head(starts, first, pieces, w_lm, before, targets, last):
    tokens, width = pieces[0].shape[1:]
    counts = tuple(p.shape[0] for p in pieces)
    share = w_lm.shape[1]
    extra = (8, tokens) if last else (1, width)
    return pl.pallas_call(
        functools.partial(head_kernel, first, counts, last),
        out_shape=(vmem_out(before.shape, jnp.float32), vmem_out(extra, jnp.float32)),
        in_specs=[IN_SMEM] + [IN_VMEM] * (3 + len(pieces)),
        out_specs=(IN_VMEM, IN_VMEM),
        name="head",
        **settings(2 * tokens * width * share * sum(counts), 8 * tokens * share, 6 * MIB),
    )(starts, near(w_lm), near(before), near(targets), *[near(p) for p in pieces])


def back_products(first, count, order, d_ref, w_ref, out_ref):
    width = out_ref.shape[3]

    @pl.loop(0, count)
    def _(q):
        for s in range(2):
            row = pl.multiple_of(order[s, first + q], 128)
            for at in range(0, width, TILE):
                out_ref[s, q, :, at : at + TILE] = lax.dot_general(
                    d_ref[...],
                    w_ref[pl.ds(row + at, TILE), :],
                    (((1,), (1,)), ((), ())),
                    preferred_element_type=jnp.float32,
                )


def back_first_kernel(first, count, order, starts, logits_ref, stats_ref, targets_ref, w_ref, out_ref, d_ref):
    logits = logits_ref[...]
    tokens, share = logits.shape
    log_total = columns_of(stats_ref[...])[:, :1]
    hit = jnp.where(target_mask(starts[starts.shape[0] - 1], targets_ref, share), 1.0, 0.0)
    d_ref[...] = ((jnp.exp(logits - log_total) - hit) / tokens).astype(d_ref.dtype)
    back_products(first, count, order, d_ref, w_ref, out_ref)


def back_first(order, starts, first, count, logits, stats, targets, w_lm, width):
    tokens, share = logits.shape
    return pl.pallas_call(
        functools.partial(back_first_kernel, first, count),
        out_shape=(vmem_out((2, count, tokens, width), jnp.float32), vmem_out((tokens, share), jnp.bfloat16)),
        in_specs=[IN_SMEM] * 2 + [IN_VMEM] * 4,
        out_specs=(IN_VMEM, IN_VMEM),
        name="back_first",
        **settings(4 * tokens * width * share * count, 8 * tokens * width * count, 6 * MIB),
    )(order, starts, near(logits), near(stats), near(targets), near(w_lm))


def back_rest_kernel(first, count, order, d_ref, w_ref, after_ref, out_ref, token_ref):
    token_ref[...] = jnp.ones_like(token_ref)
    back_products(first, count, order, d_ref, w_ref, out_ref)


def back_rest(order, first, count, dlogits, w_lm, width, after):
    tokens, share = dlogits.shape
    return pl.pallas_call(
        functools.partial(back_rest_kernel, first, count),
        out_shape=(vmem_out((2, count, tokens, width), jnp.float32), vmem_out((1, width), jnp.float32)),
        in_specs=[IN_SMEM, IN_VMEM, IN_VMEM, ANYWHERE],
        out_specs=(IN_VMEM, IN_VMEM),
        name="back_rest",
        **settings(4 * tokens * width * share * count, 8 * tokens * width * count, 6 * MIB),
    )(order, near(dlogits), near(w_lm), after)


def head_grad_kernel(first, counts, aliased, starts, d_ref, after_ref, *rest):
    pieces = rest[aliased : aliased + len(counts)]
    out_ref, token_ref, slots, sems = rest[-4:]
    width = pieces[0].shape[2]
    share = d_ref.shape[1]
    token_ref[...] = jnp.ones_like(token_ref)

    def copy(at):
        row = pl.multiple_of(starts[first + at], 128)
        return pltpu.make_async_copy(slots.at[at], out_ref.at[pl.ds(row, width), :], sems.at[at])

    offset = 0
    for piece_ref, count in zip(pieces, counts):

        @pl.loop(0, count)
        def _(q):
            turned = piece_ref[q].T
            for column in range(0, share, TILE):
                for row in range(0, width, TILE):
                    slots[offset + q, row : row + TILE, column : column + TILE] = jnp.dot(
                        turned[row : row + TILE],
                        d_ref[:, column : column + TILE],
                        preferred_element_type=jnp.float32,
                    ).astype(slots.dtype)
            copy(offset + q).start()

        offset += count

    for at in range(sum(counts)):
        copy(at).wait()


def head_grad(starts, first, pieces, dlogits, full_width, after, into):
    tokens, width = pieces[0].shape[1:]
    counts = tuple(p.shape[0] for p in pieces)
    share = dlogits.shape[1]
    extra = () if into is None else (into,)
    blocks = sum(counts)
    return pl.pallas_call(
        functools.partial(head_grad_kernel, first, counts, len(extra)),
        out_shape=(
            jax.ShapeDtypeStruct((full_width, share), jnp.bfloat16),
            vmem_out((1, width), jnp.float32),
        ),
        in_specs=[IN_SMEM, IN_VMEM, ANYWHERE] + [ANYWHERE] * len(extra) + [IN_VMEM] * len(pieces),
        out_specs=(ANYWHERE, IN_VMEM),
        scratch_shapes=[pltpu.VMEM((blocks, width, share), jnp.bfloat16), pltpu.SemaphoreType.DMA((blocks,))],
        input_output_aliases={3: 0} if extra else {},
        name="head_grad",
        **settings(1024, 1024, 14 * MIB),
    )(starts, near(dlogits), after, *extra, *[near(p) for p in pieces])


def join_grad_kernel(first, counts, aliased, starts, x_ref, *rest):
    pieces = rest[aliased : aliased + len(counts)]
    out_ref, token_ref, slots, sems = rest[-4:]
    rows, width = slots.shape[2:]
    token_ref[...] = jnp.ones_like(token_ref)

    def copy(at):
        column = pl.multiple_of(starts[first + at], 128)
        return pltpu.make_async_copy(slots.at[at], out_ref.at[:, :, pl.ds(column, width)], sems.at[at])

    offset = 0
    for piece_ref, count in zip(pieces, counts):

        @pl.loop(0, count)
        def _(q):
            for at in range(0, width, TILE):
                for j in range(3):
                    for row in range(0, rows, TILE):
                        slots[offset + q, j, row : row + TILE, at : at + TILE] = jnp.dot(
                            x_ref[j * rows + row : j * rows + row + TILE, :],
                            piece_ref[q, :, at : at + TILE],
                            preferred_element_type=jnp.float32,
                        ).astype(slots.dtype)
            copy(offset + q).start()

        offset += count

    for at in range(sum(counts)):
        copy(at).wait()


def join_grad(starts, first, pieces, x_turned, full_width, into):
    tokens, width = pieces[0].shape[1:]
    rows = x_turned.shape[0] // 3
    counts = tuple(p.shape[0] for p in pieces)
    extra = () if into is None else (into,)
    blocks = sum(counts)
    return pl.pallas_call(
        functools.partial(join_grad_kernel, first, counts, len(extra)),
        out_shape=(
            jax.ShapeDtypeStruct((3, rows, full_width), jnp.bfloat16),
            vmem_out((1, width), jnp.float32),
        ),
        in_specs=[IN_SMEM, IN_VMEM] + [ANYWHERE] * len(extra) + [IN_VMEM] * len(pieces),
        out_specs=(ANYWHERE, IN_VMEM),
        scratch_shapes=[pltpu.VMEM((blocks, 3, rows, width), jnp.bfloat16), pltpu.SemaphoreType.DMA((blocks,))],
        input_output_aliases={2: 0} if extra else {},
        name="join_grad",
        **settings(6 * tokens * rows * width * blocks, 6 * rows * width * blocks, 14 * MIB),
    )(starts, near(x_turned), *extra, *[near(p) for p in pieces])


def cut(total, order, width):
    tokens = total.shape[0]
    blocks = total.reshape(tokens, -1, width).transpose(1, 0, 2)
    blocks = jnp.take(blocks, order // width, axis=0)
    quarter = order.shape[1] // 4
    return blocks[:, :quarter], blocks[:, quarter : 2 * quarter], blocks[:, 2 * quarter :]


def whole(pieces, starts):
    blocks = jnp.take(jnp.concatenate(pieces, axis=0), jnp.argsort(starts[:-1]), axis=0)
    return blocks.transpose(1, 0, 2).reshape(blocks.shape[1], -1)


def contributions(x, group, size):
    return [x] + [exchange(x, m, size) for m in masks_of(group)]


def tree_sum(items):
    while len(items) > 1:
        items = [items[k] + items[k + 1] for k in range(0, len(items), 2)]
    return items[0]


def merge_sums(items):
    peak = functools.reduce(jnp.maximum, [i[0:1] for i in items])
    shifts = [i[0:1] - peak for i in items]
    scales = [jnp.exp(s) for s in shifts]
    return jnp.concatenate(
        [
            peak,
            tree_sum([i[1:2] * c for i, c in zip(items, scales)]),
            tree_sum([(i[2:3] + i[1:2] * s) * c for i, s, c in zip(items, shifts, scales)]),
            tree_sum([i[3:4] for i in items]),
        ],
        axis=0,
    )


def with_token(x, token):
    return x if token is None else (x.astype(jnp.float32) * token).astype(x.dtype)


def reduce_halves(low, high, rest, bits, size, pack, unpack, work):
    got = unpack(exchange(pack(high), 1, size))
    quarter = low.shape[1]
    sent = low + got[:, quarter:]
    passed = [exchange(pack(sent[0]), 2, size), exchange(pack(sent[1]), 4, size)]
    remaining, token = rest(sent)
    token = work(1, remaining, token)
    total = remaining + got[:, :quarter]
    total = total + with_token(unpack(jnp.stack(passed)), token)
    half = quarter // 2
    sent = total[:, half:]
    passed = [exchange(pack(sent[0]), 4, size), exchange(pack(sent[1]), 2, size)]
    token = work(2, sent, None)
    total = total[:, :half] + with_token(unpack(jnp.stack(passed)), token)
    for bit in range(3, bits - 1):
        half = total.shape[1] // 2
        total = total[:, :half] + unpack(exchange(pack(total[:, half:]), 1 << bit, size))
    passed = exchange(pack(total), 1 << (bits - 1), size)
    token = work(bits - 1, total, None)
    return total + with_token(unpack(jnp.stack([passed[1], passed[0]])), token)


def gather(held, bits, size, work):
    def flat(x):
        return x.reshape((-1,) + x.shape[2:])

    fresh = held
    across = []
    for bit in range(bits - 2, 2, -1):
        arrived = exchange(held, 1 << bit, size)
        across.append(exchange(fresh, 1, size))
        token = work([flat(fresh)], False)
        fresh = with_token(arrived, token)
        held = jnp.concatenate([held, fresh], axis=1)
    first = [exchange(held[0], 4, size), exchange(held[1], 2, size)]
    across.append(exchange(fresh, 1, size))
    token = work([flat(fresh)], False)
    first = with_token(jnp.stack(first), token)
    across += [first, exchange(first, 1, size)]
    both = jnp.concatenate([held, first], axis=1)
    second = [exchange(both[0], 2, size), exchange(both[1], 4, size)]
    token = work([flat(a) for a in across], False)
    second = with_token(jnp.stack(second), token)
    across = exchange(second, 1, size)
    work([flat(second)], False)
    work([flat(across)], True)


def on_device(size, low_feat, mid_feat, high_feat, w_fc, gain, w_lm, targets):
    me = lax.axis_index("section")
    rows, full_width = w_fc.shape[1], w_fc.shape[2]
    share = w_lm.shape[1]
    tokens = targets.shape[0]
    bits = size.bit_length() - 1
    count, quarter = size // 4, size // 8
    order = (jnp.asarray(reduce_places(bits)) ^ me) * rows
    starts = jnp.concatenate([(jnp.asarray(gather_places(bits)) ^ me) * rows, me[None]])
    kernels = rows % TILE == 0
    target_row = targets.reshape(1, tokens)

    sent = jnp.concatenate(
        [f.reshape(-1, size, rows) for f in (low_feat, mid_feat, high_feat)], axis=2
    ).transpose(1, 0, 2)
    x = lax.all_to_all(sent, "section", split_axis=0, concat_axis=0, tiled=True).reshape(tokens, 3 * rows)

    held = {"logits": jnp.zeros((tokens, share), jnp.float32), "grad_lm": None, "grad_fc": None}
    if kernels:
        high, _, held["x"] = join(order, count, count, x, w_fc, sent, True)
        low, _ = join(order, quarter, quarter, x, w_fc, sent, False)
    else:
        total = jnp.dot(x, w_fc.reshape(3 * rows, full_width), preferred_element_type=jnp.float32)
        remaining, low, high = cut(total, order, rows)

    def join_rest(after):
        return join(order, 0, quarter, x, w_fc, after, False) if kernels else (remaining, None)

    def bring_head(k, after, token):
        if kernels and k == 1:
            held["lm"], token = stage(w_lm, after, rows)
        return token

    joined = reduce_halves(low, high, join_rest, bits, size, lambda x: x, lambda x: x, bring_head)

    squares = jnp.sum(joined * joined, axis=(1, 3))
    squares = squares[0] + squares[1]
    for group in sum_rounds(bits - 1):
        squares = tree_sum(contributions(squares, group, size))
    inv_rms = lax.rsqrt(squares / full_width + epsilon)[:, None]
    gains = jnp.stack([gain, exchange(gain, 1 << (bits - 1), size)])[:, None, None, :]
    normed = (joined * inv_rms * gains).astype(jnp.bfloat16)

    all_normed, all_dfused = [], []

    def add_logits(pieces, last):
        first = sum(p.shape[0] for p in all_normed)
        all_normed.extend(pieces)
        if kernels:
            held["logits"], extra = head(starts, first, pieces, held["lm"], held["logits"], target_row, last)
            if last:
                held["stats"] = extra
            return extra

    gather(normed, bits, size, add_logits)
    logits = held["logits"]
    if kernels:
        stats = held["stats"][:4]
    else:
        normed_all = whole(all_normed, starts)
        logits = jnp.dot(normed_all, w_lm, preferred_element_type=jnp.float32)
        is_target = (me * share + lax.iota(jnp.int32, share))[None, :] == targets[:, None]
        peak = jnp.max(logits, axis=1)
        shifted = logits - peak[:, None]
        weight = jnp.exp(shifted)
        stats = jnp.stack(
            [
                peak,
                jnp.sum(weight, axis=1),
                jnp.sum(weight * shifted, axis=1),
                jnp.sum(jnp.where(is_target, logits, 0.0), axis=1),
            ]
        )
    for group in sum_rounds(bits):
        stats = merge_sums(contributions(stats, group, size))
    peak, exp_total, exp_moment, picked = stats[0], stats[1], stats[2], stats[3]
    log_total = peak + jnp.log(exp_total)
    token_loss = log_total - picked
    rowdot = ((exp_moment / exp_total - (picked - peak)) / tokens)[:, None] / inv_rms

    if kernels:
        spread = jnp.broadcast_to(log_total[None], (8, tokens))
        high, dlogits = back_first(order, starts, count, count, logits, spread, target_row, held["lm"], rows)
        low, _ = back_rest(order, quarter, quarter, dlogits, held["lm"], rows, high)
    else:
        dlogits = (
            (jnp.exp(logits - log_total[:, None]) - is_target.astype(jnp.float32)) / tokens
        ).astype(jnp.bfloat16)
        total = lax.dot_general(
            dlogits, w_lm, (((1,), (1,)), ((), ())), preferred_element_type=jnp.float32
        )
        left, low, high = cut(total, order, rows)

    def back_last(after):
        return back_rest(order, 0, quarter, dlogits, held["lm"], rows, after) if kernels else (left, None)

    def fill_grad_lm(k, after, token):
        if kernels and k != 2:
            middle = len(all_normed) - 4
            pieces = all_normed[:middle] if k == 1 else all_normed[middle:]
            first = 0 if k == 1 else sum(p.shape[0] for p in all_normed[:middle])
            held["grad_lm"], token = head_grad(
                starts, first, pieces, dlogits, full_width, after, held["grad_lm"]
            )
        return token

    scale = HALF_SCALE * (tokens / 128)

    def pack_half(x):
        return (x * scale).astype(jnp.float16)

    def unpack_half(x):
        return x.astype(jnp.float32) * (1.0 / scale)

    dnormed = reduce_halves(low, high, back_last, bits, size, pack_half, unpack_half, fill_grad_lm)
    if kernels:
        grad_lm = held["grad_lm"]
    else:
        grad_lm = lax.dot_general(
            normed_all, dlogits, (((0,), (0,)), ((), ())), preferred_element_type=jnp.float32
        ).astype(jnp.bfloat16)

    grad_gain = jnp.sum(dnormed[0, 0] * joined[0, 0] * inv_rms, axis=0)
    dfused = (
        inv_rms * (dnormed * gains) - joined * (inv_rms * inv_rms * inv_rms * rowdot / full_width)
    ).astype(jnp.bfloat16)

    def fill_grad_fc(pieces, last):
        first = sum(p.shape[0] for p in all_dfused)
        all_dfused.extend(pieces)
        if kernels:
            held["grad_fc"], token = join_grad(starts, first, pieces, held["x"], full_width, held["grad_fc"])
            return token

    gather(dfused, bits, size, fill_grad_fc)
    if kernels:
        grad_fc = held["grad_fc"]
    else:
        grad_fc = jnp.dot(x.T, whole(all_dfused, starts), preferred_element_type=jnp.float32)
        grad_fc = grad_fc.astype(jnp.bfloat16).reshape(3, rows, full_width)
    return (token_loss, grad_fc, grad_gain, grad_lm)


def solution(mesh):
    return jax.shard_map(
        functools.partial(on_device, mesh.shape["section"]),
        mesh=mesh,
        in_specs=(
            P(("grp", "section"), None),
            P(("grp", "section"), None),
            P(("grp", "section"), None),
            P(None, "section", None),
            P("section"),
            P(None, "section"),
            P("grp"),
        ),
        out_specs=(P("grp"), P("grp", "section", None), P(("grp", "section")), P("grp", "section")),
        check_vma=False,
    )
```

```python
import functools

import jax
import jax.numpy as jnp
import numpy as np
from jax import lax
from jax.experimental import pallas as pl
from jax.experimental.pallas import tpu as pltpu
from jax.sharding import PartitionSpec as P

epsilon = 1e-06
MIB = 1024 * 1024
HALF_SCALE = 2.0**20
TILE = 256


def reduce_places(bits):
    out = []
    for stream, order in enumerate(([1, 2], [2, 1])):
        order = order + list(range(3, bits - 1))
        spread = [
            sum(((q >> (len(order) - 1 - k)) & 1) << bit for k, bit in enumerate(order))
            for q in range(1 << len(order))
        ]
        spread = [p | (stream << (bits - 1)) for p in spread]
        out.append(spread + [p + 1 for p in spread])
    return np.array(out, np.int32)


def gather_places(bits):
    held = fresh = np.array([[0], [1 << (bits - 1)]], np.int32)
    out, across = [held], []
    for bit in range(bits - 2, 2, -1):
        across.append(fresh ^ 1)
        fresh = held ^ (1 << bit)
        held = np.concatenate([held, fresh], axis=1)
        out.append(fresh)
    first = held ^ np.array([[4], [2]], np.int32)
    second = np.concatenate([held, first], axis=1) ^ np.array([[2], [4]], np.int32)
    out += [*across, fresh ^ 1, first, first ^ 1, second, second ^ 1]
    return np.concatenate([p.reshape(-1) for p in out]).astype(np.int32)


def masks_of(group):
    return [sum(1 << b for k, b in enumerate(group) if (m >> k) & 1) for m in range(1, 1 << len(group))]


def sum_rounds(top):
    return [[bit] for bit in range(top - 1, 2, -1)] + [[1, 2], [0]]


def exchange(x, mask, size):
    return lax.ppermute(x, "section", [(i, i ^ mask) for i in range(size)])


def settings(flops, bytes_moved, limit):
    return dict(
        compiler_params=pltpu.CompilerParams(vmem_limit_bytes=limit),
        cost_estimate=pl.CostEstimate(flops=flops, bytes_accessed=bytes_moved, transcendentals=0),
    )


ANYWHERE = pl.BlockSpec(memory_space=pl.ANY)
IN_VMEM = pl.BlockSpec(memory_space=pltpu.VMEM)
IN_SMEM = pl.BlockSpec(memory_space=pltpu.SMEM)
vmem_out = pltpu.VMEM


def near(x):
    return pltpu.with_memory_space_constraint(x, pltpu.VMEM)


def far(x):
    return pltpu.with_memory_space_constraint(x, pltpu.HBM)


def stage_kernel(pieces, w_ref, after_ref, out_ref, token_ref, sems):
    copies = []
    for k, piece in enumerate(pieces):
        copies.append(pltpu.make_async_copy(w_ref.at[piece], out_ref.at[piece], sems.at[k]))
    for copy in copies:
        copy.start()
    token_ref[...] = jnp.ones_like(token_ref)
    for copy in copies:
        copy.wait()


def stage(w, after, rows):
    step = w.shape[0] // 16
    pieces = [pl.ds(k * step, step) for k in range(16)]
    return pl.pallas_call(
        functools.partial(stage_kernel, pieces),
        out_shape=(vmem_out(w.shape, w.dtype), vmem_out((1, rows), jnp.float32)),
        in_specs=[ANYWHERE, ANYWHERE],
        out_specs=(IN_VMEM, IN_VMEM),
        scratch_shapes=[pltpu.SemaphoreType.DMA((len(pieces),))],
        name="stage",
        **settings(0, w.size * 2, 2 * MIB),
    )(far(w), after)


def join_kernel(first, count, order, x_ref, w_ref, after_ref, *rest):
    out_ref, token_ref, slots, sems = rest[0], rest[1], rest[-2], rest[-1]
    rows = w_ref.shape[1]
    width = slots.shape[3]

    def copy(q, s):
        column = pl.multiple_of(order[s, first + q], 128)
        at = 2 * q + s
        return pltpu.make_async_copy(w_ref.at[:, :, pl.ds(column, width)], slots.at[at], sems.at[at])

    for q in range(count):
        for s in range(2):
            copy(q, s).start()
    token_ref[...] = jnp.ones_like(token_ref)
    if len(rest) == 5:
        rest[2][...] = x_ref[...].T

    @pl.loop(0, count)
    def _(q):
        for s in range(2):
            copy(q, s).wait()
            for at in range(0, width, TILE):
                total = jnp.dot(
                    x_ref[:, :rows], slots[2 * q + s, 0, :, at : at + TILE], preferred_element_type=jnp.float32
                )
                for j in (1, 2):
                    total += jnp.dot(
                        x_ref[:, j * rows : (j + 1) * rows],
                        slots[2 * q + s, j, :, at : at + TILE],
                        preferred_element_type=jnp.float32,
                    )
                out_ref[s, q, :, at : at + TILE] = total


def join(order, first, count, x, w_fc, after, turn):
    tokens = x.shape[0]
    rows = w_fc.shape[1]
    width = rows
    shapes = [vmem_out((2, count, tokens, width), jnp.float32), vmem_out((1, width), jnp.float32)]
    if turn:
        shapes.append(jax.ShapeDtypeStruct(x.shape[::-1], x.dtype))
    return pl.pallas_call(
        functools.partial(join_kernel, first, count),
        out_shape=tuple(shapes),
        in_specs=[IN_SMEM, IN_VMEM, ANYWHERE, ANYWHERE],
        out_specs=(IN_VMEM,) * len(shapes),
        scratch_shapes=[
            pltpu.VMEM((2 * count, 3, rows, width), jnp.bfloat16),
            pltpu.SemaphoreType.DMA((2 * count,)),
        ],
        name="join",
        **settings(12 * tokens * rows * rows * count, 12 * rows * rows * count, 20 * MIB),
    )(order, near(x), far(w_fc), after)


def columns_of(rows_of_stats):
    count, tokens = rows_of_stats.shape
    padded = jnp.concatenate([rows_of_stats, jnp.zeros((tokens - count, tokens), jnp.float32)], axis=0)
    return padded.T


def target_mask(me, targets_ref, share):
    column = me * share + lax.broadcasted_iota(jnp.int32, (targets_ref.shape[1], share), 1)
    return column == columns_of(targets_ref[...].astype(jnp.float32))[:, :1].astype(jnp.int32)


def head_kernel(first, counts, last, starts, w_ref, before_ref, targets_ref, *rest):
    pieces, (out_ref, extra_ref) = rest[:-2], rest[-2:]
    width = pieces[0].shape[2]
    out_ref[...] = before_ref[...]
    at = first
    for piece_ref, count in zip(pieces, counts):

        @pl.loop(0, count)
        def _(q):
            row = pl.multiple_of(starts[at + q], 128)
            out_ref[...] += jnp.dot(piece_ref[q], w_ref[pl.ds(row, width), :], preferred_element_type=jnp.float32)

        at += count
    if not last:
        extra_ref[...] = jnp.ones_like(extra_ref)
        return
    logits = out_ref[...]
    tokens, share = logits.shape
    peak = jnp.max(logits, axis=1, keepdims=True)
    shifted = logits - peak
    weight = jnp.exp(shifted)
    picked = jnp.where(target_mask(starts[starts.shape[0] - 1], targets_ref, share), logits, 0.0)
    lane = lax.broadcasted_iota(jnp.int32, (tokens, tokens), 1)
    stats = jnp.where(lane == 0, peak, 0.0)
    for k, part in enumerate((weight, weight * shifted, picked)):
        stats = jnp.where(lane == k + 1, jnp.sum(part, axis=1, keepdims=True), stats)
    extra_ref[...] = stats.T[: extra_ref.shape[0]]


def head(starts, first, pieces, w_lm, before, targets, last):
    tokens, width = pieces[0].shape[1:]
    counts = tuple(p.shape[0] for p in pieces)
    share = w_lm.shape[1]
    extra = (8, tokens) if last else (1, width)
    return pl.pallas_call(
        functools.partial(head_kernel, first, counts, last),
        out_shape=(vmem_out(before.shape, jnp.float32), vmem_out(extra, jnp.float32)),
        in_specs=[IN_SMEM] + [IN_VMEM] * (3 + len(pieces)),
        out_specs=(IN_VMEM, IN_VMEM),
        name="head",
        **settings(2 * tokens * width * share * sum(counts), 8 * tokens * share, 6 * MIB),
    )(starts, near(w_lm), near(before), near(targets), *[near(p) for p in pieces])


def back_products(first, count, order, d_ref, w_ref, out_ref):
    width = out_ref.shape[3]

    @pl.loop(0, count)
    def _(q):
        for s in range(2):
            row = pl.multiple_of(order[s, first + q], 128)
            for at in range(0, width, TILE):
                out_ref[s, q, :, at : at + TILE] = lax.dot_general(
                    d_ref[...],
                    w_ref[pl.ds(row + at, TILE), :],
                    (((1,), (1,)), ((), ())),
                    preferred_element_type=jnp.float32,
                )


def back_first_kernel(first, count, order, starts, logits_ref, stats_ref, targets_ref, w_ref, out_ref, d_ref):
    logits = logits_ref[...]
    tokens, share = logits.shape
    log_total = columns_of(stats_ref[...])[:, :1]
    hit = jnp.where(target_mask(starts[starts.shape[0] - 1], targets_ref, share), 1.0, 0.0)
    d_ref[...] = ((jnp.exp(logits - log_total) - hit) / tokens).astype(d_ref.dtype)
    back_products(first, count, order, d_ref, w_ref, out_ref)


def back_first(order, starts, first, count, logits, stats, targets, w_lm, width):
    tokens, share = logits.shape
    return pl.pallas_call(
        functools.partial(back_first_kernel, first, count),
        out_shape=(vmem_out((2, count, tokens, width), jnp.float32), vmem_out((tokens, share), jnp.bfloat16)),
        in_specs=[IN_SMEM] * 2 + [IN_VMEM] * 4,
        out_specs=(IN_VMEM, IN_VMEM),
        name="back_first",
        **settings(4 * tokens * width * share * count, 8 * tokens * width * count, 6 * MIB),
    )(order, starts, near(logits), near(stats), near(targets), near(w_lm))


def back_rest_kernel(first, count, order, d_ref, w_ref, after_ref, out_ref, token_ref):
    token_ref[...] = jnp.ones_like(token_ref)
    back_products(first, count, order, d_ref, w_ref, out_ref)


def back_rest(order, first, count, dlogits, w_lm, width, after):
    tokens, share = dlogits.shape
    return pl.pallas_call(
        functools.partial(back_rest_kernel, first, count),
        out_shape=(vmem_out((2, count, tokens, width), jnp.float32), vmem_out((1, width), jnp.float32)),
        in_specs=[IN_SMEM, IN_VMEM, IN_VMEM, ANYWHERE],
        out_specs=(IN_VMEM, IN_VMEM),
        name="back_rest",
        **settings(4 * tokens * width * share * count, 8 * tokens * width * count, 6 * MIB),
    )(order, near(dlogits), near(w_lm), after)


def head_grad_kernel(counts, starts, d_ref, after_ref, *rest):
    pieces = rest[: len(counts)]
    out_ref, token_ref, slots, sems = rest[-4:]
    width = pieces[0].shape[2]
    share = d_ref.shape[1]
    token_ref[...] = jnp.ones_like(token_ref)

    def copy(at):
        row = pl.multiple_of(starts[at], 128)
        return pltpu.make_async_copy(slots.at[at], out_ref.at[pl.ds(row, width), :], sems.at[at])

    offset = 0
    for piece_ref, count in zip(pieces, counts):

        @pl.loop(0, count)
        def _(q):
            turned = piece_ref[q].T
            for column in range(0, share, TILE):
                for row in range(0, width, TILE):
                    slots[offset + q, row : row + TILE, column : column + TILE] = jnp.dot(
                        turned[row : row + TILE],
                        d_ref[:, column : column + TILE],
                        preferred_element_type=jnp.float32,
                    ).astype(slots.dtype)
            copy(offset + q).start()

        offset += count

    for at in range(sum(counts)):
        copy(at).wait()


def head_grad(starts, pieces, dlogits, full_width, after):
    tokens, width = pieces[0].shape[1:]
    counts = tuple(p.shape[0] for p in pieces)
    share = dlogits.shape[1]
    blocks = sum(counts)
    return pl.pallas_call(
        functools.partial(head_grad_kernel, counts),
        out_shape=(
            jax.ShapeDtypeStruct((full_width, share), jnp.bfloat16),
            vmem_out((1, width), jnp.float32),
        ),
        in_specs=[IN_SMEM, IN_VMEM, ANYWHERE] + [IN_VMEM] * len(pieces),
        out_specs=(ANYWHERE, IN_VMEM),
        scratch_shapes=[pltpu.VMEM((blocks, width, share), jnp.bfloat16), pltpu.SemaphoreType.DMA((blocks,))],
        name="head_grad",
        **settings(2 * tokens * width * share * blocks, 2 * width * share * blocks, 22 * MIB),
    )(starts, near(dlogits), after, *[near(p) for p in pieces])


def join_grad_kernel(first, counts, aliased, starts, x_ref, *rest):
    pieces = rest[aliased : aliased + len(counts)]
    out_ref, token_ref, slots, sems = rest[-4:]
    rows, width = slots.shape[2:]
    token_ref[...] = jnp.ones_like(token_ref)

    def copy(at, j):
        column = pl.multiple_of(starts[first + at], 128)
        return pltpu.make_async_copy(
            slots.at[at, j], out_ref.at[j, :, pl.ds(column, width)], sems.at[3 * at + j]
        )

    offset = 0
    for piece_ref, count in zip(pieces, counts):

        @pl.loop(0, count)
        def _(q):
            for j in range(3):
                for at in range(0, width, TILE):
                    for row in range(0, rows, TILE):
                        slots[offset + q, j, row : row + TILE, at : at + TILE] = jnp.dot(
                            x_ref[j * rows + row : j * rows + row + TILE, :],
                            piece_ref[q, :, at : at + TILE],
                            preferred_element_type=jnp.float32,
                        ).astype(slots.dtype)
                copy(offset + q, j).start()

        offset += count

    for at in range(sum(counts)):
        for j in range(3):
            copy(at, j).wait()


def join_grad(starts, first, pieces, x_turned, full_width, into):
    tokens, width = pieces[0].shape[1:]
    rows = x_turned.shape[0] // 3
    counts = tuple(p.shape[0] for p in pieces)
    extra = () if into is None else (into,)
    blocks = sum(counts)
    return pl.pallas_call(
        functools.partial(join_grad_kernel, first, counts, len(extra)),
        out_shape=(
            jax.ShapeDtypeStruct((3, rows, full_width), jnp.bfloat16),
            vmem_out((1, width), jnp.float32),
        ),
        in_specs=[IN_SMEM, IN_VMEM] + [ANYWHERE] * len(extra) + [IN_VMEM] * len(pieces),
        out_specs=(ANYWHERE, IN_VMEM),
        scratch_shapes=[
            pltpu.VMEM((blocks, 3, rows, width), jnp.bfloat16),
            pltpu.SemaphoreType.DMA((3 * blocks,)),
        ],
        input_output_aliases={2: 0} if extra else {},
        name="join_grad",
        **settings(6 * tokens * rows * width * blocks, 6 * rows * width * blocks, 14 * MIB),
    )(starts, near(x_turned), *extra, *[near(p) for p in pieces])


def cut(total, order, width):
    tokens = total.shape[0]
    blocks = total.reshape(tokens, -1, width).transpose(1, 0, 2)
    blocks = jnp.take(blocks, order // width, axis=0)
    quarter = order.shape[1] // 4
    return blocks[:, :quarter], blocks[:, quarter : 2 * quarter], blocks[:, 2 * quarter :]


def whole(pieces, starts):
    blocks = jnp.take(jnp.concatenate(pieces, axis=0), jnp.argsort(starts[:-1]), axis=0)
    return blocks.transpose(1, 0, 2).reshape(blocks.shape[1], -1)


def contributions(x, group, size):
    return [x] + [exchange(x, m, size) for m in masks_of(group)]


def tree_sum(items):
    while len(items) > 1:
        items = [items[k] + items[k + 1] for k in range(0, len(items), 2)]
    return items[0]


def merge_sums(items):
    peak = functools.reduce(jnp.maximum, [i[0:1] for i in items])
    shifts = [i[0:1] - peak for i in items]
    scales = [jnp.exp(s) for s in shifts]
    return jnp.concatenate(
        [
            peak,
            tree_sum([i[1:2] * c for i, c in zip(items, scales)]),
            tree_sum([(i[2:3] + i[1:2] * s) * c for i, s, c in zip(items, shifts, scales)]),
            tree_sum([i[3:4] for i in items]),
        ],
        axis=0,
    )


def with_token(x, token):
    return x if token is None else (x.astype(jnp.float32) * token).astype(x.dtype)


def reduce_halves(low, high, rest, bits, size, pack, unpack, work):
    got = unpack(exchange(pack(high), 1, size))
    quarter = low.shape[1]
    sent = low + got[:, quarter:]
    passed = [exchange(pack(sent[0]), 2, size), exchange(pack(sent[1]), 4, size)]
    remaining, token = rest(sent)
    token = work(1, remaining, token)
    total = remaining + got[:, :quarter]
    total = total + with_token(unpack(jnp.stack(passed)), token)
    half = quarter // 2
    sent = total[:, half:]
    passed = [exchange(pack(sent[0]), 4, size), exchange(pack(sent[1]), 2, size)]
    token = work(2, sent, None)
    total = total[:, :half] + with_token(unpack(jnp.stack(passed)), token)
    for bit in range(3, bits - 1):
        half = total.shape[1] // 2
        total = total[:, :half] + unpack(exchange(pack(total[:, half:]), 1 << bit, size))
    return total


def gather(held, bits, size, work):
    def flat(x):
        return x.reshape((-1,) + x.shape[2:])

    fresh = held
    across = []
    for bit in range(bits - 2, 2, -1):
        arrived = exchange(held, 1 << bit, size)
        across.append(exchange(fresh, 1, size))
        token = work([flat(fresh)], False)
        fresh = with_token(arrived, token)
        held = jnp.concatenate([held, fresh], axis=1)
    first = [exchange(held[0], 4, size), exchange(held[1], 2, size)]
    across.append(exchange(fresh, 1, size))
    token = work([flat(fresh)], False)
    first = with_token(jnp.stack(first), token)
    across += [first, exchange(first, 1, size)]
    both = jnp.concatenate([held, first], axis=1)
    second = [exchange(both[0], 2, size), exchange(both[1], 4, size)]
    token = work([flat(a) for a in across], False)
    second = with_token(jnp.stack(second), token)
    across = exchange(second, 1, size)
    work([flat(second)], False)
    work([flat(across)], True)


def on_device(size, low_feat, mid_feat, high_feat, w_fc, gain, w_lm, targets):
    me = lax.axis_index("section")
    rows, full_width = w_fc.shape[1], w_fc.shape[2]
    share = w_lm.shape[1]
    tokens = targets.shape[0]
    bits = size.bit_length() - 1
    count, quarter = size // 4, size // 8
    order = (jnp.asarray(reduce_places(bits)) ^ me) * rows
    starts = jnp.concatenate([(jnp.asarray(gather_places(bits)) ^ me) * rows, me[None]])
    kernels = rows % TILE == 0
    target_row = targets.reshape(1, tokens)

    sent = jnp.concatenate(
        [f.reshape(-1, size, rows) for f in (low_feat, mid_feat, high_feat)], axis=2
    ).transpose(1, 0, 2)
    x = lax.all_to_all(sent, "section", split_axis=0, concat_axis=0, tiled=True).reshape(tokens, 3 * rows)

    held = {"logits": jnp.zeros((tokens, share), jnp.float32), "grad_lm": None, "grad_fc": None}
    if kernels:
        high, _, held["x"] = join(order, count, count, x, w_fc, sent, True)
        low, _ = join(order, quarter, quarter, x, w_fc, sent, False)
    else:
        total = jnp.dot(x, w_fc.reshape(3 * rows, full_width), preferred_element_type=jnp.float32)
        remaining, low, high = cut(total, order, rows)

    def join_rest(after):
        return join(order, 0, quarter, x, w_fc, after, False) if kernels else (remaining, None)

    def bring_head(k, after, token):
        if kernels and k == 1:
            held["lm"], token = stage(w_lm, after, rows)
        return token

    total = reduce_halves(low, high, join_rest, bits, size, lambda x: x, lambda x: x, bring_head)
    partner = 1 << (bits - 1)

    def finish(total, pack, unpack, beside):
        passed = unpack(exchange(pack(total), partner, size))
        return total + with_token(jnp.stack([passed[1], passed[0]]), beside(total))

    joined = finish(total, lambda x: x, lambda x: x, lambda after: None)

    squares = jnp.sum(joined * joined, axis=(1, 3))
    squares = squares[0] + squares[1]
    for group in sum_rounds(bits - 1):
        squares = tree_sum(contributions(squares, group, size))
    inv_rms = lax.rsqrt(squares / full_width + epsilon)[:, None]
    gains = jnp.stack([gain, exchange(gain, partner, size)])[:, None, None, :]
    normed = (joined * inv_rms * gains).astype(jnp.bfloat16)

    all_normed, all_dfused = [], []

    def add_logits(pieces, last):
        first = sum(p.shape[0] for p in all_normed)
        all_normed.extend(pieces)
        if kernels:
            held["logits"], extra = head(starts, first, pieces, held["lm"], held["logits"], target_row, last)
            if last:
                held["stats"] = extra
            return extra

    gather(normed, bits, size, add_logits)
    logits = held["logits"]
    if kernels:
        stats = held["stats"][:4]
    else:
        normed_all = whole(all_normed, starts)
        logits = jnp.dot(normed_all, w_lm, preferred_element_type=jnp.float32)
        is_target = (me * share + lax.iota(jnp.int32, share))[None, :] == targets[:, None]
        peak = jnp.max(logits, axis=1)
        shifted = logits - peak[:, None]
        weight = jnp.exp(shifted)
        stats = jnp.stack(
            [
                peak,
                jnp.sum(weight, axis=1),
                jnp.sum(weight * shifted, axis=1),
                jnp.sum(jnp.where(is_target, logits, 0.0), axis=1),
            ]
        )
    for group in sum_rounds(bits):
        stats = merge_sums(contributions(stats, group, size))
    peak, exp_total, exp_moment, picked = stats[0], stats[1], stats[2], stats[3]
    log_total = peak + jnp.log(exp_total)
    token_loss = log_total - picked
    rowdot = ((exp_moment / exp_total - (picked - peak)) / tokens)[:, None] / inv_rms

    if kernels:
        spread = jnp.broadcast_to(log_total[None], (8, tokens))
        high, dlogits = back_first(order, starts, count, count, logits, spread, target_row, held["lm"], rows)
        low, _ = back_rest(order, quarter, quarter, dlogits, held["lm"], rows, high)
    else:
        dlogits = (
            (jnp.exp(logits - log_total[:, None]) - is_target.astype(jnp.float32)) / tokens
        ).astype(jnp.bfloat16)
        total = lax.dot_general(
            dlogits, w_lm, (((1,), (1,)), ((), ())), preferred_element_type=jnp.float32
        )
        left, low, high = cut(total, order, rows)

    def back_last(after):
        return back_rest(order, 0, quarter, dlogits, held["lm"], rows, after) if kernels else (left, None)

    scale = HALF_SCALE * (tokens / 128)

    def pack_half(x):
        return (x * scale).astype(jnp.float16)

    def unpack_half(x):
        return x.astype(jnp.float32) * (1.0 / scale)

    def nothing(k, after, token):
        return token

    total = reduce_halves(low, high, back_last, bits, size, pack_half, unpack_half, nothing)

    def fill_grad_lm(after):
        if kernels:
            held["grad_lm"], token = head_grad(starts, all_normed, dlogits, full_width, after)
            return token

    dnormed = finish(total, pack_half, unpack_half, fill_grad_lm)
    if kernels:
        grad_lm = held["grad_lm"]
    else:
        grad_lm = lax.dot_general(
            normed_all, dlogits, (((0,), (0,)), ((), ())), preferred_element_type=jnp.float32
        ).astype(jnp.bfloat16)

    grad_gain = jnp.sum(dnormed[0, 0] * joined[0, 0] * inv_rms, axis=0)
    dfused = (
        inv_rms * (dnormed * gains) - joined * (inv_rms * inv_rms * inv_rms * rowdot / full_width)
    ).astype(jnp.bfloat16)

    def fill_grad_fc(pieces, last):
        first = sum(p.shape[0] for p in all_dfused)
        all_dfused.extend(pieces)
        if kernels:
            held["grad_fc"], token = join_grad(starts, first, pieces, held["x"], full_width, held["grad_fc"])
            return token

    gather(dfused, bits, size, fill_grad_fc)
    if kernels:
        grad_fc = held["grad_fc"]
    else:
        grad_fc = jnp.dot(x.T, whole(all_dfused, starts), preferred_element_type=jnp.float32)
        grad_fc = grad_fc.astype(jnp.bfloat16).reshape(3, rows, full_width)
    return (token_loss, grad_fc, grad_gain, grad_lm)


def solution(mesh):
    return jax.shard_map(
        functools.partial(on_device, mesh.shape["section"]),
        mesh=mesh,
        in_specs=(
            P(("grp", "section"), None),
            P(("grp", "section"), None),
            P(("grp", "section"), None),
            P(None, "section", None),
            P("section"),
            P(None, "section"),
            P("grp"),
        ),
        out_specs=(P("grp"), P("grp", "section", None), P(("grp", "section")), P("grp", "section")),
        check_vma=False,
    )
```

```python
import functools

import jax
import jax.numpy as jnp
import numpy as np
from jax import lax
from jax.experimental import pallas as pl
from jax.experimental.pallas import tpu as pltpu
from jax.sharding import PartitionSpec as P

epsilon = 1e-06
MIB = 1024 * 1024
HALF_SCALE = 2.0**20
TILE = 256


def reduce_places(bits):
    out = []
    for stream, order in enumerate(([1, 2], [2, 1])):
        order = order + list(range(3, bits - 1))
        spread = [
            sum(((q >> (len(order) - 1 - k)) & 1) << bit for k, bit in enumerate(order))
            for q in range(1 << len(order))
        ]
        spread = [p | (stream << (bits - 1)) for p in spread]
        out.append(spread + [p + 1 for p in spread])
    return np.array(out, np.int32)


def gather_places(bits):
    held = fresh = np.array([[0], [1 << (bits - 1)]], np.int32)
    out, across = [held], []
    for bit in range(bits - 2, 2, -1):
        across.append(fresh ^ 1)
        fresh = held ^ (1 << bit)
        held = np.concatenate([held, fresh], axis=1)
        out.append(fresh)
    over_y, over_z = held ^ 2, held ^ 4
    second = np.stack([over_z[0] ^ 2, over_y[1] ^ 4])
    out += [*across, fresh ^ 1, over_y, over_z, over_y ^ 1, over_z ^ 1, second, second ^ 1]
    return np.concatenate([p.reshape(-1) for p in out]).astype(np.int32)


def masks_of(group):
    return [sum(1 << b for k, b in enumerate(group) if (m >> k) & 1) for m in range(1, 1 << len(group))]


def sum_rounds(top):
    return [[bit] for bit in range(top - 1, 2, -1)] + [[1, 2], [0]]


def exchange(x, mask, size):
    return lax.ppermute(x, "section", [(i, i ^ mask) for i in range(size)])


def settings(flops, bytes_moved, limit):
    return dict(
        compiler_params=pltpu.CompilerParams(vmem_limit_bytes=limit),
        cost_estimate=pl.CostEstimate(flops=flops, bytes_accessed=bytes_moved, transcendentals=0),
    )


ANYWHERE = pl.BlockSpec(memory_space=pl.ANY)
IN_VMEM = pl.BlockSpec(memory_space=pltpu.VMEM)
IN_SMEM = pl.BlockSpec(memory_space=pltpu.SMEM)
vmem_out = pltpu.VMEM


def near(x):
    return pltpu.with_memory_space_constraint(x, pltpu.VMEM)


def far(x):
    return pltpu.with_memory_space_constraint(x, pltpu.HBM)


def stage_kernel(pieces, w_ref, after_ref, out_ref, token_ref, sems):
    copies = []
    for k, piece in enumerate(pieces):
        copies.append(pltpu.make_async_copy(w_ref.at[piece], out_ref.at[piece], sems.at[k]))
    for copy in copies:
        copy.start()
    token_ref[...] = jnp.ones_like(token_ref)
    for copy in copies:
        copy.wait()


def stage(w, after, rows):
    step = w.shape[0] // 16
    pieces = [pl.ds(k * step, step) for k in range(16)]
    return pl.pallas_call(
        functools.partial(stage_kernel, pieces),
        out_shape=(vmem_out(w.shape, w.dtype), vmem_out((1, rows), jnp.float32)),
        in_specs=[ANYWHERE, ANYWHERE],
        out_specs=(IN_VMEM, IN_VMEM),
        scratch_shapes=[pltpu.SemaphoreType.DMA((len(pieces),))],
        name="stage",
        **settings(0, w.size * 2, 2 * MIB),
    )(far(w), after)


def join_kernel(first, count, order, x_ref, w_ref, after_ref, *rest):
    out_ref, token_ref, slots, sems = rest[0], rest[1], rest[-2], rest[-1]
    rows = w_ref.shape[1]
    width = slots.shape[3]

    def copy(q, s):
        column = pl.multiple_of(order[s, first + q], 128)
        at = 2 * q + s
        return pltpu.make_async_copy(w_ref.at[:, :, pl.ds(column, width)], slots.at[at], sems.at[at])

    for q in range(count):
        for s in range(2):
            copy(q, s).start()
    token_ref[...] = jnp.ones_like(token_ref)
    if len(rest) == 5:
        rest[2][...] = x_ref[...].T

    @pl.loop(0, count)
    def _(q):
        for s in range(2):
            copy(q, s).wait()
            for at in range(0, width, TILE):
                total = jnp.dot(
                    x_ref[:, :rows], slots[2 * q + s, 0, :, at : at + TILE], preferred_element_type=jnp.float32
                )
                for j in (1, 2):
                    total += jnp.dot(
                        x_ref[:, j * rows : (j + 1) * rows],
                        slots[2 * q + s, j, :, at : at + TILE],
                        preferred_element_type=jnp.float32,
                    )
                out_ref[s, q, :, at : at + TILE] = total


def join(order, first, count, x, w_fc, after, turn):
    tokens = x.shape[0]
    rows = w_fc.shape[1]
    width = rows
    shapes = [vmem_out((2, count, tokens, width), jnp.float32), vmem_out((1, width), jnp.float32)]
    if turn:
        shapes.append(jax.ShapeDtypeStruct(x.shape[::-1], x.dtype))
    return pl.pallas_call(
        functools.partial(join_kernel, first, count),
        out_shape=tuple(shapes),
        in_specs=[IN_SMEM, IN_VMEM, ANYWHERE, ANYWHERE],
        out_specs=(IN_VMEM,) * len(shapes),
        scratch_shapes=[
            pltpu.VMEM((2 * count, 3, rows, width), jnp.bfloat16),
            pltpu.SemaphoreType.DMA((2 * count,)),
        ],
        name="join",
        **settings(12 * tokens * rows * rows * count, 12 * rows * rows * count, 20 * MIB),
    )(order, near(x), far(w_fc), after)


def columns_of(rows_of_stats):
    count, tokens = rows_of_stats.shape
    padded = jnp.concatenate([rows_of_stats, jnp.zeros((tokens - count, tokens), jnp.float32)], axis=0)
    return padded.T


def target_mask(me, targets_ref, share):
    column = me * share + lax.broadcasted_iota(jnp.int32, (targets_ref.shape[1], share), 1)
    return column == columns_of(targets_ref[...].astype(jnp.float32))[:, :1].astype(jnp.int32)


def head_kernel(first, counts, last, starts, w_ref, before_ref, targets_ref, *rest):
    pieces, (out_ref, extra_ref) = rest[:-2], rest[-2:]
    width = pieces[0].shape[2]
    out_ref[...] = before_ref[...]
    at = first
    for piece_ref, count in zip(pieces, counts):

        @pl.loop(0, count)
        def _(q):
            row = pl.multiple_of(starts[at + q], 128)
            out_ref[...] += jnp.dot(piece_ref[q], w_ref[pl.ds(row, width), :], preferred_element_type=jnp.float32)

        at += count
    if not last:
        extra_ref[...] = jnp.ones_like(extra_ref)
        return
    logits = out_ref[...]
    tokens, share = logits.shape
    peak = jnp.max(logits, axis=1, keepdims=True)
    shifted = logits - peak
    weight = jnp.exp(shifted)
    picked = jnp.where(target_mask(starts[starts.shape[0] - 1], targets_ref, share), logits, 0.0)
    lane = lax.broadcasted_iota(jnp.int32, (tokens, tokens), 1)
    stats = jnp.where(lane == 0, peak, 0.0)
    for k, part in enumerate((weight, weight * shifted, picked)):
        stats = jnp.where(lane == k + 1, jnp.sum(part, axis=1, keepdims=True), stats)
    extra_ref[...] = stats.T[: extra_ref.shape[0]]


def head(starts, first, pieces, w_lm, before, targets, last):
    tokens, width = pieces[0].shape[1:]
    counts = tuple(p.shape[0] for p in pieces)
    share = w_lm.shape[1]
    extra = (8, tokens) if last else (1, width)
    return pl.pallas_call(
        functools.partial(head_kernel, first, counts, last),
        out_shape=(vmem_out(before.shape, jnp.float32), vmem_out(extra, jnp.float32)),
        in_specs=[IN_SMEM] + [IN_VMEM] * (3 + len(pieces)),
        out_specs=(IN_VMEM, IN_VMEM),
        name="head",
        **settings(2 * tokens * width * share * sum(counts), 8 * tokens * share, 6 * MIB),
    )(starts, near(w_lm), near(before), near(targets), *[near(p) for p in pieces])


def back_products(first, count, order, d_ref, w_ref, out_ref):
    width = out_ref.shape[3]

    @pl.loop(0, count)
    def _(q):
        for s in range(2):
            row = pl.multiple_of(order[s, first + q], 128)
            for at in range(0, width, TILE):
                out_ref[s, q, :, at : at + TILE] = lax.dot_general(
                    d_ref[...],
                    w_ref[pl.ds(row + at, TILE), :],
                    (((1,), (1,)), ((), ())),
                    preferred_element_type=jnp.float32,
                )


def back_first_kernel(first, count, order, starts, logits_ref, stats_ref, targets_ref, w_ref, out_ref, d_ref):
    logits = logits_ref[...]
    tokens, share = logits.shape
    log_total = columns_of(stats_ref[...])[:, :1]
    hit = jnp.where(target_mask(starts[starts.shape[0] - 1], targets_ref, share), 1.0, 0.0)
    d_ref[...] = ((jnp.exp(logits - log_total) - hit) / tokens).astype(d_ref.dtype)
    back_products(first, count, order, d_ref, w_ref, out_ref)


def back_first(order, starts, first, count, logits, stats, targets, w_lm, width):
    tokens, share = logits.shape
    return pl.pallas_call(
        functools.partial(back_first_kernel, first, count),
        out_shape=(vmem_out((2, count, tokens, width), jnp.float32), vmem_out((tokens, share), jnp.bfloat16)),
        in_specs=[IN_SMEM] * 2 + [IN_VMEM] * 4,
        out_specs=(IN_VMEM, IN_VMEM),
        name="back_first",
        **settings(4 * tokens * width * share * count, 8 * tokens * width * count, 6 * MIB),
    )(order, starts, near(logits), near(stats), near(targets), near(w_lm))


def back_rest_kernel(first, count, order, d_ref, w_ref, after_ref, out_ref, token_ref):
    token_ref[...] = jnp.ones_like(token_ref)
    back_products(first, count, order, d_ref, w_ref, out_ref)


def back_rest(order, first, count, dlogits, w_lm, width, after):
    tokens, share = dlogits.shape
    return pl.pallas_call(
        functools.partial(back_rest_kernel, first, count),
        out_shape=(vmem_out((2, count, tokens, width), jnp.float32), vmem_out((1, width), jnp.float32)),
        in_specs=[IN_SMEM, IN_VMEM, IN_VMEM, ANYWHERE],
        out_specs=(IN_VMEM, IN_VMEM),
        name="back_rest",
        **settings(4 * tokens * width * share * count, 8 * tokens * width * count, 6 * MIB),
    )(order, near(dlogits), near(w_lm), after)


def head_grad_kernel(counts, starts, d_ref, after_ref, *rest):
    pieces = rest[: len(counts)]
    out_ref, token_ref, slots, sems = rest[-4:]
    width = pieces[0].shape[2]
    share = d_ref.shape[1]
    token_ref[...] = jnp.ones_like(token_ref)

    def copy(at):
        row = pl.multiple_of(starts[at], 128)
        return pltpu.make_async_copy(slots.at[at], out_ref.at[pl.ds(row, width), :], sems.at[at])

    offset = 0
    for piece_ref, count in zip(pieces, counts):

        @pl.loop(0, count)
        def _(q):
            turned = piece_ref[q].T
            for column in range(0, share, TILE):
                slots[offset + q, :, column : column + TILE] = jnp.dot(
                    turned, d_ref[:, column : column + TILE], preferred_element_type=jnp.float32
                ).astype(slots.dtype)
            copy(offset + q).start()

        offset += count

    for at in range(sum(counts)):
        copy(at).wait()


def head_grad(starts, pieces, dlogits, full_width, after):
    tokens, width = pieces[0].shape[1:]
    counts = tuple(p.shape[0] for p in pieces)
    share = dlogits.shape[1]
    blocks = sum(counts)
    return pl.pallas_call(
        functools.partial(head_grad_kernel, counts),
        out_shape=(
            jax.ShapeDtypeStruct((full_width, share), jnp.bfloat16),
            vmem_out((1, width), jnp.float32),
        ),
        in_specs=[IN_SMEM, IN_VMEM, ANYWHERE] + [IN_VMEM] * len(pieces),
        out_specs=(ANYWHERE, IN_VMEM),
        scratch_shapes=[pltpu.VMEM((blocks, width, share), jnp.bfloat16), pltpu.SemaphoreType.DMA((blocks,))],
        name="head_grad",
        **settings(2 * tokens * width * share * blocks, 2 * width * share * blocks, 22 * MIB),
    )(starts, near(dlogits), after, *[near(p) for p in pieces])


def join_grad_kernel(first, counts, aliased, starts, x_ref, *rest):
    pieces = rest[aliased : aliased + len(counts)]
    out_ref, token_ref, slots, sems = rest[-4:]
    rows, width = slots.shape[2:]
    token_ref[...] = jnp.ones_like(token_ref)

    def copy(at, j):
        column = pl.multiple_of(starts[first + at], 128)
        return pltpu.make_async_copy(
            slots.at[at, j], out_ref.at[j, :, pl.ds(column, width)], sems.at[3 * at + j]
        )

    offset = 0
    for piece_ref, count in zip(pieces, counts):

        @pl.loop(0, count)
        def _(q):
            for j in range(3):
                for at in range(0, width, TILE):
                    slots[offset + q, j, :, at : at + TILE] = jnp.dot(
                        x_ref[j * rows : (j + 1) * rows, :],
                        piece_ref[q, :, at : at + TILE],
                        preferred_element_type=jnp.float32,
                    ).astype(slots.dtype)
                copy(offset + q, j).start()

        offset += count

    for at in range(sum(counts)):
        for j in range(3):
            copy(at, j).wait()


def join_grad(starts, first, pieces, x_turned, full_width, into):
    tokens, width = pieces[0].shape[1:]
    rows = x_turned.shape[0] // 3
    counts = tuple(p.shape[0] for p in pieces)
    extra = () if into is None else (into,)
    blocks = sum(counts)
    return pl.pallas_call(
        functools.partial(join_grad_kernel, first, counts, len(extra)),
        out_shape=(
            jax.ShapeDtypeStruct((3, rows, full_width), jnp.bfloat16),
            vmem_out((1, width), jnp.float32),
        ),
        in_specs=[IN_SMEM, IN_VMEM] + [ANYWHERE] * len(extra) + [IN_VMEM] * len(pieces),
        out_specs=(ANYWHERE, IN_VMEM),
        scratch_shapes=[
            pltpu.VMEM((blocks, 3, rows, width), jnp.bfloat16),
            pltpu.SemaphoreType.DMA((3 * blocks,)),
        ],
        input_output_aliases={2: 0} if extra else {},
        name="join_grad",
        **settings(6 * tokens * rows * width * blocks, 6 * rows * width * blocks, 14 * MIB),
    )(starts, near(x_turned), *extra, *[near(p) for p in pieces])


def cut(total, order, width):
    tokens = total.shape[0]
    blocks = total.reshape(tokens, -1, width).transpose(1, 0, 2)
    blocks = jnp.take(blocks, order // width, axis=0)
    quarter = order.shape[1] // 4
    return blocks[:, :quarter], blocks[:, quarter : 2 * quarter], blocks[:, 2 * quarter :]


def whole(pieces, starts):
    blocks = jnp.take(jnp.concatenate(pieces, axis=0), jnp.argsort(starts[:-1]), axis=0)
    return blocks.transpose(1, 0, 2).reshape(blocks.shape[1], -1)


def contributions(x, group, size):
    return [x] + [exchange(x, m, size) for m in masks_of(group)]


def tree_sum(items):
    while len(items) > 1:
        items = [items[k] + items[k + 1] for k in range(0, len(items), 2)]
    return items[0]


def merge_sums(items):
    peak = functools.reduce(jnp.maximum, [i[0:1] for i in items])
    shifts = [i[0:1] - peak for i in items]
    scales = [jnp.exp(s) for s in shifts]
    return jnp.concatenate(
        [
            peak,
            tree_sum([i[1:2] * c for i, c in zip(items, scales)]),
            tree_sum([(i[2:3] + i[1:2] * s) * c for i, s, c in zip(items, shifts, scales)]),
            tree_sum([i[3:4] for i in items]),
        ],
        axis=0,
    )


def with_token(x, token):
    return x if token is None else (x.astype(jnp.float32) * token).astype(x.dtype)


def reduce_halves(low, high, rest, bits, size, pack, unpack, work):
    got = unpack(exchange(pack(high), 1, size))
    quarter = low.shape[1]
    sent = low + got[:, quarter:]
    passed = [exchange(pack(sent[0]), 2, size), exchange(pack(sent[1]), 4, size)]
    remaining, token = rest(sent)
    token = work(1, remaining, token)
    total = remaining + got[:, :quarter]
    total = total + with_token(unpack(jnp.stack(passed)), token)
    half = quarter // 2
    sent = total[:, half:]
    passed = [exchange(pack(sent[0]), 4, size), exchange(pack(sent[1]), 2, size)]
    token = work(2, sent, None)
    total = total[:, :half] + with_token(unpack(jnp.stack(passed)), token)
    for bit in range(3, bits - 1):
        half = total.shape[1] // 2
        total = total[:, :half] + unpack(exchange(pack(total[:, half:]), 1 << bit, size))
    return total


def gather(held, bits, size, work):
    def flat(x):
        return x.reshape((-1,) + x.shape[2:])

    fresh = held
    across = []
    for bit in range(bits - 2, 2, -1):
        arrived = exchange(held, 1 << bit, size)
        across.append(exchange(fresh, 1, size))
        token = work([flat(fresh)], False)
        fresh = with_token(arrived, token)
        held = jnp.concatenate([held, fresh], axis=1)
    over_y, over_z = exchange(held, 2, size), exchange(held, 4, size)
    across.append(exchange(fresh, 1, size))
    token = work([flat(fresh)] + [flat(a) for a in across], False)
    over_y, over_z = with_token(over_y, token), with_token(over_z, token)
    second = [exchange(over_z[0], 2, size), exchange(over_y[1], 4, size)]
    across = [exchange(over_y, 1, size), exchange(over_z, 1, size)]
    token = work([flat(x) for x in (over_y, over_z, *across)], False)
    second = [with_token(x, token) for x in second]
    across = exchange(jnp.stack(second), 1, size)
    work(second, False)
    work([flat(across)], True)


def on_device(size, low_feat, mid_feat, high_feat, w_fc, gain, w_lm, targets):
    me = lax.axis_index("section")
    rows, full_width = w_fc.shape[1], w_fc.shape[2]
    share = w_lm.shape[1]
    tokens = targets.shape[0]
    bits = size.bit_length() - 1
    count, quarter = size // 4, size // 8
    order = (jnp.asarray(reduce_places(bits)) ^ me) * rows
    starts = jnp.concatenate([(jnp.asarray(gather_places(bits)) ^ me) * rows, me[None]])
    kernels = rows % TILE == 0
    target_row = targets.reshape(1, tokens)

    sent = jnp.concatenate(
        [f.reshape(-1, size, rows) for f in (low_feat, mid_feat, high_feat)], axis=2
    ).transpose(1, 0, 2)
    x = lax.all_to_all(sent, "section", split_axis=0, concat_axis=0, tiled=True).reshape(tokens, 3 * rows)

    held = {"logits": jnp.zeros((tokens, share), jnp.float32), "grad_lm": None, "grad_fc": None}
    if kernels:
        high, _, held["x"] = join(order, count, count, x, w_fc, sent, True)
        low, _ = join(order, quarter, quarter, x, w_fc, sent, False)
    else:
        total = jnp.dot(x, w_fc.reshape(3 * rows, full_width), preferred_element_type=jnp.float32)
        remaining, low, high = cut(total, order, rows)

    def join_rest(after):
        return join(order, 0, quarter, x, w_fc, after, False) if kernels else (remaining, None)

    def bring_head(k, after, token):
        if kernels and k == 1:
            held["lm"], token = stage(w_lm, after, rows)
        return token

    total = reduce_halves(low, high, join_rest, bits, size, lambda x: x, lambda x: x, bring_head)
    partner = 1 << (bits - 1)

    def finish(total, pack, unpack, beside):
        passed = unpack(exchange(pack(total), partner, size))
        return total + with_token(jnp.stack([passed[1], passed[0]]), beside(total))

    joined = finish(total, lambda x: x, lambda x: x, lambda after: None)

    squares = jnp.sum(joined * joined, axis=(1, 3))
    squares = squares[0] + squares[1]
    for group in sum_rounds(bits - 1):
        squares = tree_sum(contributions(squares, group, size))
    inv_rms = lax.rsqrt(squares / full_width + epsilon)[:, None]
    gains = jnp.stack([gain, exchange(gain, partner, size)])[:, None, None, :]
    normed = (joined * inv_rms * gains).astype(jnp.bfloat16)

    all_normed, all_dfused = [], []

    def add_logits(pieces, last):
        first = sum(p.shape[0] for p in all_normed)
        all_normed.extend(pieces)
        if kernels:
            held["logits"], extra = head(starts, first, pieces, held["lm"], held["logits"], target_row, last)
            if last:
                held["stats"] = extra
            return extra

    gather(normed, bits, size, add_logits)
    logits = held["logits"]
    if kernels:
        stats = held["stats"][:4]
    else:
        normed_all = whole(all_normed, starts)
        logits = jnp.dot(normed_all, w_lm, preferred_element_type=jnp.float32)
        is_target = (me * share + lax.iota(jnp.int32, share))[None, :] == targets[:, None]
        peak = jnp.max(logits, axis=1)
        shifted = logits - peak[:, None]
        weight = jnp.exp(shifted)
        stats = jnp.stack(
            [
                peak,
                jnp.sum(weight, axis=1),
                jnp.sum(weight * shifted, axis=1),
                jnp.sum(jnp.where(is_target, logits, 0.0), axis=1),
            ]
        )
    for group in sum_rounds(bits):
        stats = merge_sums(contributions(stats, group, size))
    peak, exp_total, exp_moment, picked = stats[0], stats[1], stats[2], stats[3]
    log_total = peak + jnp.log(exp_total)
    token_loss = log_total - picked
    rowdot = ((exp_moment / exp_total - (picked - peak)) / tokens)[:, None] / inv_rms

    if kernels:
        spread = jnp.broadcast_to(log_total[None], (8, tokens))
        high, dlogits = back_first(order, starts, count, count, logits, spread, target_row, held["lm"], rows)
        low, _ = back_rest(order, quarter, quarter, dlogits, held["lm"], rows, high)
    else:
        dlogits = (
            (jnp.exp(logits - log_total[:, None]) - is_target.astype(jnp.float32)) / tokens
        ).astype(jnp.bfloat16)
        total = lax.dot_general(
            dlogits, w_lm, (((1,), (1,)), ((), ())), preferred_element_type=jnp.float32
        )
        left, low, high = cut(total, order, rows)

    def back_last(after):
        return back_rest(order, 0, quarter, dlogits, held["lm"], rows, after) if kernels else (left, None)

    scale = HALF_SCALE * (tokens / 128)

    def pack_half(x):
        return (x * scale).astype(jnp.float16)

    def unpack_half(x):
        return x.astype(jnp.float32) * (1.0 / scale)

    def nothing(k, after, token):
        return token

    total = reduce_halves(low, high, back_last, bits, size, pack_half, unpack_half, nothing)

    def fill_grad_lm(after):
        if kernels:
            held["grad_lm"], token = head_grad(starts, all_normed, dlogits, full_width, after)
            return token

    dnormed = finish(total, pack_half, unpack_half, fill_grad_lm)
    if kernels:
        grad_lm = held["grad_lm"]
    else:
        grad_lm = lax.dot_general(
            normed_all, dlogits, (((0,), (0,)), ((), ())), preferred_element_type=jnp.float32
        ).astype(jnp.bfloat16)

    grad_gain = jnp.sum(dnormed[0, 0] * joined[0, 0] * inv_rms, axis=0)
    dfused = (
        inv_rms * (dnormed * gains) - joined * (inv_rms * inv_rms * inv_rms * rowdot / full_width)
    ).astype(jnp.bfloat16)

    def fill_grad_fc(pieces, last):
        first = sum(p.shape[0] for p in all_dfused)
        all_dfused.extend(pieces)
        if kernels:
            held["grad_fc"], token = join_grad(starts, first, pieces, held["x"], full_width, held["grad_fc"])
            return token

    gather(dfused, bits, size, fill_grad_fc)
    if kernels:
        grad_fc = held["grad_fc"]
    else:
        grad_fc = jnp.dot(x.T, whole(all_dfused, starts), preferred_element_type=jnp.float32)
        grad_fc = grad_fc.astype(jnp.bfloat16).reshape(3, rows, full_width)
    return (token_loss, grad_fc, grad_gain, grad_lm)


def solution(mesh):
    return jax.shard_map(
        functools.partial(on_device, mesh.shape["section"]),
        mesh=mesh,
        in_specs=(
            P(("grp", "section"), None),
            P(("grp", "section"), None),
            P(("grp", "section"), None),
            P(None, "section", None),
            P("section"),
            P(None, "section"),
            P("grp"),
        ),
        out_specs=(P("grp"), P("grp", "section", None), P(("grp", "section")), P("grp", "section")),
        check_vma=False,
    )
```

```python
import functools

import jax
import jax.numpy as jnp
import numpy as np
from jax import lax
from jax.experimental import pallas as pl
from jax.experimental.pallas import tpu as pltpu
from jax.sharding import PartitionSpec as P

epsilon = 1e-06
MIB = 1024 * 1024
HALF_SCALE = 2.0**20
TILE = 256


def reduce_places(bits):
    out = []
    for stream, order in enumerate(([1, 2], [2, 1])):
        order = order + list(range(3, bits - 1))
        spread = [
            sum(((q >> (len(order) - 1 - k)) & 1) << bit for k, bit in enumerate(order))
            for q in range(1 << len(order))
        ]
        spread = [p | (stream << (bits - 1)) for p in spread]
        out.append(spread + [p + 1 for p in spread])
    return np.array(out, np.int32)


def gather_places(bits):
    held = fresh = np.array([[0], [1 << (bits - 1)]], np.int32)
    out, across = [held], []
    for bit in range(bits - 2, 2, -1):
        across.append(fresh ^ 1)
        fresh = held ^ (1 << bit)
        held = np.concatenate([held, fresh], axis=1)
        out.append(fresh)
    over_y, over_z = held ^ 2, held ^ 4
    second = np.stack([over_z[0] ^ 2, over_y[1] ^ 4])
    out += [*across, fresh ^ 1, over_y, over_z, over_y ^ 1, over_z ^ 1, second, second ^ 1]
    return np.concatenate([p.reshape(-1) for p in out]).astype(np.int32)


def masks_of(group):
    return [sum(1 << b for k, b in enumerate(group) if (m >> k) & 1) for m in range(1, 1 << len(group))]


def sum_rounds(top):
    return [[bit] for bit in range(top - 1, 2, -1)] + [[1, 2], [0]]


def exchange(x, mask, size):
    return lax.ppermute(x, "section", [(i, i ^ mask) for i in range(size)])


def settings(flops, bytes_moved, limit):
    return dict(
        compiler_params=pltpu.CompilerParams(vmem_limit_bytes=limit),
        cost_estimate=pl.CostEstimate(flops=flops, bytes_accessed=bytes_moved, transcendentals=0),
    )


ANYWHERE = pl.BlockSpec(memory_space=pl.ANY)
IN_VMEM = pl.BlockSpec(memory_space=pltpu.VMEM)
IN_SMEM = pl.BlockSpec(memory_space=pltpu.SMEM)
vmem_out = pltpu.VMEM


def near(x):
    return pltpu.with_memory_space_constraint(x, pltpu.VMEM)


def far(x):
    return pltpu.with_memory_space_constraint(x, pltpu.HBM)


def stage_kernel(pieces, w_ref, after_ref, out_ref, token_ref, sems):
    copies = []
    for k, piece in enumerate(pieces):
        copies.append(pltpu.make_async_copy(w_ref.at[piece], out_ref.at[piece], sems.at[k]))
    for copy in copies:
        copy.start()
    token_ref[...] = jnp.ones_like(token_ref)
    for copy in copies:
        copy.wait()


def stage(w, after, rows):
    step = w.shape[0] // 16
    pieces = [pl.ds(k * step, step) for k in range(16)]
    return pl.pallas_call(
        functools.partial(stage_kernel, pieces),
        out_shape=(vmem_out(w.shape, w.dtype), vmem_out((1, rows), jnp.float32)),
        in_specs=[ANYWHERE, ANYWHERE],
        out_specs=(IN_VMEM, IN_VMEM),
        scratch_shapes=[pltpu.SemaphoreType.DMA((len(pieces),))],
        name="stage",
        **settings(0, w.size * 2, 2 * MIB),
    )(far(w), after)


def join_kernel(first, count, order, x_ref, w_ref, after_ref, *rest):
    out_ref, token_ref, slots, sems = rest[0], rest[1], rest[-2], rest[-1]
    rows = w_ref.shape[1]
    width = slots.shape[3]

    def copy(q, s):
        column = pl.multiple_of(order[s, first + q], 128)
        at = 2 * q + s
        return pltpu.make_async_copy(w_ref.at[:, :, pl.ds(column, width)], slots.at[at], sems.at[at])

    for q in range(count):
        for s in range(2):
            copy(q, s).start()
    token_ref[...] = jnp.ones_like(token_ref)
    if len(rest) == 5:
        rest[2][...] = x_ref[...].T

    @pl.loop(0, count)
    def _(q):
        for s in range(2):
            copy(q, s).wait()
            for at in range(0, width, TILE):
                total = jnp.dot(
                    x_ref[:, :rows], slots[2 * q + s, 0, :, at : at + TILE], preferred_element_type=jnp.float32
                )
                for j in (1, 2):
                    total += jnp.dot(
                        x_ref[:, j * rows : (j + 1) * rows],
                        slots[2 * q + s, j, :, at : at + TILE],
                        preferred_element_type=jnp.float32,
                    )
                out_ref[s, q, :, at : at + TILE] = total


def join(order, first, count, x, w_fc, after, turn):
    tokens = x.shape[0]
    rows = w_fc.shape[1]
    width = rows
    shapes = [vmem_out((2, count, tokens, width), jnp.float32), vmem_out((1, width), jnp.float32)]
    if turn:
        shapes.append(jax.ShapeDtypeStruct(x.shape[::-1], x.dtype))
    return pl.pallas_call(
        functools.partial(join_kernel, first, count),
        out_shape=tuple(shapes),
        in_specs=[IN_SMEM, IN_VMEM, ANYWHERE, ANYWHERE],
        out_specs=(IN_VMEM,) * len(shapes),
        scratch_shapes=[
            pltpu.VMEM((2 * count, 3, rows, width), jnp.bfloat16),
            pltpu.SemaphoreType.DMA((2 * count,)),
        ],
        name="join",
        **settings(12 * tokens * rows * rows * count, 12 * rows * rows * count, 20 * MIB),
    )(order, near(x), far(w_fc), after)


def columns_of(rows_of_stats):
    count, tokens = rows_of_stats.shape
    padded = jnp.concatenate([rows_of_stats, jnp.zeros((tokens - count, tokens), jnp.float32)], axis=0)
    return padded.T


def target_mask(me, targets_ref, share):
    column = me * share + lax.broadcasted_iota(jnp.int32, (targets_ref.shape[1], share), 1)
    return column == columns_of(targets_ref[...].astype(jnp.float32))[:, :1].astype(jnp.int32)


def head_kernel(first, counts, last, starts, w_ref, before_ref, targets_ref, *rest):
    pieces, (out_ref, extra_ref) = rest[:-2], rest[-2:]
    width = pieces[0].shape[2]
    out_ref[...] = before_ref[...]
    at = first
    for piece_ref, count in zip(pieces, counts):

        @pl.loop(0, count)
        def _(q):
            row = pl.multiple_of(starts[at + q], 128)
            out_ref[...] += jnp.dot(piece_ref[q], w_ref[pl.ds(row, width), :], preferred_element_type=jnp.float32)

        at += count
    if not last:
        extra_ref[...] = jnp.ones_like(extra_ref)
        return
    logits = out_ref[...]
    tokens, share = logits.shape
    peak = jnp.max(logits, axis=1, keepdims=True)
    shifted = logits - peak
    weight = jnp.exp(shifted)
    picked = jnp.where(target_mask(starts[starts.shape[0] - 1], targets_ref, share), logits, 0.0)
    lane = lax.broadcasted_iota(jnp.int32, (tokens, tokens), 1)
    stats = jnp.where(lane == 0, peak, 0.0)
    for k, part in enumerate((weight, weight * shifted, picked)):
        stats = jnp.where(lane == k + 1, jnp.sum(part, axis=1, keepdims=True), stats)
    extra_ref[...] = stats.T[: extra_ref.shape[0]]


def head(starts, first, pieces, w_lm, before, targets, last):
    tokens, width = pieces[0].shape[1:]
    counts = tuple(p.shape[0] for p in pieces)
    share = w_lm.shape[1]
    extra = (8, tokens) if last else (1, width)
    return pl.pallas_call(
        functools.partial(head_kernel, first, counts, last),
        out_shape=(vmem_out(before.shape, jnp.float32), vmem_out(extra, jnp.float32)),
        in_specs=[IN_SMEM] + [IN_VMEM] * (3 + len(pieces)),
        out_specs=(IN_VMEM, IN_VMEM),
        name="head",
        **settings(2 * tokens * width * share * sum(counts), 8 * tokens * share, 6 * MIB),
    )(starts, near(w_lm), near(before), near(targets), *[near(p) for p in pieces])


def back_products(first, count, order, d_ref, w_ref, out_ref):
    width = out_ref.shape[3]

    @pl.loop(0, count)
    def _(q):
        for s in range(2):
            row = pl.multiple_of(order[s, first + q], 128)
            for at in range(0, width, TILE):
                out_ref[s, q, :, at : at + TILE] = lax.dot_general(
                    d_ref[...],
                    w_ref[pl.ds(row + at, TILE), :],
                    (((1,), (1,)), ((), ())),
                    preferred_element_type=jnp.float32,
                )


def back_first_kernel(first, count, order, starts, logits_ref, stats_ref, targets_ref, w_ref, out_ref, d_ref):
    logits = logits_ref[...]
    tokens, share = logits.shape
    log_total = columns_of(stats_ref[...])[:, :1]
    hit = jnp.where(target_mask(starts[starts.shape[0] - 1], targets_ref, share), 1.0, 0.0)
    d_ref[...] = ((jnp.exp(logits - log_total) - hit) / tokens).astype(d_ref.dtype)
    back_products(first, count, order, d_ref, w_ref, out_ref)


def back_first(order, starts, first, count, logits, stats, targets, w_lm, width):
    tokens, share = logits.shape
    return pl.pallas_call(
        functools.partial(back_first_kernel, first, count),
        out_shape=(vmem_out((2, count, tokens, width), jnp.float32), vmem_out((tokens, share), jnp.bfloat16)),
        in_specs=[IN_SMEM] * 2 + [IN_VMEM] * 4,
        out_specs=(IN_VMEM, IN_VMEM),
        name="back_first",
        **settings(4 * tokens * width * share * count, 8 * tokens * width * count, 6 * MIB),
    )(order, starts, near(logits), near(stats), near(targets), near(w_lm))


def back_rest_kernel(first, count, order, d_ref, w_ref, after_ref, out_ref, token_ref):
    token_ref[...] = jnp.ones_like(token_ref)
    back_products(first, count, order, d_ref, w_ref, out_ref)


def back_rest(order, first, count, dlogits, w_lm, width, after):
    tokens, share = dlogits.shape
    return pl.pallas_call(
        functools.partial(back_rest_kernel, first, count),
        out_shape=(vmem_out((2, count, tokens, width), jnp.float32), vmem_out((1, width), jnp.float32)),
        in_specs=[IN_SMEM, IN_VMEM, IN_VMEM, ANYWHERE],
        out_specs=(IN_VMEM, IN_VMEM),
        name="back_rest",
        **settings(4 * tokens * width * share * count, 8 * tokens * width * count, 6 * MIB),
    )(order, near(dlogits), near(w_lm), after)


def head_grad_kernel(counts, starts, d_ref, after_ref, *rest):
    pieces = rest[: len(counts)]
    out_ref, token_ref, slots, sems = rest[-4:]
    width = pieces[0].shape[2]
    share = d_ref.shape[1]
    token_ref[...] = jnp.ones_like(token_ref)

    def copy(at):
        row = pl.multiple_of(starts[at], 128)
        return pltpu.make_async_copy(slots.at[at], out_ref.at[pl.ds(row, width), :], sems.at[at])

    offset = 0
    for piece_ref, count in zip(pieces, counts):

        @pl.loop(0, count)
        def _(q):
            turned = piece_ref[q].T
            for column in range(0, share, TILE):
                slots[offset + q, :, column : column + TILE] = jnp.dot(
                    turned, d_ref[:, column : column + TILE], preferred_element_type=jnp.float32
                ).astype(slots.dtype)
            copy(offset + q).start()

        offset += count

    for at in range(sum(counts)):
        copy(at).wait()


def head_grad(starts, pieces, dlogits, full_width, after):
    tokens, width = pieces[0].shape[1:]
    counts = tuple(p.shape[0] for p in pieces)
    share = dlogits.shape[1]
    blocks = sum(counts)
    return pl.pallas_call(
        functools.partial(head_grad_kernel, counts),
        out_shape=(
            jax.ShapeDtypeStruct((full_width, share), jnp.bfloat16),
            vmem_out((1, width), jnp.float32),
        ),
        in_specs=[IN_SMEM, IN_VMEM, ANYWHERE] + [IN_VMEM] * len(pieces),
        out_specs=(ANYWHERE, IN_VMEM),
        scratch_shapes=[pltpu.VMEM((blocks, width, share), jnp.bfloat16), pltpu.SemaphoreType.DMA((blocks,))],
        name="head_grad",
        **settings(2 * tokens * width * share * blocks, 2 * width * share * blocks, 22 * MIB),
    )(starts, near(dlogits), after, *[near(p) for p in pieces])


def join_grad_kernel(first, counts, aliased, starts, x_ref, *rest):
    pieces = rest[aliased : aliased + len(counts)]
    out_ref, token_ref, slots, sems = rest[-4:]
    rows, width = slots.shape[2:]
    token_ref[...] = jnp.ones_like(token_ref)

    def copy(at, j):
        column = pl.multiple_of(starts[first + at], 128)
        return pltpu.make_async_copy(
            slots.at[at, j], out_ref.at[j, :, pl.ds(column, width)], sems.at[3 * at + j]
        )

    offset = 0
    for piece_ref, count in zip(pieces, counts):

        @pl.loop(0, count)
        def _(q):
            for j in range(3):
                for at in range(0, width, TILE):
                    slots[offset + q, j, :, at : at + TILE] = jnp.dot(
                        x_ref[j * rows : (j + 1) * rows, :],
                        piece_ref[q, :, at : at + TILE],
                        preferred_element_type=jnp.float32,
                    ).astype(slots.dtype)
                copy(offset + q, j).start()

        offset += count

    for at in range(sum(counts)):
        for j in range(3):
            copy(at, j).wait()


def join_grad(starts, first, pieces, x_turned, full_width, into):
    tokens, width = pieces[0].shape[1:]
    rows = x_turned.shape[0] // 3
    counts = tuple(p.shape[0] for p in pieces)
    extra = () if into is None else (into,)
    blocks = sum(counts)
    return pl.pallas_call(
        functools.partial(join_grad_kernel, first, counts, len(extra)),
        out_shape=(
            jax.ShapeDtypeStruct((3, rows, full_width), jnp.bfloat16),
            vmem_out((1, width), jnp.float32),
        ),
        in_specs=[IN_SMEM, IN_VMEM] + [ANYWHERE] * len(extra) + [IN_VMEM] * len(pieces),
        out_specs=(ANYWHERE, IN_VMEM),
        scratch_shapes=[
            pltpu.VMEM((blocks, 3, rows, width), jnp.bfloat16),
            pltpu.SemaphoreType.DMA((3 * blocks,)),
        ],
        input_output_aliases={2: 0} if extra else {},
        name="join_grad",
        **settings(6 * tokens * rows * width * blocks, 6 * rows * width * blocks, 14 * MIB),
    )(starts, near(x_turned), *extra, *[near(p) for p in pieces])


def cut(total, order, width):
    tokens = total.shape[0]
    blocks = total.reshape(tokens, -1, width).transpose(1, 0, 2)
    blocks = jnp.take(blocks, order // width, axis=0)
    quarter = order.shape[1] // 4
    return blocks[:, :quarter], blocks[:, quarter : 2 * quarter], blocks[:, 2 * quarter :]


def whole(pieces, starts):
    blocks = jnp.take(jnp.concatenate(pieces, axis=0), jnp.argsort(starts[:-1]), axis=0)
    return blocks.transpose(1, 0, 2).reshape(blocks.shape[1], -1)


def contributions(x, group, size):
    return [x] + [exchange(x, m, size) for m in masks_of(group)]


def tree_sum(items):
    while len(items) > 1:
        items = [items[k] + items[k + 1] for k in range(0, len(items), 2)]
    return items[0]


def merge_sums(items):
    peak = functools.reduce(jnp.maximum, [i[0:1] for i in items])
    shifts = [i[0:1] - peak for i in items]
    scales = [jnp.exp(s) for s in shifts]
    return jnp.concatenate(
        [
            peak,
            tree_sum([i[1:2] * c for i, c in zip(items, scales)]),
            tree_sum([(i[2:3] + i[1:2] * s) * c for i, s, c in zip(items, shifts, scales)]),
            tree_sum([i[3:4] for i in items]),
        ],
        axis=0,
    )


def with_token(x, token):
    return x if token is None else (x.astype(jnp.float32) * token).astype(x.dtype)


def reduce_halves(low, high, rest, bits, size, pack, unpack, work):
    got = unpack(exchange(pack(high), 1, size))
    quarter = low.shape[1]
    sent = low + got[:, quarter:]
    passed = [exchange(pack(sent[0]), 2, size), exchange(pack(sent[1]), 4, size)]
    remaining, token = rest(sent)
    token = work(1, remaining, token)
    total = remaining + got[:, :quarter]
    total = total + with_token(unpack(jnp.stack(passed)), token)
    half = quarter // 2
    sent = total[:, half:]
    passed = [exchange(pack(sent[0]), 4, size), exchange(pack(sent[1]), 2, size)]
    token = work(2, sent, None)
    total = total[:, :half] + with_token(unpack(jnp.stack(passed)), token)
    for bit in range(3, bits - 1):
        half = total.shape[1] // 2
        total = total[:, :half] + unpack(exchange(pack(total[:, half:]), 1 << bit, size))
    return total


def gather(held, bits, size, work):
    def flat(x):
        return x.reshape((-1,) + x.shape[2:])

    fresh = held
    across = []
    for bit in range(bits - 2, 2, -1):
        arrived = exchange(held, 1 << bit, size)
        across.append(exchange(fresh, 1, size))
        token = work([flat(fresh)], False)
        fresh = with_token(arrived, token)
        held = jnp.concatenate([held, fresh], axis=1)
    over_y, over_z = exchange(held, 2, size), exchange(held, 4, size)
    across.append(exchange(fresh, 1, size))
    token = work([flat(fresh)] + [flat(a) for a in across], False)
    over_y, over_z = with_token(over_y, token), with_token(over_z, token)
    second = [exchange(over_z[0], 2, size), exchange(over_y[1], 4, size)]
    across = [exchange(over_y, 1, size), exchange(over_z, 1, size)]
    token = work([flat(x) for x in (over_y, over_z, *across)], False)
    second = [with_token(x, token) for x in second]
    across = exchange(jnp.stack(second), 1, size)
    work(second, False)
    work([flat(across)], True)


def on_device(size, low_feat, mid_feat, high_feat, w_fc, gain, w_lm, targets):
    me = lax.axis_index("section")
    rows, full_width = w_fc.shape[1], w_fc.shape[2]
    share = w_lm.shape[1]
    tokens = targets.shape[0]
    bits = size.bit_length() - 1
    count, quarter = size // 4, size // 8
    order = (jnp.asarray(reduce_places(bits)) ^ me) * rows
    starts = jnp.concatenate([(jnp.asarray(gather_places(bits)) ^ me) * rows, me[None]])
    kernels = rows % TILE == 0
    target_row = targets.reshape(1, tokens)

    sent = jnp.concatenate(
        [f.reshape(-1, size, rows) for f in (low_feat, mid_feat, high_feat)], axis=2
    ).transpose(1, 0, 2)
    x = lax.all_to_all(sent, "section", split_axis=0, concat_axis=0, tiled=True).reshape(tokens, 3 * rows)

    held = {"logits": jnp.zeros((tokens, share), jnp.float32), "grad_lm": None, "grad_fc": None}
    if kernels:
        high, _, held["x"] = join(order, count, count, x, w_fc, sent, True)
        low, _ = join(order, quarter, quarter, x, w_fc, sent, False)
    else:
        total = jnp.dot(x, w_fc.reshape(3 * rows, full_width), preferred_element_type=jnp.float32)
        remaining, low, high = cut(total, order, rows)

    def join_rest(after):
        return join(order, 0, quarter, x, w_fc, after, False) if kernels else (remaining, None)

    def bring_head(k, after, token):
        if kernels and k == 1:
            held["lm"], token = stage(w_lm, after, rows)
        return token

    total = reduce_halves(low, high, join_rest, bits, size, lambda x: x, lambda x: x, bring_head)
    partner = 1 << (bits - 1)

    def finish(total, pack, unpack, beside):
        passed = unpack(exchange(pack(total), partner, size))
        return total + with_token(jnp.stack([passed[1], passed[0]]), beside(total))

    own = total[0] + exchange(total[1], partner, size)
    other = exchange(own, partner, size)
    joined = jnp.stack([own, other])

    squares = jnp.sum(own * own, axis=(0, 2))
    rounds = sum_rounds(bits)
    for group in rounds:
        if group is rounds[-1]:
            squares = squares * (other[0, 0, :1] * 0.0 + 1.0)
        squares = tree_sum(contributions(squares, group, size))
    inv_rms = lax.rsqrt(squares / full_width + epsilon)[:, None]
    gains = jnp.stack([gain, exchange(gain, partner, size)])[:, None, None, :]
    normed = (joined * inv_rms * gains).astype(jnp.bfloat16)

    all_normed, all_dfused = [], []

    def add_logits(pieces, last):
        first = sum(p.shape[0] for p in all_normed)
        all_normed.extend(pieces)
        if kernels:
            held["logits"], extra = head(starts, first, pieces, held["lm"], held["logits"], target_row, last)
            if last:
                held["stats"] = extra
            return extra

    gather(normed, bits, size, add_logits)
    logits = held["logits"]
    if kernels:
        stats = held["stats"][:4]
    else:
        normed_all = whole(all_normed, starts)
        logits = jnp.dot(normed_all, w_lm, preferred_element_type=jnp.float32)
        is_target = (me * share + lax.iota(jnp.int32, share))[None, :] == targets[:, None]
        peak = jnp.max(logits, axis=1)
        shifted = logits - peak[:, None]
        weight = jnp.exp(shifted)
        stats = jnp.stack(
            [
                peak,
                jnp.sum(weight, axis=1),
                jnp.sum(weight * shifted, axis=1),
                jnp.sum(jnp.where(is_target, logits, 0.0), axis=1),
            ]
        )
    for group in sum_rounds(bits):
        stats = merge_sums(contributions(stats, group, size))
    peak, exp_total, exp_moment, picked = stats[0], stats[1], stats[2], stats[3]
    log_total = peak + jnp.log(exp_total)
    token_loss = log_total - picked
    rowdot = ((exp_moment / exp_total - (picked - peak)) / tokens)[:, None] / inv_rms

    if kernels:
        spread = jnp.broadcast_to(log_total[None], (8, tokens))
        high, dlogits = back_first(order, starts, count, count, logits, spread, target_row, held["lm"], rows)
        low, _ = back_rest(order, quarter, quarter, dlogits, held["lm"], rows, high)
    else:
        dlogits = (
            (jnp.exp(logits - log_total[:, None]) - is_target.astype(jnp.float32)) / tokens
        ).astype(jnp.bfloat16)
        total = lax.dot_general(
            dlogits, w_lm, (((1,), (1,)), ((), ())), preferred_element_type=jnp.float32
        )
        left, low, high = cut(total, order, rows)

    def back_last(after):
        return back_rest(order, 0, quarter, dlogits, held["lm"], rows, after) if kernels else (left, None)

    scale = HALF_SCALE * (tokens / 128)

    def pack_half(x):
        return (x * scale).astype(jnp.float16)

    def unpack_half(x):
        return x.astype(jnp.float32) * (1.0 / scale)

    def nothing(k, after, token):
        return token

    total = reduce_halves(low, high, back_last, bits, size, pack_half, unpack_half, nothing)

    def fill_grad_lm(after):
        if kernels:
            held["grad_lm"], token = head_grad(starts, all_normed, dlogits, full_width, after)
            return token

    dnormed = finish(total, pack_half, unpack_half, fill_grad_lm)
    if kernels:
        grad_lm = held["grad_lm"]
    else:
        grad_lm = lax.dot_general(
            normed_all, dlogits, (((0,), (0,)), ((), ())), preferred_element_type=jnp.float32
        ).astype(jnp.bfloat16)

    grad_gain = jnp.sum(dnormed[0, 0] * joined[0, 0] * inv_rms, axis=0)
    dfused = (
        inv_rms * (dnormed * gains) - joined * (inv_rms * inv_rms * inv_rms * rowdot / full_width)
    ).astype(jnp.bfloat16)

    def fill_grad_fc(pieces, last):
        first = sum(p.shape[0] for p in all_dfused)
        all_dfused.extend(pieces)
        if kernels:
            held["grad_fc"], token = join_grad(starts, first, pieces, held["x"], full_width, held["grad_fc"])
            return token

    gather(dfused, bits, size, fill_grad_fc)
    if kernels:
        grad_fc = held["grad_fc"]
    else:
        grad_fc = jnp.dot(x.T, whole(all_dfused, starts), preferred_element_type=jnp.float32)
        grad_fc = grad_fc.astype(jnp.bfloat16).reshape(3, rows, full_width)
    return (token_loss, grad_fc, grad_gain, grad_lm)


def solution(mesh):
    return jax.shard_map(
        functools.partial(on_device, mesh.shape["section"]),
        mesh=mesh,
        in_specs=(
            P(("grp", "section"), None),
            P(("grp", "section"), None),
            P(("grp", "section"), None),
            P(None, "section", None),
            P("section"),
            P(None, "section"),
            P("grp"),
        ),
        out_specs=(P("grp"), P("grp", "section", None), P(("grp", "section")), P("grp", "section")),
        check_vma=False,
    )
```

```python
import functools

import jax
import jax.numpy as jnp
import numpy as np
from jax import lax
from jax.experimental import pallas as pl
from jax.experimental.pallas import tpu as pltpu
from jax.sharding import PartitionSpec as P

epsilon = 1e-06
MIB = 1024 * 1024
HALF_SCALE = 2.0**20
TILE = 256


def reduce_places(bits):
    out = []
    for stream, order in enumerate(([1, 2], [2, 1])):
        order = order + list(range(3, bits - 1))
        spread = [
            sum(((q >> (len(order) - 1 - k)) & 1) << bit for k, bit in enumerate(order))
            for q in range(1 << len(order))
        ]
        spread = [p | (stream << (bits - 1)) for p in spread]
        out.append(spread + [p + 1 for p in spread])
    return np.array(out, np.int32)


def gather_places(bits):
    held = fresh = np.array([[0], [1 << (bits - 1)]], np.int32)
    out, across = [held], []
    for bit in range(bits - 2, 2, -1):
        across.append(fresh ^ 1)
        fresh = held ^ (1 << bit)
        held = np.concatenate([held, fresh], axis=1)
        out.append(fresh)
    over_y, over_z = held ^ 2, held ^ 4
    second = np.stack([over_z[0] ^ 2, over_y[1] ^ 4])
    out += [*across, fresh ^ 1, over_y, over_z, over_y ^ 1, over_z ^ 1, second, second ^ 1]
    return np.concatenate([p.reshape(-1) for p in out]).astype(np.int32)


def gather_crossing_places(bits):
    held = fresh = np.array([[0], [1 << (bits - 1)]], np.int32)
    out, across = [held], []
    for bit in range(bits - 2, 2, -1):
        across.append(fresh ^ 1)
        fresh = held ^ (1 << bit)
        held = np.concatenate([held, fresh], axis=1)
        out.append(fresh)
    first = held ^ np.array([[4], [2]], np.int32)
    second = np.concatenate([held, first], axis=1) ^ np.array([[2], [4]], np.int32)
    out += [*across, fresh ^ 1, first, first ^ 1, second, second ^ 1]
    return np.concatenate([p.reshape(-1) for p in out]).astype(np.int32)


def masks_of(group):
    return [sum(1 << b for k, b in enumerate(group) if (m >> k) & 1) for m in range(1, 1 << len(group))]


def sum_rounds(top):
    return [[bit] for bit in range(top - 1, 2, -1)] + [[1, 2], [0]]


def exchange(x, mask, size):
    return lax.ppermute(x, "section", [(i, i ^ mask) for i in range(size)])


def settings(flops, bytes_moved, limit):
    return dict(
        compiler_params=pltpu.CompilerParams(vmem_limit_bytes=limit),
        cost_estimate=pl.CostEstimate(flops=flops, bytes_accessed=bytes_moved, transcendentals=0),
    )


ANYWHERE = pl.BlockSpec(memory_space=pl.ANY)
IN_VMEM = pl.BlockSpec(memory_space=pltpu.VMEM)
IN_SMEM = pl.BlockSpec(memory_space=pltpu.SMEM)
vmem_out = pltpu.VMEM


def near(x):
    return pltpu.with_memory_space_constraint(x, pltpu.VMEM)


def far(x):
    return pltpu.with_memory_space_constraint(x, pltpu.HBM)


def stage_kernel(pieces, w_ref, after_ref, out_ref, token_ref, sems):
    copies = []
    for k, piece in enumerate(pieces):
        copies.append(pltpu.make_async_copy(w_ref.at[piece], out_ref.at[piece], sems.at[k]))
    for copy in copies:
        copy.start()
    token_ref[...] = jnp.ones_like(token_ref)
    for copy in copies:
        copy.wait()


def stage(w, after, rows):
    step = w.shape[0] // 16
    pieces = [pl.ds(k * step, step) for k in range(16)]
    return pl.pallas_call(
        functools.partial(stage_kernel, pieces),
        out_shape=(vmem_out(w.shape, w.dtype), vmem_out((1, rows), jnp.float32)),
        in_specs=[ANYWHERE, ANYWHERE],
        out_specs=(IN_VMEM, IN_VMEM),
        scratch_shapes=[pltpu.SemaphoreType.DMA((len(pieces),))],
        name="stage",
        **settings(0, w.size * 2, 2 * MIB),
    )(far(w), after)


def join_kernel(first, count, order, x_ref, w_ref, after_ref, *rest):
    out_ref, token_ref, slots, sems = rest[0], rest[1], rest[-2], rest[-1]
    rows = w_ref.shape[1]
    width = slots.shape[3]

    def copy(q, s):
        column = pl.multiple_of(order[s, first + q], 128)
        at = 2 * q + s
        return pltpu.make_async_copy(w_ref.at[:, :, pl.ds(column, width)], slots.at[at], sems.at[at])

    for q in range(count):
        for s in range(2):
            copy(q, s).start()
    token_ref[...] = jnp.ones_like(token_ref)
    if len(rest) == 5:
        rest[2][...] = x_ref[...].T

    @pl.loop(0, count)
    def _(q):
        for s in range(2):
            copy(q, s).wait()
            for at in range(0, width, TILE):
                total = jnp.dot(
                    x_ref[:, :rows], slots[2 * q + s, 0, :, at : at + TILE], preferred_element_type=jnp.float32
                )
                for j in (1, 2):
                    total += jnp.dot(
                        x_ref[:, j * rows : (j + 1) * rows],
                        slots[2 * q + s, j, :, at : at + TILE],
                        preferred_element_type=jnp.float32,
                    )
                out_ref[s, q, :, at : at + TILE] = total


def join(order, first, count, x, w_fc, after, turn):
    tokens = x.shape[0]
    rows = w_fc.shape[1]
    width = rows
    shapes = [vmem_out((2, count, tokens, width), jnp.float32), vmem_out((1, width), jnp.float32)]
    if turn:
        shapes.append(jax.ShapeDtypeStruct(x.shape[::-1], x.dtype))
    return pl.pallas_call(
        functools.partial(join_kernel, first, count),
        out_shape=tuple(shapes),
        in_specs=[IN_SMEM, IN_VMEM, ANYWHERE, ANYWHERE],
        out_specs=(IN_VMEM,) * len(shapes),
        scratch_shapes=[
            pltpu.VMEM((2 * count, 3, rows, width), jnp.bfloat16),
            pltpu.SemaphoreType.DMA((2 * count,)),
        ],
        name="join",
        **settings(12 * tokens * rows * rows * count, 12 * rows * rows * count, 20 * MIB),
    )(order, near(x), far(w_fc), after)


def columns_of(rows_of_stats):
    count, tokens = rows_of_stats.shape
    padded = jnp.concatenate([rows_of_stats, jnp.zeros((tokens - count, tokens), jnp.float32)], axis=0)
    return padded.T


def target_mask(me, targets_ref, share):
    column = me * share + lax.broadcasted_iota(jnp.int32, (targets_ref.shape[1], share), 1)
    return column == columns_of(targets_ref[...].astype(jnp.float32))[:, :1].astype(jnp.int32)


def head_kernel(first, counts, last, starts, w_ref, before_ref, targets_ref, *rest):
    pieces, (out_ref, extra_ref) = rest[:-2], rest[-2:]
    width = pieces[0].shape[2]
    out_ref[...] = before_ref[...]
    at = first
    for piece_ref, count in zip(pieces, counts):

        @pl.loop(0, count)
        def _(q):
            row = pl.multiple_of(starts[at + q], 128)
            out_ref[...] += jnp.dot(piece_ref[q], w_ref[pl.ds(row, width), :], preferred_element_type=jnp.float32)

        at += count
    if not last:
        extra_ref[...] = jnp.ones_like(extra_ref)
        return
    logits = out_ref[...]
    tokens, share = logits.shape
    peak = jnp.max(logits, axis=1, keepdims=True)
    shifted = logits - peak
    weight = jnp.exp(shifted)
    picked = jnp.where(target_mask(starts[starts.shape[0] - 1], targets_ref, share), logits, 0.0)
    lane = lax.broadcasted_iota(jnp.int32, (tokens, tokens), 1)
    stats = jnp.where(lane == 0, peak, 0.0)
    for k, part in enumerate((weight, weight * shifted, picked)):
        stats = jnp.where(lane == k + 1, jnp.sum(part, axis=1, keepdims=True), stats)
    extra_ref[...] = stats.T[: extra_ref.shape[0]]


def head(starts, first, pieces, w_lm, before, targets, last):
    tokens, width = pieces[0].shape[1:]
    counts = tuple(p.shape[0] for p in pieces)
    share = w_lm.shape[1]
    extra = (8, tokens) if last else (1, width)
    return pl.pallas_call(
        functools.partial(head_kernel, first, counts, last),
        out_shape=(vmem_out(before.shape, jnp.float32), vmem_out(extra, jnp.float32)),
        in_specs=[IN_SMEM] + [IN_VMEM] * (3 + len(pieces)),
        out_specs=(IN_VMEM, IN_VMEM),
        name="head",
        **settings(2 * tokens * width * share * sum(counts), 8 * tokens * share, 6 * MIB),
    )(starts, near(w_lm), near(before), near(targets), *[near(p) for p in pieces])


def back_products(first, count, order, d_ref, w_ref, out_ref):
    width = out_ref.shape[3]

    @pl.loop(0, count)
    def _(q):
        for s in range(2):
            row = pl.multiple_of(order[s, first + q], 128)
            for at in range(0, width, TILE):
                out_ref[s, q, :, at : at + TILE] = lax.dot_general(
                    d_ref[...],
                    w_ref[pl.ds(row + at, TILE), :],
                    (((1,), (1,)), ((), ())),
                    preferred_element_type=jnp.float32,
                )


def back_first_kernel(first, count, order, starts, logits_ref, stats_ref, targets_ref, w_ref, out_ref, d_ref):
    logits = logits_ref[...]
    tokens, share = logits.shape
    log_total = columns_of(stats_ref[...])[:, :1]
    hit = jnp.where(target_mask(starts[starts.shape[0] - 1], targets_ref, share), 1.0, 0.0)
    d_ref[...] = ((jnp.exp(logits - log_total) - hit) / tokens).astype(d_ref.dtype)
    back_products(first, count, order, d_ref, w_ref, out_ref)


def back_first(order, starts, first, count, logits, stats, targets, w_lm, width):
    tokens, share = logits.shape
    return pl.pallas_call(
        functools.partial(back_first_kernel, first, count),
        out_shape=(vmem_out((2, count, tokens, width), jnp.float32), vmem_out((tokens, share), jnp.bfloat16)),
        in_specs=[IN_SMEM] * 2 + [IN_VMEM] * 4,
        out_specs=(IN_VMEM, IN_VMEM),
        name="back_first",
        **settings(4 * tokens * width * share * count, 8 * tokens * width * count, 6 * MIB),
    )(order, starts, near(logits), near(stats), near(targets), near(w_lm))


def back_rest_kernel(first, count, order, d_ref, w_ref, after_ref, out_ref, token_ref):
    token_ref[...] = jnp.ones_like(token_ref)
    back_products(first, count, order, d_ref, w_ref, out_ref)


def back_rest(order, first, count, dlogits, w_lm, width, after):
    tokens, share = dlogits.shape
    return pl.pallas_call(
        functools.partial(back_rest_kernel, first, count),
        out_shape=(vmem_out((2, count, tokens, width), jnp.float32), vmem_out((1, width), jnp.float32)),
        in_specs=[IN_SMEM, IN_VMEM, IN_VMEM, ANYWHERE],
        out_specs=(IN_VMEM, IN_VMEM),
        name="back_rest",
        **settings(4 * tokens * width * share * count, 8 * tokens * width * count, 6 * MIB),
    )(order, near(dlogits), near(w_lm), after)


def head_grad_kernel(counts, starts, d_ref, after_ref, *rest):
    pieces = rest[: len(counts)]
    out_ref, token_ref, slots, sems = rest[-4:]
    width = pieces[0].shape[2]
    share = d_ref.shape[1]
    token_ref[...] = jnp.ones_like(token_ref)

    def copy(at):
        row = pl.multiple_of(starts[at], 128)
        return pltpu.make_async_copy(slots.at[at], out_ref.at[pl.ds(row, width), :], sems.at[at])

    offset = 0
    for piece_ref, count in zip(pieces, counts):

        @pl.loop(0, count)
        def _(q):
            turned = piece_ref[q].T
            for column in range(0, share, TILE):
                slots[offset + q, :, column : column + TILE] = jnp.dot(
                    turned, d_ref[:, column : column + TILE], preferred_element_type=jnp.float32
                ).astype(slots.dtype)
            copy(offset + q).start()

        offset += count

    for at in range(sum(counts)):
        copy(at).wait()


def head_grad(starts, pieces, dlogits, full_width, after):
    tokens, width = pieces[0].shape[1:]
    counts = tuple(p.shape[0] for p in pieces)
    share = dlogits.shape[1]
    blocks = sum(counts)
    return pl.pallas_call(
        functools.partial(head_grad_kernel, counts),
        out_shape=(
            jax.ShapeDtypeStruct((full_width, share), jnp.bfloat16),
            vmem_out((1, width), jnp.float32),
        ),
        in_specs=[IN_SMEM, IN_VMEM, ANYWHERE] + [IN_VMEM] * len(pieces),
        out_specs=(ANYWHERE, IN_VMEM),
        scratch_shapes=[pltpu.VMEM((blocks, width, share), jnp.bfloat16), pltpu.SemaphoreType.DMA((blocks,))],
        name="head_grad",
        **settings(2 * tokens * width * share * blocks, 2 * width * share * blocks, 22 * MIB),
    )(starts, near(dlogits), after, *[near(p) for p in pieces])


def join_grad_kernel(first, counts, aliased, starts, x_ref, *rest):
    pieces = rest[aliased : aliased + len(counts)]
    out_ref, token_ref, slots, sems = rest[-4:]
    rows, width = slots.shape[2:]
    token_ref[...] = jnp.ones_like(token_ref)

    def copy(at, j):
        column = pl.multiple_of(starts[first + at], 128)
        return pltpu.make_async_copy(
            slots.at[at, j], out_ref.at[j, :, pl.ds(column, width)], sems.at[3 * at + j]
        )

    offset = 0
    for piece_ref, count in zip(pieces, counts):

        @pl.loop(0, count)
        def _(q):
            for j in range(3):
                for at in range(0, width, TILE):
                    slots[offset + q, j, :, at : at + TILE] = jnp.dot(
                        x_ref[j * rows : (j + 1) * rows, :],
                        piece_ref[q, :, at : at + TILE],
                        preferred_element_type=jnp.float32,
                    ).astype(slots.dtype)
                copy(offset + q, j).start()

        offset += count

    for at in range(sum(counts)):
        for j in range(3):
            copy(at, j).wait()


def join_grad(starts, first, pieces, x_turned, full_width, into):
    tokens, width = pieces[0].shape[1:]
    rows = x_turned.shape[0] // 3
    counts = tuple(p.shape[0] for p in pieces)
    extra = () if into is None else (into,)
    blocks = sum(counts)
    return pl.pallas_call(
        functools.partial(join_grad_kernel, first, counts, len(extra)),
        out_shape=(
            jax.ShapeDtypeStruct((3, rows, full_width), jnp.bfloat16),
            vmem_out((1, width), jnp.float32),
        ),
        in_specs=[IN_SMEM, IN_VMEM] + [ANYWHERE] * len(extra) + [IN_VMEM] * len(pieces),
        out_specs=(ANYWHERE, IN_VMEM),
        scratch_shapes=[
            pltpu.VMEM((blocks, 3, rows, width), jnp.bfloat16),
            pltpu.SemaphoreType.DMA((3 * blocks,)),
        ],
        input_output_aliases={2: 0} if extra else {},
        name="join_grad",
        **settings(6 * tokens * rows * width * blocks, 6 * rows * width * blocks, 14 * MIB),
    )(starts, near(x_turned), *extra, *[near(p) for p in pieces])


def cut(total, order, width):
    tokens = total.shape[0]
    blocks = total.reshape(tokens, -1, width).transpose(1, 0, 2)
    blocks = jnp.take(blocks, order // width, axis=0)
    quarter = order.shape[1] // 4
    return blocks[:, :quarter], blocks[:, quarter : 2 * quarter], blocks[:, 2 * quarter :]


def whole(pieces, starts):
    blocks = jnp.take(jnp.concatenate(pieces, axis=0), jnp.argsort(starts[:-1]), axis=0)
    return blocks.transpose(1, 0, 2).reshape(blocks.shape[1], -1)


def contributions(x, group, size):
    return [x] + [exchange(x, m, size) for m in masks_of(group)]


def tree_sum(items):
    while len(items) > 1:
        items = [items[k] + items[k + 1] for k in range(0, len(items), 2)]
    return items[0]


def merge_sums(items):
    peak = functools.reduce(jnp.maximum, [i[0:1] for i in items])
    shifts = [i[0:1] - peak for i in items]
    scales = [jnp.exp(s) for s in shifts]
    return jnp.concatenate(
        [
            peak,
            tree_sum([i[1:2] * c for i, c in zip(items, scales)]),
            tree_sum([(i[2:3] + i[1:2] * s) * c for i, s, c in zip(items, shifts, scales)]),
            tree_sum([i[3:4] for i in items]),
        ],
        axis=0,
    )


def with_token(x, token):
    return x if token is None else (x.astype(jnp.float32) * token).astype(x.dtype)


def reduce_halves(low, high, rest, bits, size, pack, unpack, work):
    got = unpack(exchange(pack(high), 1, size))
    quarter = low.shape[1]
    sent = low + got[:, quarter:]
    passed = [exchange(pack(sent[0]), 2, size), exchange(pack(sent[1]), 4, size)]
    remaining, token = rest(sent)
    token = work(1, remaining, token)
    total = remaining + got[:, :quarter]
    total = total + with_token(unpack(jnp.stack(passed)), token)
    half = quarter // 2
    sent = total[:, half:]
    passed = [exchange(pack(sent[0]), 4, size), exchange(pack(sent[1]), 2, size)]
    token = work(2, sent, None)
    total = total[:, :half] + with_token(unpack(jnp.stack(passed)), token)
    for bit in range(3, bits - 1):
        half = total.shape[1] // 2
        total = total[:, :half] + unpack(exchange(pack(total[:, half:]), 1 << bit, size))
    return total


def gather(held, bits, size, work):
    def flat(x):
        return x.reshape((-1,) + x.shape[2:])

    fresh = held
    across = []
    for bit in range(bits - 2, 2, -1):
        arrived = exchange(held, 1 << bit, size)
        across.append(exchange(fresh, 1, size))
        token = work([flat(fresh)], False)
        fresh = with_token(arrived, token)
        held = jnp.concatenate([held, fresh], axis=1)
    over_y, over_z = exchange(held, 2, size), exchange(held, 4, size)
    across.append(exchange(fresh, 1, size))
    token = work([flat(fresh)] + [flat(a) for a in across], False)
    over_y, over_z = with_token(over_y, token), with_token(over_z, token)
    second = [exchange(over_z[0], 2, size), exchange(over_y[1], 4, size)]
    across = [exchange(over_y, 1, size), exchange(over_z, 1, size)]
    token = work([flat(x) for x in (over_y, over_z, *across)], False)
    second = [with_token(x, token) for x in second]
    across = exchange(jnp.stack(second), 1, size)
    work(second, False)
    work([flat(across)], True)


def gather_crossing(held, bits, size, work):
    def flat(x):
        return x.reshape((-1,) + x.shape[2:])

    fresh = held
    across = []
    for bit in range(bits - 2, 2, -1):
        arrived = exchange(held, 1 << bit, size)
        across.append(exchange(fresh, 1, size))
        token = work([flat(fresh)], False)
        fresh = with_token(arrived, token)
        held = jnp.concatenate([held, fresh], axis=1)
    first = [exchange(held[0], 4, size), exchange(held[1], 2, size)]
    across.append(exchange(fresh, 1, size))
    token = work([flat(fresh)], False)
    first = with_token(jnp.stack(first), token)
    across += [first, exchange(first, 1, size)]
    both = jnp.concatenate([held, first], axis=1)
    second = [exchange(both[0], 2, size), exchange(both[1], 4, size)]
    token = work([flat(a) for a in across], False)
    second = with_token(jnp.stack(second), token)
    across = exchange(second, 1, size)
    work([flat(second)], False)
    work([flat(across)], True)


def on_device(size, low_feat, mid_feat, high_feat, w_fc, gain, w_lm, targets):
    me = lax.axis_index("section")
    rows, full_width = w_fc.shape[1], w_fc.shape[2]
    share = w_lm.shape[1]
    tokens = targets.shape[0]
    bits = size.bit_length() - 1
    count, quarter = size // 4, size // 8
    order = (jnp.asarray(reduce_places(bits)) ^ me) * rows
    starts = jnp.concatenate([(jnp.asarray(gather_places(bits)) ^ me) * rows, me[None]])
    crossing_starts = jnp.concatenate([(jnp.asarray(gather_crossing_places(bits)) ^ me) * rows, me[None]])
    kernels = rows % TILE == 0
    target_row = targets.reshape(1, tokens)

    sent = jnp.concatenate(
        [f.reshape(-1, size, rows) for f in (low_feat, mid_feat, high_feat)], axis=2
    ).transpose(1, 0, 2)
    x = lax.all_to_all(sent, "section", split_axis=0, concat_axis=0, tiled=True).reshape(tokens, 3 * rows)

    held = {"logits": jnp.zeros((tokens, share), jnp.float32), "grad_lm": None, "grad_fc": None}
    if kernels:
        high, _, held["x"] = join(order, count, count, x, w_fc, sent, True)
        low, _ = join(order, quarter, quarter, x, w_fc, sent, False)
    else:
        total = jnp.dot(x, w_fc.reshape(3 * rows, full_width), preferred_element_type=jnp.float32)
        remaining, low, high = cut(total, order, rows)

    def join_rest(after):
        return join(order, 0, quarter, x, w_fc, after, False) if kernels else (remaining, None)

    def bring_head(k, after, token):
        if kernels and k == 1:
            held["lm"], token = stage(w_lm, after, rows)
        return token

    total = reduce_halves(low, high, join_rest, bits, size, lambda x: x, lambda x: x, bring_head)
    partner = 1 << (bits - 1)

    def finish(total, pack, unpack, beside):
        passed = unpack(exchange(pack(total), partner, size))
        return total + with_token(jnp.stack([passed[1], passed[0]]), beside(total))

    joined = finish(total, lambda x: x, lambda x: x, lambda after: None)

    squares = jnp.sum(joined * joined, axis=(1, 3))
    squares = squares[0] + squares[1]
    for group in sum_rounds(bits - 1):
        squares = tree_sum(contributions(squares, group, size))
    inv_rms = lax.rsqrt(squares / full_width + epsilon)[:, None]
    gains = jnp.stack([gain, exchange(gain, partner, size)])[:, None, None, :]
    normed = (joined * inv_rms * gains).astype(jnp.bfloat16)

    all_normed, all_dfused = [], []

    def add_logits(pieces, last):
        first = sum(p.shape[0] for p in all_normed)
        all_normed.extend(pieces)
        if kernels:
            held["logits"], extra = head(starts, first, pieces, held["lm"], held["logits"], target_row, last)
            if last:
                held["stats"] = extra
            return extra

    gather(normed, bits, size, add_logits)
    logits = held["logits"]
    if kernels:
        stats = held["stats"][:4]
    else:
        normed_all = whole(all_normed, starts)
        logits = jnp.dot(normed_all, w_lm, preferred_element_type=jnp.float32)
        is_target = (me * share + lax.iota(jnp.int32, share))[None, :] == targets[:, None]
        peak = jnp.max(logits, axis=1)
        shifted = logits - peak[:, None]
        weight = jnp.exp(shifted)
        stats = jnp.stack(
            [
                peak,
                jnp.sum(weight, axis=1),
                jnp.sum(weight * shifted, axis=1),
                jnp.sum(jnp.where(is_target, logits, 0.0), axis=1),
            ]
        )
    for group in sum_rounds(bits):
        stats = merge_sums(contributions(stats, group, size))
    peak, exp_total, exp_moment, picked = stats[0], stats[1], stats[2], stats[3]
    log_total = peak + jnp.log(exp_total)
    token_loss = log_total - picked
    rowdot = ((exp_moment / exp_total - (picked - peak)) / tokens)[:, None] / inv_rms

    if kernels:
        spread = jnp.broadcast_to(log_total[None], (8, tokens))
        high, dlogits = back_first(order, starts, count, count, logits, spread, target_row, held["lm"], rows)
        low, _ = back_rest(order, quarter, quarter, dlogits, held["lm"], rows, high)
    else:
        dlogits = (
            (jnp.exp(logits - log_total[:, None]) - is_target.astype(jnp.float32)) / tokens
        ).astype(jnp.bfloat16)
        total = lax.dot_general(
            dlogits, w_lm, (((1,), (1,)), ((), ())), preferred_element_type=jnp.float32
        )
        left, low, high = cut(total, order, rows)

    def back_last(after):
        return back_rest(order, 0, quarter, dlogits, held["lm"], rows, after) if kernels else (left, None)

    scale = HALF_SCALE * (tokens / 128)

    def pack_half(x):
        return (x * scale).astype(jnp.float16)

    def unpack_half(x):
        return x.astype(jnp.float32) * (1.0 / scale)

    def nothing(k, after, token):
        return token

    total = reduce_halves(low, high, back_last, bits, size, pack_half, unpack_half, nothing)

    def fill_grad_lm(after):
        if kernels:
            held["grad_lm"], token = head_grad(starts, all_normed, dlogits, full_width, after)
            return token

    dnormed = finish(total, pack_half, unpack_half, fill_grad_lm)
    if kernels:
        grad_lm = held["grad_lm"]
    else:
        grad_lm = lax.dot_general(
            normed_all, dlogits, (((0,), (0,)), ((), ())), preferred_element_type=jnp.float32
        ).astype(jnp.bfloat16)

    grad_gain = jnp.sum(dnormed[0, 0] * joined[0, 0] * inv_rms, axis=0)
    dfused = (
        inv_rms * (dnormed * gains) - joined * (inv_rms * inv_rms * inv_rms * rowdot / full_width)
    ).astype(jnp.bfloat16)

    def fill_grad_fc(pieces, last):
        first = sum(p.shape[0] for p in all_dfused)
        all_dfused.extend(pieces)
        if kernels:
            held["grad_fc"], token = join_grad(crossing_starts, first, pieces, held["x"], full_width, held["grad_fc"])
            return token

    gather_crossing(dfused, bits, size, fill_grad_fc)
    if kernels:
        grad_fc = held["grad_fc"]
    else:
        grad_fc = jnp.dot(x.T, whole(all_dfused, crossing_starts), preferred_element_type=jnp.float32)
        grad_fc = grad_fc.astype(jnp.bfloat16).reshape(3, rows, full_width)
    return (token_loss, grad_fc, grad_gain, grad_lm)


def solution(mesh):
    return jax.shard_map(
        functools.partial(on_device, mesh.shape["section"]),
        mesh=mesh,
        in_specs=(
            P(("grp", "section"), None),
            P(("grp", "section"), None),
            P(("grp", "section"), None),
            P(None, "section", None),
            P("section"),
            P(None, "section"),
            P("grp"),
        ),
        out_specs=(P("grp"), P("grp", "section", None), P(("grp", "section")), P("grp", "section")),
        check_vma=False,
    )
```

```python
import functools

import jax
import jax.numpy as jnp
import numpy as np
from jax import lax
from jax.experimental import pallas as pl
from jax.experimental.pallas import tpu as pltpu
from jax.sharding import PartitionSpec as P

epsilon = 1e-06
MIB = 1024 * 1024
HALF_SCALE = 2.0**20
TILE = 256


def reduce_places(bits):
    out = []
    for stream, order in enumerate(([1, 2], [2, 1])):
        order = order + list(range(3, bits - 1))
        spread = [
            sum(((q >> (len(order) - 1 - k)) & 1) << bit for k, bit in enumerate(order))
            for q in range(1 << len(order))
        ]
        spread = [p | (stream << (bits - 1)) for p in spread]
        out.append(spread + [p + 1 for p in spread])
    return np.array(out, np.int32)


def gather_places(bits):
    held = fresh = np.array([[0], [1 << (bits - 1)]], np.int32)
    out, across = [held], []
    for bit in range(bits - 2, 2, -1):
        across.append(fresh ^ 1)
        fresh = held ^ (1 << bit)
        held = np.concatenate([held, fresh], axis=1)
        out.append(fresh)
    over_y, over_z = held ^ 2, held ^ 4
    second = np.stack([over_z[0] ^ 2, over_y[1] ^ 4])
    out += [*across, fresh ^ 1, over_y, over_z, over_y ^ 1, over_z ^ 1, second, second ^ 1]
    return np.concatenate([p.reshape(-1) for p in out]).astype(np.int32)


def gather_crossing_places(bits):
    held = fresh = np.array([[0], [1 << (bits - 1)]], np.int32)
    out, across = [held], []
    for bit in range(bits - 2, 2, -1):
        across.append(fresh ^ 1)
        fresh = held ^ (1 << bit)
        held = np.concatenate([held, fresh], axis=1)
        out.append(fresh)
    first = held ^ np.array([[4], [2]], np.int32)
    second = np.concatenate([held, first], axis=1) ^ np.array([[2], [4]], np.int32)
    out += [*across, fresh ^ 1, first, first ^ 1, second, second ^ 1]
    return np.concatenate([p.reshape(-1) for p in out]).astype(np.int32)


def masks_of(group):
    return [sum(1 << b for k, b in enumerate(group) if (m >> k) & 1) for m in range(1, 1 << len(group))]


def sum_rounds(top):
    return [[bit] for bit in range(top - 1, 2, -1)] + [[1, 2], [0]]


def exchange(x, mask, size):
    return lax.ppermute(x, "section", [(i, i ^ mask) for i in range(size)])


def settings(flops, bytes_moved, limit):
    return dict(
        compiler_params=pltpu.CompilerParams(vmem_limit_bytes=limit),
        cost_estimate=pl.CostEstimate(flops=flops, bytes_accessed=bytes_moved, transcendentals=0),
    )


ANYWHERE = pl.BlockSpec(memory_space=pl.ANY)
IN_VMEM = pl.BlockSpec(memory_space=pltpu.VMEM)
IN_SMEM = pl.BlockSpec(memory_space=pltpu.SMEM)
vmem_out = pltpu.VMEM


def near(x):
    return pltpu.with_memory_space_constraint(x, pltpu.VMEM)


def far(x):
    return pltpu.with_memory_space_constraint(x, pltpu.HBM)


def stage_kernel(pieces, w_ref, after_ref, out_ref, token_ref, sems):
    copies = []
    for k, piece in enumerate(pieces):
        copies.append(pltpu.make_async_copy(w_ref.at[piece], out_ref.at[piece], sems.at[k]))
    for copy in copies:
        copy.start()
    token_ref[...] = jnp.ones_like(token_ref)
    for copy in copies:
        copy.wait()


def stage(w, after, rows):
    step = w.shape[0] // 16
    pieces = [pl.ds(k * step, step) for k in range(16)]
    return pl.pallas_call(
        functools.partial(stage_kernel, pieces),
        out_shape=(vmem_out(w.shape, w.dtype), vmem_out((1, rows), jnp.float32)),
        in_specs=[ANYWHERE, ANYWHERE],
        out_specs=(IN_VMEM, IN_VMEM),
        scratch_shapes=[pltpu.SemaphoreType.DMA((len(pieces),))],
        name="stage",
        **settings(0, w.size * 2, 2 * MIB),
    )(far(w), after)


def join_kernel(first, count, order, x_ref, w_ref, after_ref, *rest):
    out_ref, token_ref, slots, sems = rest[0], rest[1], rest[-2], rest[-1]
    rows = w_ref.shape[1]
    width = slots.shape[3]

    def copy(q, s):
        column = pl.multiple_of(order[s, first + q], 128)
        at = 2 * q + s
        return pltpu.make_async_copy(w_ref.at[:, :, pl.ds(column, width)], slots.at[at], sems.at[at])

    for q in range(count):
        for s in range(2):
            copy(q, s).start()
    token_ref[...] = jnp.ones_like(token_ref)
    if len(rest) == 5:
        rest[2][...] = x_ref[...].T

    @pl.loop(0, count)
    def _(q):
        for s in range(2):
            copy(q, s).wait()
            for at in range(0, width, TILE):
                total = jnp.dot(
                    x_ref[:, :rows], slots[2 * q + s, 0, :, at : at + TILE], preferred_element_type=jnp.float32
                )
                for j in (1, 2):
                    total += jnp.dot(
                        x_ref[:, j * rows : (j + 1) * rows],
                        slots[2 * q + s, j, :, at : at + TILE],
                        preferred_element_type=jnp.float32,
                    )
                out_ref[s, q, :, at : at + TILE] = total


def join(order, first, count, x, w_fc, after, turn):
    tokens = x.shape[0]
    rows = w_fc.shape[1]
    width = rows
    shapes = [vmem_out((2, count, tokens, width), jnp.float32), vmem_out((1, width), jnp.float32)]
    if turn:
        shapes.append(jax.ShapeDtypeStruct(x.shape[::-1], x.dtype))
    return pl.pallas_call(
        functools.partial(join_kernel, first, count),
        out_shape=tuple(shapes),
        in_specs=[IN_SMEM, IN_VMEM, ANYWHERE, ANYWHERE],
        out_specs=(IN_VMEM,) * len(shapes),
        scratch_shapes=[
            pltpu.VMEM((2 * count, 3, rows, width), jnp.bfloat16),
            pltpu.SemaphoreType.DMA((2 * count,)),
        ],
        name="join",
        **settings(12 * tokens * rows * rows * count, 12 * rows * rows * count, 20 * MIB),
    )(order, near(x), far(w_fc), after)


def columns_of(rows_of_stats):
    count, tokens = rows_of_stats.shape
    padded = jnp.concatenate([rows_of_stats, jnp.zeros((tokens - count, tokens), jnp.float32)], axis=0)
    return padded.T


def target_mask(me, targets_ref, share):
    column = me * share + lax.broadcasted_iota(jnp.int32, (targets_ref.shape[1], share), 1)
    return column == columns_of(targets_ref[...].astype(jnp.float32))[:, :1].astype(jnp.int32)


def head_kernel(first, counts, last, starts, w_ref, before_ref, targets_ref, *rest):
    pieces, (out_ref, extra_ref) = rest[:-2], rest[-2:]
    width = pieces[0].shape[2]
    out_ref[...] = before_ref[...]
    at = first
    for piece_ref, count in zip(pieces, counts):

        @pl.loop(0, count)
        def _(q):
            row = pl.multiple_of(starts[at + q], 128)
            out_ref[...] += jnp.dot(piece_ref[q], w_ref[pl.ds(row, width), :], preferred_element_type=jnp.float32)

        at += count
    if not last:
        extra_ref[...] = jnp.ones_like(extra_ref)
        return
    logits = out_ref[...]
    tokens, share = logits.shape
    peak = jnp.max(logits, axis=1, keepdims=True)
    shifted = logits - peak
    weight = jnp.exp(shifted)
    picked = jnp.where(target_mask(starts[starts.shape[0] - 1], targets_ref, share), logits, 0.0)
    lane = lax.broadcasted_iota(jnp.int32, (tokens, tokens), 1)
    stats = jnp.where(lane == 0, peak, 0.0)
    for k, part in enumerate((weight, weight * shifted, picked)):
        stats = jnp.where(lane == k + 1, jnp.sum(part, axis=1, keepdims=True), stats)
    extra_ref[...] = stats.T[: extra_ref.shape[0]]


def head(starts, first, pieces, w_lm, before, targets, last):
    tokens, width = pieces[0].shape[1:]
    counts = tuple(p.shape[0] for p in pieces)
    share = w_lm.shape[1]
    extra = (8, tokens) if last else (1, width)
    return pl.pallas_call(
        functools.partial(head_kernel, first, counts, last),
        out_shape=(vmem_out(before.shape, jnp.float32), vmem_out(extra, jnp.float32)),
        in_specs=[IN_SMEM] + [IN_VMEM] * (3 + len(pieces)),
        out_specs=(IN_VMEM, IN_VMEM),
        name="head",
        **settings(2 * tokens * width * share * sum(counts), 8 * tokens * share, 6 * MIB),
    )(starts, near(w_lm), near(before), near(targets), *[near(p) for p in pieces])


def back_products(first, count, order, d_ref, w_ref, out_ref):
    width = out_ref.shape[3]

    @pl.loop(0, count)
    def _(q):
        for s in range(2):
            row = pl.multiple_of(order[s, first + q], 128)
            for at in range(0, width, TILE):
                out_ref[s, q, :, at : at + TILE] = lax.dot_general(
                    d_ref[...],
                    w_ref[pl.ds(row + at, TILE), :],
                    (((1,), (1,)), ((), ())),
                    preferred_element_type=jnp.float32,
                )


def back_first_kernel(first, count, order, starts, logits_ref, stats_ref, targets_ref, w_ref, out_ref, d_ref):
    logits = logits_ref[...]
    tokens, share = logits.shape
    log_total = columns_of(stats_ref[...])[:, :1]
    hit = jnp.where(target_mask(starts[starts.shape[0] - 1], targets_ref, share), 1.0, 0.0)
    d_ref[...] = ((jnp.exp(logits - log_total) - hit) / tokens).astype(d_ref.dtype)
    back_products(first, count, order, d_ref, w_ref, out_ref)


def back_first(order, starts, first, count, logits, stats, targets, w_lm, width):
    tokens, share = logits.shape
    return pl.pallas_call(
        functools.partial(back_first_kernel, first, count),
        out_shape=(vmem_out((2, count, tokens, width), jnp.float32), vmem_out((tokens, share), jnp.bfloat16)),
        in_specs=[IN_SMEM] * 2 + [IN_VMEM] * 4,
        out_specs=(IN_VMEM, IN_VMEM),
        name="back_first",
        **settings(4 * tokens * width * share * count, 8 * tokens * width * count, 6 * MIB),
    )(order, starts, near(logits), near(stats), near(targets), near(w_lm))


def back_rest_kernel(first, count, order, d_ref, w_ref, after_ref, out_ref, token_ref):
    token_ref[...] = jnp.ones_like(token_ref)
    back_products(first, count, order, d_ref, w_ref, out_ref)


def back_rest(order, first, count, dlogits, w_lm, width, after):
    tokens, share = dlogits.shape
    return pl.pallas_call(
        functools.partial(back_rest_kernel, first, count),
        out_shape=(vmem_out((2, count, tokens, width), jnp.float32), vmem_out((1, width), jnp.float32)),
        in_specs=[IN_SMEM, IN_VMEM, IN_VMEM, ANYWHERE],
        out_specs=(IN_VMEM, IN_VMEM),
        name="back_rest",
        **settings(4 * tokens * width * share * count, 8 * tokens * width * count, 6 * MIB),
    )(order, near(dlogits), near(w_lm), after)


def head_grad_kernel(counts, starts, d_ref, after_ref, *rest):
    pieces = rest[: len(counts)]
    out_ref, token_ref, slots, sems = rest[-4:]
    width = pieces[0].shape[2]
    share = d_ref.shape[1]
    token_ref[...] = jnp.ones_like(token_ref)

    def copy(at):
        row = pl.multiple_of(starts[at], 128)
        return pltpu.make_async_copy(slots.at[at], out_ref.at[pl.ds(row, width), :], sems.at[at])

    offset = 0
    for piece_ref, count in zip(pieces, counts):

        @pl.loop(0, count)
        def _(q):
            turned = piece_ref[q].T
            for column in range(0, share, TILE):
                slots[offset + q, :, column : column + TILE] = jnp.dot(
                    turned, d_ref[:, column : column + TILE], preferred_element_type=jnp.float32
                ).astype(slots.dtype)
            copy(offset + q).start()

        offset += count

    for at in range(sum(counts)):
        copy(at).wait()


def head_grad(starts, pieces, dlogits, full_width, after):
    tokens, width = pieces[0].shape[1:]
    counts = tuple(p.shape[0] for p in pieces)
    share = dlogits.shape[1]
    blocks = sum(counts)
    return pl.pallas_call(
        functools.partial(head_grad_kernel, counts),
        out_shape=(
            jax.ShapeDtypeStruct((full_width, share), jnp.bfloat16),
            vmem_out((1, width), jnp.float32),
        ),
        in_specs=[IN_SMEM, IN_VMEM, ANYWHERE] + [IN_VMEM] * len(pieces),
        out_specs=(ANYWHERE, IN_VMEM),
        scratch_shapes=[pltpu.VMEM((blocks, width, share), jnp.bfloat16), pltpu.SemaphoreType.DMA((blocks,))],
        name="head_grad",
        **settings(2 * tokens * width * share * blocks, 2 * width * share * blocks, 22 * MIB),
    )(starts, near(dlogits), after, *[near(p) for p in pieces])


def join_grad_kernel(first, counts, aliased, starts, x_ref, *rest):
    pieces = rest[aliased : aliased + len(counts)]
    out_ref, token_ref, slots, sems = rest[-4:]
    rows, width = slots.shape[2:]
    token_ref[...] = jnp.ones_like(token_ref)

    def copy(at, j):
        column = pl.multiple_of(starts[first + at], 128)
        return pltpu.make_async_copy(
            slots.at[at, j], out_ref.at[j, :, pl.ds(column, width)], sems.at[3 * at + j]
        )

    offset = 0
    for piece_ref, count in zip(pieces, counts):

        @pl.loop(0, count)
        def _(q):
            for j in range(3):
                for at in range(0, width, TILE):
                    slots[offset + q, j, :, at : at + TILE] = jnp.dot(
                        x_ref[j * rows : (j + 1) * rows, :],
                        piece_ref[q, :, at : at + TILE],
                        preferred_element_type=jnp.float32,
                    ).astype(slots.dtype)
                copy(offset + q, j).start()

        offset += count

    for at in range(sum(counts)):
        for j in range(3):
            copy(at, j).wait()


def join_grad(starts, first, pieces, x_turned, full_width, into):
    tokens, width = pieces[0].shape[1:]
    rows = x_turned.shape[0] // 3
    counts = tuple(p.shape[0] for p in pieces)
    extra = () if into is None else (into,)
    blocks = sum(counts)
    return pl.pallas_call(
        functools.partial(join_grad_kernel, first, counts, len(extra)),
        out_shape=(
            jax.ShapeDtypeStruct((3, rows, full_width), jnp.bfloat16),
            vmem_out((1, width), jnp.float32),
        ),
        in_specs=[IN_SMEM, IN_VMEM] + [ANYWHERE] * len(extra) + [IN_VMEM] * len(pieces),
        out_specs=(ANYWHERE, IN_VMEM),
        scratch_shapes=[
            pltpu.VMEM((blocks, 3, rows, width), jnp.bfloat16),
            pltpu.SemaphoreType.DMA((3 * blocks,)),
        ],
        input_output_aliases={2: 0} if extra else {},
        name="join_grad",
        **settings(6 * tokens * rows * width * blocks, 6 * rows * width * blocks, 14 * MIB),
    )(starts, near(x_turned), *extra, *[near(p) for p in pieces])


def cut(total, order, width):
    tokens = total.shape[0]
    blocks = total.reshape(tokens, -1, width).transpose(1, 0, 2)
    blocks = jnp.take(blocks, order // width, axis=0)
    quarter = order.shape[1] // 4
    return blocks[:, :quarter], blocks[:, quarter : 2 * quarter], blocks[:, 2 * quarter :]


def whole(pieces, starts):
    blocks = jnp.take(jnp.concatenate(pieces, axis=0), jnp.argsort(starts[:-1]), axis=0)
    return blocks.transpose(1, 0, 2).reshape(blocks.shape[1], -1)


def contributions(x, group, size):
    return [x] + [exchange(x, m, size) for m in masks_of(group)]


def tree_sum(items):
    while len(items) > 1:
        items = [items[k] + items[k + 1] for k in range(0, len(items), 2)]
    return items[0]


def merge_sums(items):
    peak = functools.reduce(jnp.maximum, [i[0:1] for i in items])
    shifts = [i[0:1] - peak for i in items]
    scales = [jnp.exp(s) for s in shifts]
    return jnp.concatenate(
        [
            peak,
            tree_sum([i[1:2] * c for i, c in zip(items, scales)]),
            tree_sum([(i[2:3] + i[1:2] * s) * c for i, s, c in zip(items, shifts, scales)]),
            tree_sum([i[3:4] for i in items]),
        ],
        axis=0,
    )


def with_token(x, token):
    return x if token is None else (x.astype(jnp.float32) * token).astype(x.dtype)


def reduce_halves(low, high, rest, bits, size, pack, unpack, work):
    got = unpack(exchange(pack(high), 1, size))
    quarter = low.shape[1]
    sent = low + got[:, quarter:]
    passed = [exchange(pack(sent[0]), 2, size), exchange(pack(sent[1]), 4, size)]
    remaining, token = rest(sent)
    token = work(1, remaining, token)
    total = remaining + got[:, :quarter]
    total = total + with_token(unpack(jnp.stack(passed)), token)
    half = quarter // 2
    sent = total[:, half:]
    passed = [exchange(pack(sent[0]), 4, size), exchange(pack(sent[1]), 2, size)]
    token = work(2, sent, None)
    total = total[:, :half] + with_token(unpack(jnp.stack(passed)), token)
    for bit in range(3, bits - 1):
        half = total.shape[1] // 2
        total = total[:, :half] + unpack(exchange(pack(total[:, half:]), 1 << bit, size))
    return total


def gather(held, bits, size, work):
    def flat(x):
        return x.reshape((-1,) + x.shape[2:])

    fresh = held
    across = []
    for bit in range(bits - 2, 2, -1):
        arrived = exchange(held, 1 << bit, size)
        across.append(exchange(fresh, 1, size))
        token = work([flat(fresh)], False)
        fresh = with_token(arrived, token)
        held = jnp.concatenate([held, fresh], axis=1)
    over_y, over_z = exchange(held, 2, size), exchange(held, 4, size)
    across.append(exchange(fresh, 1, size))
    token = work([flat(fresh)] + [flat(a) for a in across], False)
    over_y, over_z = with_token(over_y, token), with_token(over_z, token)
    second = [exchange(over_z[0], 2, size), exchange(over_y[1], 4, size)]
    across = [exchange(over_y, 1, size), exchange(over_z, 1, size)]
    token = work([flat(x) for x in (over_y, over_z, *across)], False)
    second = [with_token(x, token) for x in second]
    across = exchange(jnp.stack(second), 1, size)
    work(second, False)
    work([flat(across)], True)


def gather_crossing(held, bits, size, work):
    def flat(x):
        return x.reshape((-1,) + x.shape[2:])

    fresh = held
    across = []
    for bit in range(bits - 2, 2, -1):
        arrived = exchange(held, 1 << bit, size)
        across.append(exchange(fresh, 1, size))
        token = work([flat(fresh)], False)
        fresh = with_token(arrived, token)
        held = jnp.concatenate([held, fresh], axis=1)
    first = [exchange(held[0], 4, size), exchange(held[1], 2, size)]
    across.append(exchange(fresh, 1, size))
    token = work([flat(fresh)], False)
    first = with_token(jnp.stack(first), token)
    across += [first, exchange(first, 1, size)]
    both = jnp.concatenate([held, first], axis=1)
    second = [exchange(both[0], 2, size), exchange(both[1], 4, size)]
    token = work([flat(a) for a in across], False)
    second = [with_token(x, token) for x in second]
    across = [exchange(x, 1, size) for x in second]
    work(second, False)
    work(across, True)


def on_device(size, low_feat, mid_feat, high_feat, w_fc, gain, w_lm, targets):
    me = lax.axis_index("section")
    rows, full_width = w_fc.shape[1], w_fc.shape[2]
    share = w_lm.shape[1]
    tokens = targets.shape[0]
    bits = size.bit_length() - 1
    count, quarter = size // 4, size // 8
    order = (jnp.asarray(reduce_places(bits)) ^ me) * rows
    starts = jnp.concatenate([(jnp.asarray(gather_places(bits)) ^ me) * rows, me[None]])
    crossing_starts = jnp.concatenate([(jnp.asarray(gather_crossing_places(bits)) ^ me) * rows, me[None]])
    kernels = rows % TILE == 0
    target_row = targets.reshape(1, tokens)

    sent = jnp.concatenate(
        [f.reshape(-1, size, rows) for f in (low_feat, mid_feat, high_feat)], axis=2
    ).transpose(1, 0, 2)
    x = lax.all_to_all(sent, "section", split_axis=0, concat_axis=0, tiled=True).reshape(tokens, 3 * rows)

    held = {"logits": jnp.zeros((tokens, share), jnp.float32), "grad_lm": None, "grad_fc": None}
    if kernels:
        high, _, held["x"] = join(order, count, count, x, w_fc, sent, True)
        low, _ = join(order, quarter, quarter, x, w_fc, sent, False)
    else:
        total = jnp.dot(x, w_fc.reshape(3 * rows, full_width), preferred_element_type=jnp.float32)
        remaining, low, high = cut(total, order, rows)

    def join_rest(after):
        return join(order, 0, quarter, x, w_fc, after, False) if kernels else (remaining, None)

    def bring_head(k, after, token):
        if kernels and k == 1:
            held["lm"], token = stage(w_lm, after, rows)
        return token

    total = reduce_halves(low, high, join_rest, bits, size, lambda x: x, lambda x: x, bring_head)
    partner = 1 << (bits - 1)

    def finish(total, pack, unpack, beside):
        passed = unpack(exchange(pack(total), partner, size))
        return total + with_token(jnp.stack([passed[1], passed[0]]), beside(total))

    joined = finish(total, lambda x: x, lambda x: x, lambda after: None)

    squares = jnp.sum(joined * joined, axis=(1, 3))
    squares = squares[0] + squares[1]
    for group in sum_rounds(bits - 1):
        squares = tree_sum(contributions(squares, group, size))
    inv_rms = lax.rsqrt(squares / full_width + epsilon)[:, None]
    gains = jnp.stack([gain, exchange(gain, partner, size)])[:, None, None, :]
    normed = (joined * inv_rms * gains).astype(jnp.bfloat16)

    all_normed, all_dfused = [], []

    def add_logits(pieces, last):
        first = sum(p.shape[0] for p in all_normed)
        all_normed.extend(pieces)
        if kernels:
            held["logits"], extra = head(starts, first, pieces, held["lm"], held["logits"], target_row, last)
            if last:
                held["stats"] = extra
            return extra

    gather(normed, bits, size, add_logits)
    logits = held["logits"]
    if kernels:
        stats = held["stats"][:4]
    else:
        normed_all = whole(all_normed, starts)
        logits = jnp.dot(normed_all, w_lm, preferred_element_type=jnp.float32)
        is_target = (me * share + lax.iota(jnp.int32, share))[None, :] == targets[:, None]
        peak = jnp.max(logits, axis=1)
        shifted = logits - peak[:, None]
        weight = jnp.exp(shifted)
        stats = jnp.stack(
            [
                peak,
                jnp.sum(weight, axis=1),
                jnp.sum(weight * shifted, axis=1),
                jnp.sum(jnp.where(is_target, logits, 0.0), axis=1),
            ]
        )
    for group in sum_rounds(bits):
        stats = merge_sums(contributions(stats, group, size))
    peak, exp_total, exp_moment, picked = stats[0], stats[1], stats[2], stats[3]
    log_total = peak + jnp.log(exp_total)
    log_total, token_loss = lax.optimization_barrier((log_total, log_total - picked))
    rowdot = ((exp_moment / exp_total - (picked - peak)) / tokens)[:, None] / inv_rms

    if kernels:
        spread = jnp.broadcast_to(log_total[None], (8, tokens))
        high, dlogits = back_first(order, starts, count, count, logits, spread, target_row, held["lm"], rows)
        low, _ = back_rest(order, quarter, quarter, dlogits, held["lm"], rows, high)
    else:
        dlogits = (
            (jnp.exp(logits - log_total[:, None]) - is_target.astype(jnp.float32)) / tokens
        ).astype(jnp.bfloat16)
        total = lax.dot_general(
            dlogits, w_lm, (((1,), (1,)), ((), ())), preferred_element_type=jnp.float32
        )
        left, low, high = cut(total, order, rows)

    def back_last(after):
        return back_rest(order, 0, quarter, dlogits, held["lm"], rows, after) if kernels else (left, None)

    scale = HALF_SCALE * (tokens / 128)

    def pack_half(x):
        return (x * scale).astype(jnp.float16)

    def unpack_half(x):
        return x.astype(jnp.float32) * (1.0 / scale)

    def nothing(k, after, token):
        return token

    total = reduce_halves(low, high, back_last, bits, size, pack_half, unpack_half, nothing)

    def fill_grad_lm(after):
        if kernels:
            held["grad_lm"], token = head_grad(starts, all_normed, dlogits, full_width, after)
            return token

    dnormed = finish(total, pack_half, unpack_half, fill_grad_lm)
    if kernels:
        grad_lm = held["grad_lm"]
    else:
        grad_lm = lax.dot_general(
            normed_all, dlogits, (((0,), (0,)), ((), ())), preferred_element_type=jnp.float32
        ).astype(jnp.bfloat16)

    grad_gain = jnp.sum(dnormed[0, 0] * joined[0, 0] * inv_rms, axis=0)
    dfused = (
        inv_rms * (dnormed * gains) - joined * (inv_rms * inv_rms * inv_rms * rowdot / full_width)
    ).astype(jnp.bfloat16)

    def fill_grad_fc(pieces, last):
        first = sum(p.shape[0] for p in all_dfused)
        all_dfused.extend(pieces)
        if kernels:
            held["grad_fc"], token = join_grad(crossing_starts, first, pieces, held["x"], full_width, held["grad_fc"])
            return token

    gather_crossing(dfused, bits, size, fill_grad_fc)
    if kernels:
        grad_fc = held["grad_fc"]
    else:
        grad_fc = jnp.dot(x.T, whole(all_dfused, crossing_starts), preferred_element_type=jnp.float32)
        grad_fc = grad_fc.astype(jnp.bfloat16).reshape(3, rows, full_width)
    return (token_loss, grad_fc, grad_gain, grad_lm)


def solution(mesh):
    return jax.shard_map(
        functools.partial(on_device, mesh.shape["section"]),
        mesh=mesh,
        in_specs=(
            P(("grp", "section"), None),
            P(("grp", "section"), None),
            P(("grp", "section"), None),
            P(None, "section", None),
            P("section"),
            P(None, "section"),
            P("grp"),
        ),
        out_specs=(P("grp"), P("grp", "section", None), P(("grp", "section")), P("grp", "section")),
        check_vma=False,
    )
```
